32 devices in a mesh: groups: 2 (over y), sub: 4 (over z), rhs: 2 (over x), face: 2 (over core).
Axes of the slice: x: 2, y: 2, z: 4, core: 2. Of those that a mesh axis runs over, the one named last changes fastest.
Arguments:
- mortar_in: bfloat16 [1024, 64, 256], P(('groups', 'sub'), 'rhs'), parts along dimension 0, may hold values from -6 to 6
- pump_rate: float32 [128], P(('groups', 'rhs')), parts along dimension 0, may hold values from 4 to 16
- well_cell: int32 [128], P(('groups', 'rhs')), parts along dimension 0, may hold values from 0 to 131071
- face_owner: int32 [2048, 1], P(('groups', 'sub', 'face')), parts along dimension 0, may hold values from 0 to 3; in each aligned block of 128 rows (0 to 127, 128 to 255, ...) at most 64 rows name the same one
- face_slot: int32 [2048], P(('groups', 'sub', 'face')), parts along dimension 0, may hold values from 0 to 127
- face_scale: bfloat16 [2048, 256], P(('groups', 'sub', 'face')), parts along dimension 0, may hold values from 0.5 to 2
- section: int32 [8], P(('groups', 'sub')), parts along dimension 0, may hold values 0 or 1
- basis: bfloat16 [8, 256, 256], P(('groups', 'sub')), parts along dimension 0, may hold values from -0.375 to 0.375
- projection: bfloat16 [256, 256], replicated, may hold values from -0.375 to 0.375
Outputs:
- result: float32 [1024, 64, 256], P(('groups', 'sub', 'face'), 'rhs'), parts along dimension 0
The draws below stay inside these ranges and needn't reach their ends.
There are 2 independent parts, one for each index of `groups`. The reference program is written for one: setup_inputs(seed, part) draws one part's arguments, and reference() takes and returns one part's arrays. A program takes and returns all parts, laid end to end along the dimension named above; an argument that names none is the same for every part. Nothing has to cross between parts.
Inputs may be any that keep to these rules, and one draw needn't show every extreme that they name: `face_owner`: among the 128 faces of one device no subdomain is named by more than 64 faces, a bound that some block reaches.
All inputs are finite; a program needn't handle non-finite values. No bound on the sum of `section` on one device may be relied on, other than what follows from the above.
Results may differ from the reference program's by a relative error of at most 0.004.
Values may be sent and summed in bfloat16 or wider, within the bound.
No kernel may reach another device: no remote copies, remote signals or barrier semaphores. Data moves between devices by JAX's collectives and lax.ppermute only.
A program may use at most 64 MiB of HBM per device.

```python
import math
import jax
import jax.numpy as jnp
import numpy as np
from jax import lax

K = 256
COLS = 64
F_DEV = 128
SUBS = 4
MB_DEV = 128
MBLK = 512
FACES = 1024
CAP = 64
N_FACE = 2


def with_ends(entries, rng, smallest, high):
    longest = entries.shape.index(max(entries.shape))
    spots = []
    for shift in (0, 1):
        where = [jax.random.randint(jax.random.fold_in(rng, axis), (), 0, length) for axis, length in enumerate(entries.shape)]
        where[longest] = (where[longest] + shift) % entries.shape[longest]
        spots.append(tuple(where))
    return entries.at[spots[0]].set(smallest).at[spots[1]].set(high)


def block_scale(rng, extent, cuts, smallest, high):
    level, own = 1.0, jax.random.fold_in(rng, 6)
    for axis_at, shards_of in cuts:
        steps = jnp.exp(jax.random.uniform(jax.random.fold_in(own, axis_at), (shards_of,), jnp.float32, smallest / len(cuts), high / len(cuts)))
        level = level * jnp.repeat(steps, extent[axis_at] // shards_of).reshape([-1 if axis == axis_at else 1 for axis in range(len(extent))])
    return level


def assign_block(key, own, number, rows, number_of, top, limit, slope):
    order = jax.random.permutation(key, number_of)
    crowded, ordinary = shares(number_of, rows * top, limit, slope, True), shares(number_of, rows * top, limit, slope, False)
    places = jnp.arange(number_of)

    def named(tallies, rotation):
        used = int((tallies > 0).sum())
        fixed = max(1, used // 4)
        shifted = fixed + (places - fixed + rotation * (used - fixed)) % max(1, number_of - fixed)
        return jnp.zeros((number_of,), jnp.int32).at[order[jnp.where(places < fixed, places, shifted)]].set(jnp.asarray(tallies, jnp.int32))

    tallies = jnp.where(number % 4 == 0, named(crowded, number // 4), named(ordinary, number - number // 4 - 1))
    mixed = jax.random.permutation(jax.random.fold_in(own, 3), number_of)
    source_of, receiver = mixed[0:number_of // 2 * 2:2], mixed[1:number_of // 2 * 2:2]
    room = jnp.minimum(tallies[source_of] - 1, limit - tallies[receiver]) // 2
    room = jnp.where((source_of == order[0]) | (receiver == order[0]) | (tallies[receiver] == 0), 0, jnp.maximum(room, 0))
    shifted = jax.random.randint(jax.random.fold_in(own, 4), (number_of // 2,), 0, 1 << 20) % (room + 1)
    tallies = tallies.at[source_of].add(-shifted).at[receiver].add(shifted)
    members = jnp.searchsorted(jnp.cumsum(tallies), jnp.arange(rows * top), side="right").astype(jnp.int32)
    table = members.reshape(top, rows).T
    table = table[jax.random.permutation(jax.random.fold_in(own, 1), rows)]
    rotation = jax.random.randint(jax.random.fold_in(own, 2), (rows, 1), 0, top)
    return jnp.take_along_axis(table, (jnp.arange(top)[None, :] + rotation) % top, axis=1)


def shares(amount, total, bound, skew, full):
    loads = [(1 << 20) // math.isqrt(rank ** skew) + 1 for rank in range(1, amount + 1)]
    largest = bound if full else min(bound, max(-(-total // amount), total * loads[0] // sum(loads)))
    least = 1 if total - largest >= amount - 1 else 0
    given, surplus = [largest] + [least] * (amount - 1), total - largest - least * (amount - 1)
    while surplus > 0:
        movable = [i for i in range(1, amount) if given[i] < largest] or [i for i in range(1, amount) if given[i] < bound]
        whole, remaining = sum([loads[i] for i in movable]), surplus
        for i in movable:
            addition = min(bound - given[i], max(1, remaining * loads[i] // whole), surplus)
            given[i] = given[i] + addition
            surplus = surplus - addition
    return np.array(given)


def gaussian(key, shape, spread, most, pieces=(), kind=jnp.bfloat16):
    array = jax.random.normal(key, shape, jnp.float32) * spread
    if len(pieces) > 0:
        array = block_scale(key, shape, pieces, -0.22, 0.18) * array
    return jnp.clip(array, min=-most, max=most).astype(kind)


def setup_inputs(seed: int = 0, part: int = 0) -> dict:
    key_list = jax.random.split(jax.random.key(seed), 10)
    own_keys = jax.random.split(jax.random.fold_in(key_list[9], part), 10)
    mortar_in = gaussian(own_keys[0], (MBLK, COLS, K), 1.0, 6.0, ((0, 4), (1, 2)))
    pump_rate = jnp.clip(jnp.exp(math.log(16.0) - 1.3862944 * jax.random.uniform(own_keys[1], (COLS,), jnp.float32) ** block_scale(own_keys[1], (COLS,), ((0, 2),), -0.2, 0.2)), 4.0, 16.0)
    well_cell = with_ends(jax.random.randint(own_keys[2], (COLS,), 0, MBLK * K), jax.random.fold_in(own_keys[2], 1), 0, (MBLK * K) - 1).astype(jnp.int32)
    face_owner_keys = jax.random.split(jax.random.fold_in(own_keys[3], 1), FACES // F_DEV)
    face_owner_turns = jax.random.permutation(jax.random.fold_in(own_keys[3], 3), FACES // F_DEV)
    face_owner = jax.vmap(lambda own, number: assign_block(jax.random.fold_in(own_keys[3], 2), own, number, F_DEV, SUBS, 1, CAP, 2))(face_owner_keys, face_owner_turns).reshape((FACES, 1))
    face_slot = with_ends(jax.random.randint(own_keys[4], (FACES,), 0, MB_DEV), jax.random.fold_in(own_keys[4], 1), 0, MB_DEV - 1).astype(jnp.int32)
    face_scale = jnp.clip(jnp.exp(math.log(2.0) - 1.3862944 * jax.random.uniform(own_keys[5], (FACES, K), jnp.float32) ** block_scale(own_keys[5], (FACES, K), ((0, 8),), -0.2, 0.2)), 0.5, 2.0).astype(jnp.bfloat16)
    section = with_ends((jax.random.randint(own_keys[6], (SUBS,), 0, 4) < 1).astype(jnp.int32), jax.random.fold_in(own_keys[6], 1), 0, 1)
    basis = gaussian(own_keys[7], (SUBS, K, K), K ** -0.5, 0.375, ((0, 4),))
    projection = gaussian(key_list[8], (K, K), K ** -0.5, 0.375)
    return {"mortar_in": mortar_in, "pump_rate": pump_rate, "well_cell": well_cell, "face_owner": face_owner, "face_slot": face_slot, "face_scale": face_scale, "section": section, "basis": basis, "projection": projection}


def reference(mortar_in, pump_rate, well_cell, face_owner, face_slot, face_scale, section, basis, projection):
    columns = jnp.arange(COLS, dtype=jnp.int32)
    well_terms = jnp.zeros((MBLK, COLS, K), jnp.float32).at[well_cell // K, columns, well_cell % K].add(pump_rate)
    pumped = (mortar_in.astype(jnp.float32) + well_terms).astype(jnp.bfloat16)
    wanted = (face_owner[:, 0] * MB_DEV + face_slot).astype(jnp.int32)
    face_values = pumped[wanted]
    scaled = (face_values.astype(jnp.float32) * face_scale.astype(jnp.float32)[:, None, :]).astype(jnp.bfloat16)
    grouped = scaled.reshape(SUBS, F_DEV * N_FACE * COLS, K)
    signs = (1 - 2 * section).astype(jnp.float32)

    def one_subdomain(items):
        rows, local_basis, orient = items
        return jnp.dot(rows, local_basis, preferred_element_type=jnp.float32) * orient

    flux_rows = lax.map(one_subdomain, (grouped, basis, signs)).reshape(FACES, COLS, K)
    summed = jax.ops.segment_sum(flux_rows, wanted, num_segments=MBLK)
    summed_low = summed.astype(jnp.bfloat16).reshape(MBLK * COLS, K)
    result = jnp.dot(summed_low, projection, preferred_element_type=jnp.float32)
    return result.reshape(MBLK, COLS, K)
```

```python
import functools

import jax
import jax.numpy as jnp
from jax import lax
from jax.experimental import pallas as pl
from jax.experimental.pallas import tpu as pltpu
from jax.sharding import PartitionSpec as P

META_ROWS = 16


def apply_kernel(subdomains, faces_dev, tile_blocks, pumped_ref, projection_ref, *rest):
    packs, (result_ref, weight_ref, basis_ref) = rest[: 2 * subdomains], rest[2 * subdomains :]
    dof_count = projection_ref.shape[0]
    half_rows = dof_count // 2
    blocks_own = weight_ref.shape[1]
    face_id = lax.axis_index("face")

    @pl.when(pl.program_id(0) == 0)
    def _():
        owner_id = lax.axis_index("sub")
        block_ids = face_id * blocks_own + lax.broadcasted_iota(
            jnp.int32, (blocks_own, faces_dev), 0
        )
        for s in range(subdomains):
            total = None
            for which in range(2):
                pack = packs[2 * s + which]
                meta = pack[faces_dev : faces_dev + META_ROWS, :].astype(jnp.int32)
                slots = meta[0:1, :faces_dev]
                owners = meta[0:1, faces_dev : 2 * faces_dev]
                hit = (slots == block_ids) & (owners == owner_id)
                part = jnp.dot(
                    hit.astype(jnp.bfloat16), pack[:faces_dev, :], preferred_element_type=jnp.float32
                )
                total = part if total is None else total + part
                half = face_id if which == 0 else 1 - face_id
                at = pl.multiple_of(s * dof_count + half * half_rows, half_rows)
                basis_ref[pl.ds(at, half_rows), :] = pack[faces_dev + META_ROWS :, :]
            weight_ref[s] = total

    first = pl.program_id(0) * tile_blocks
    columns = pumped_ref.shape[1]
    values = pumped_ref[...].astype(jnp.float32)
    total = None
    for s in range(subdomains):
        weight = weight_ref[s, pl.ds(first, tile_blocks), :]
        scaled = (values * weight[:, None, :]).astype(jnp.bfloat16)
        flux = jnp.dot(
            scaled.reshape(tile_blocks * columns, dof_count),
            basis_ref[s * dof_count : (s + 1) * dof_count, :],
            preferred_element_type=jnp.float32,
        )
        total = flux if total is None else total + flux
    result = jnp.dot(
        total.astype(jnp.bfloat16), projection_ref[...], preferred_element_type=jnp.float32
    )
    result_ref[...] = result.reshape(result_ref.shape)


def on_device(
    mortar_in, pump_rate, well_cell, face_owner, face_slot, face_scale, section, basis, projection
):
    blocks_dev, cols_dev, dof_count = mortar_in.shape
    faces_dev = face_slot.shape[0]
    subdomains = lax.axis_size("sub")
    halves = lax.axis_size("face")
    face_id = lax.axis_index("face")
    blocks_own = blocks_dev // halves
    half_rows = dof_count // halves

    orient = (1 - 2 * section[0]).astype(jnp.bfloat16)
    my_rows = lax.dynamic_slice_in_dim(basis[0], face_id * half_rows, half_rows, 0) * orient
    meta = jnp.concatenate([face_slot, face_owner[:, 0]]).astype(jnp.bfloat16)
    meta = jnp.zeros((META_ROWS, dof_count), jnp.bfloat16).at[0, : 2 * faces_dev].set(meta)
    pack = jnp.concatenate([face_scale, meta, my_rows], axis=0)

    swap = [(i, (i + 1) % halves) for i in range(halves)]
    packs = []
    for shift in range(subdomains):
        if shift:
            ring = [(i, (i + shift) % subdomains) for i in range(subdomains)]
            here = lax.ppermute(pack, "sub", ring)
        else:
            here = pack
        packs += [here, lax.ppermute(here, "face", swap)]

    first_block = face_id * blocks_own
    mine = lax.dynamic_slice_in_dim(mortar_in, first_block, blocks_own, 0)
    block_ids = lax.axis_index("sub") * blocks_dev + first_block + jnp.arange(blocks_own, dtype=jnp.int32)
    cell = block_ids[:, None, None] * dof_count + jnp.arange(dof_count, dtype=jnp.int32)[None, None, :]
    wells = jnp.where(cell == well_cell[None, :, None], pump_rate[None, :, None], 0.0)
    pumped = (mine.astype(jnp.float32) + wells).astype(jnp.bfloat16)

    tile_blocks = 8
    whole = lambda a: pl.BlockSpec(a.shape, lambda i: (0,) * a.ndim)
    tile = pl.BlockSpec((tile_blocks, cols_dev, dof_count), lambda i: (i, 0, 0))
    return pl.pallas_call(
        functools.partial(apply_kernel, subdomains, faces_dev, tile_blocks),
        grid=(blocks_own // tile_blocks,),
        out_shape=jax.ShapeDtypeStruct((blocks_own, cols_dev, dof_count), jnp.float32),
        in_specs=[tile, whole(projection)] + [whole(p) for p in packs],
        out_specs=tile,
        scratch_shapes=[
            pltpu.VMEM((subdomains, blocks_own, dof_count), jnp.float32),
            pltpu.VMEM((subdomains * dof_count, dof_count), jnp.bfloat16),
        ],
        compiler_params=pltpu.CompilerParams(vmem_limit_bytes=48 * 1024 * 1024),
        name="apply_blocks",
    )(pumped, projection, *packs)


def solution(mesh):
    in_specs = (
        P(("groups", "sub"), "rhs", None),
        P(("groups", "rhs")),
        P(("groups", "rhs")),
        P(("groups", "sub", "face"), None),
        P(("groups", "sub", "face")),
        P(("groups", "sub", "face"), None),
        P(("groups", "sub")),
        P(("groups", "sub"), None, None),
        P(),
    )
    out_specs = P(("groups", "sub", "face"), "rhs", None)
    return jax.shard_map(
        on_device, mesh=mesh, in_specs=in_specs, out_specs=out_specs, check_vma=False
    )
```

```python
import functools

import jax
import jax.numpy as jnp
from jax import lax
from jax.experimental import pallas as pl
from jax.experimental.pallas import tpu as pltpu
from jax.sharding import PartitionSpec as P

ROW_TILE = 16
VMEM = pl.BlockSpec(memory_space=pltpu.VMEM)
SMEM = pl.BlockSpec(memory_space=pltpu.SMEM)
MIB = 1024 * 1024


def pack_kernel(subdomains, capacity, owner_ref, slot_ref, scale_ref, section_ref, *packs):
    faces = owner_ref.shape[1]
    rows = packs[0].shape[0] - ROW_TILE
    here = lax.axis_index("sub")
    sign = (1 - 2 * section_ref[0]).astype(jnp.float32)
    owners = owner_ref[...]
    shifts = lax.broadcasted_iota(jnp.int32, (subdomains, faces), 0)
    named = lax.rem(here + shifts, subdomains) == owners
    earlier = lax.broadcasted_iota(jnp.int32, (faces, faces), 0) < lax.broadcasted_iota(
        jnp.int32, (faces, faces), 1
    )
    rank = jnp.dot(
        named.astype(jnp.bfloat16), earlier.astype(jnp.bfloat16), preferred_element_type=jnp.float32
    )
    place = jnp.where(named, rank.astype(jnp.int32), -1)
    slots = slot_ref[...].astype(jnp.bfloat16)
    for shift in range(subdomains):
        hit = place[shift : shift + 1, :] == lax.broadcasted_iota(jnp.int32, (rows, faces), 0)
        hit = hit.astype(jnp.bfloat16)
        packed = jnp.dot(hit, scale_ref[...], preferred_element_type=jnp.float32) * sign
        listed = lax.dot_general(
            slots, hit, (((1,), (1,)), ((), ())), preferred_element_type=jnp.float32
        )
        meta = jnp.concatenate(
            [listed, jnp.zeros((1, packs[shift].shape[1] - rows), jnp.float32)], axis=1
        )
        meta = jnp.broadcast_to(meta, (ROW_TILE, meta.shape[1]))
        packs[shift][:rows, :] = packed.astype(jnp.bfloat16)
        packs[shift][rows:, :] = meta.astype(jnp.bfloat16)


def apply_kernel(subdomains, groups, tiles, *refs):
    pumped_ref, projection_ref, own_ref = refs[:3]
    bases, refs = refs[3 : 3 + 4 * len(groups)], refs[3 + 4 * len(groups) :]
    packs, (result_ref, weight_ref, basis_ref, out_ref, sems) = refs[: 2 * subdomains], refs[2 * subdomains :]
    blocks_own, columns, dof_count = pumped_ref.shape
    face_id = lax.axis_index("face")
    lane = 2 * lax.rem(lax.axis_index("rhs"), 2) + face_id

    def pick(*by_lane):
        value = by_lane[3]
        for which in range(3):
            value = jnp.where(lane == which, by_lane[which], value)
        return value

    spare = subdomains
    basis_ref[0] = own_ref[0]
    for at, (a, b, c) in enumerate(groups):
        places = (
            pick(a, spare, b, c),
            pick(b, c, a, spare),
            pick(spare, a, c, b),
            pick(c, b, spare, a),
        )
        for which in range(4):
            basis_ref[places[which]] = bases[4 * at + which][0]

    rows = packs[0].shape[0] - ROW_TILE
    block_ids = face_id * blocks_own + lax.broadcasted_iota(jnp.int32, (blocks_own, rows), 0)
    for s in range(subdomains):
        total = None
        for pack in packs[2 * s : 2 * s + 2]:
            slots = pack[rows:, :].astype(jnp.int32)[:1, :rows]
            part = jnp.dot(
                (slots == block_ids).astype(jnp.bfloat16), pack[:rows, :], preferred_element_type=jnp.float32
            )
            total = part if total is None else total + part
        weight_ref[s] = total

    tile_blocks = blocks_own // tiles
    copies = []
    for tile in range(tiles):
        at = slice(tile * tile_blocks, (tile + 1) * tile_blocks)
        values = pumped_ref[at].astype(jnp.float32)
        total = None
        for s in range(subdomains):
            scaled = (values * weight_ref[s, at][:, None, :]).astype(jnp.bfloat16)
            flux = jnp.dot(
                scaled.reshape(tile_blocks * columns, dof_count),
                basis_ref[s],
                preferred_element_type=jnp.float32,
            )
            total = flux if total is None else total + flux
        result = jnp.dot(
            total.astype(jnp.bfloat16), projection_ref[...], preferred_element_type=jnp.float32
        )
        out_ref[at] = result.reshape(tile_blocks, columns, dof_count)
        copies.append(pltpu.make_async_copy(out_ref.at[at], result_ref.at[at], sems.at[tile]))
        copies[-1].start()
    for copy in copies:
        copy.wait()


def on_device(
    mortar_in, pump_rate, well_cell, face_owner, face_slot, face_scale, section, basis, projection
):
    blocks_dev, cols_dev, dof_count = mortar_in.shape
    faces_dev = face_slot.shape[0]
    subdomains, rights, halves = lax.axis_size("sub"), lax.axis_size("rhs"), lax.axis_size("face")
    face_id = lax.axis_index("face")
    blocks_own = blocks_dev // halves
    capacity = max(2, 2 * faces_dev // subdomains)
    pack_rows = -(-capacity // ROW_TILE) * ROW_TILE + ROW_TILE

    first_block = face_id * blocks_own
    mine = lax.dynamic_slice_in_dim(mortar_in, first_block, blocks_own, 0)
    block_ids = lax.axis_index("sub") * blocks_dev + first_block + jnp.arange(blocks_own, dtype=jnp.int32)
    cell = block_ids[:, None, None] * dof_count + jnp.arange(dof_count, dtype=jnp.int32)[None, None, :]
    wells = jnp.where(cell == well_cell[None, :, None], pump_rate[None, :, None], 0.0)
    pumped = (mine.astype(jnp.float32) + wells).astype(jnp.bfloat16)

    def flat(sub, right, face):
        return ((sub % subdomains) * rights + right) * halves + face

    cells = [(s, r) for s in range(subdomains) for r in range(rights)]
    cross = [(i, i ^ 1) for i in range(rights)]
    swap = [(i, i ^ 1) for i in range(halves)]
    shifts = list(range(1, subdomains))
    if len(shifts) > 1:
        shifts[0], shifts[1] = shifts[1], shifts[0]
    groups = [tuple(shifts[i : i + 3]) for i in range(0, len(shifts), 3)]
    groups = [g + (subdomains,) * (3 - len(g)) for g in groups]
    bases = []
    for a, b, c in groups:
        pairs = []
        for s, r in cells:
            for face, shift in ((0, b), (1, c)) if r % 2 else ((0, a),):
                if shift < subdomains:
                    pairs.append((flat(s, r, face), flat(s + shift, r, face)))
        first = lax.ppermute(basis, ("sub", "rhs", "face"), pairs)
        first, pumped = lax.optimization_barrier((first, pumped))
        second = lax.ppermute(first, "rhs", cross)
        bases += [first, second, lax.ppermute(first, "face", swap), lax.ppermute(second, "face", swap)]

    packs = pl.pallas_call(
        functools.partial(pack_kernel, subdomains, capacity),
        out_shape=[jax.ShapeDtypeStruct((pack_rows, dof_count), jnp.bfloat16)] * subdomains,
        in_specs=[VMEM, VMEM, VMEM, SMEM],
        out_specs=[VMEM] * subdomains,
        name="pack_weights",
    )(face_owner.reshape(1, faces_dev), face_slot.reshape(1, faces_dev), face_scale, section)
    weights = []
    for shift in range(subdomains):
        here = packs[shift]
        if shift:
            here = lax.ppermute(here, "sub", [(i, (i + shift) % subdomains) for i in range(subdomains)])
        weights += [here, lax.ppermute(here, "face", swap)]

    tiles = 4
    operands = [pumped, projection, basis, *bases, *weights]
    return pl.pallas_call(
        functools.partial(apply_kernel, subdomains, groups, tiles),
        out_shape=jax.ShapeDtypeStruct((blocks_own, cols_dev, dof_count), jnp.float32),
        in_specs=[VMEM] * len(operands),
        out_specs=pl.BlockSpec(memory_space=pl.ANY),
        scratch_shapes=[
            pltpu.VMEM((subdomains, blocks_own, dof_count), jnp.float32),
            pltpu.VMEM((subdomains + 1, dof_count, dof_count), jnp.bfloat16),
            pltpu.VMEM((blocks_own, cols_dev, dof_count), jnp.float32),
            pltpu.SemaphoreType.DMA((tiles,)),
        ],
        compiler_params=pltpu.CompilerParams(vmem_limit_bytes=24 * MIB),
        name="apply_blocks",
    )(*operands)


def solution(mesh):
    in_specs = (
        P(("groups", "sub"), "rhs", None),
        P(("groups", "rhs")),
        P(("groups", "rhs")),
        P(("groups", "sub", "face"), None),
        P(("groups", "sub", "face")),
        P(("groups", "sub", "face"), None),
        P(("groups", "sub")),
        P(("groups", "sub"), None, None),
        P(),
    )
    out_specs = P(("groups", "sub", "face"), "rhs", None)
    return jax.shard_map(
        on_device, mesh=mesh, in_specs=in_specs, out_specs=out_specs, check_vma=False
    )
```

```python
import functools

import jax
import jax.numpy as jnp
from jax import lax
from jax.experimental import pallas as pl
from jax.experimental.pallas import tpu as pltpu
from jax.sharding import PartitionSpec as P

ROW_TILE = 16
VMEM = pl.BlockSpec(memory_space=pltpu.VMEM)
HBM = pl.BlockSpec(memory_space=pltpu.HBM)
SMEM = pl.BlockSpec(memory_space=pltpu.SMEM)
MIB = 1024 * 1024
PREPARE_VMEM = 52


def prepare_kernel(
    subdomains, mortar_ref, owner_any, slot_any, scale_any, rate_ref, cell_ref, section_ref, *refs
):
    packs, (pumped_ref, owner_ref, slot_ref, scale_ref, sems) = refs[:subdomains], refs[subdomains:]
    blocks_own, columns, dof_count = pumped_ref.shape
    here = lax.axis_index("sub")
    first_block = lax.axis_index("face") * blocks_own
    fetches = [
        pltpu.make_async_copy(source, target, sems.at[i])
        for i, (source, target) in enumerate(
            [
                (owner_any, owner_ref),
                (slot_any, slot_ref),
                (scale_any, scale_ref),
                (mortar_ref.at[pl.ds(first_block, blocks_own)], pumped_ref),
            ]
        )
    ]
    for fetch in fetches:
        fetch.start()

    faces = owner_ref.shape[1]
    rows = packs[0].shape[0] - ROW_TILE
    sign = (1 - 2 * section_ref[0]).astype(jnp.float32)
    shifts = lax.broadcasted_iota(jnp.int32, (subdomains, faces), 0)
    owner_ids = lax.rem(here + shifts, subdomains)
    earlier = lax.broadcasted_iota(jnp.int32, (faces, faces), 0) < lax.broadcasted_iota(
        jnp.int32, (faces, faces), 1
    )
    for fetch in fetches[:3]:
        fetch.wait()
    named = owner_ids == owner_ref[...]
    rank = jnp.dot(
        named.astype(jnp.bfloat16), earlier.astype(jnp.bfloat16), preferred_element_type=jnp.float32
    )
    place = jnp.where(named, rank.astype(jnp.int32), -1)
    slots = slot_ref[...].astype(jnp.bfloat16)
    for shift in range(subdomains):
        hit = place[shift : shift + 1, :] == lax.broadcasted_iota(jnp.int32, (rows, faces), 0)
        hit = hit.astype(jnp.bfloat16)
        packed = jnp.dot(hit, scale_ref[...], preferred_element_type=jnp.float32) * sign
        listed = lax.dot_general(
            slots, hit, (((1,), (1,)), ((), ())), preferred_element_type=jnp.float32
        )
        meta = jnp.concatenate([listed, jnp.zeros((1, dof_count - rows), jnp.float32)], axis=1)
        meta = jnp.broadcast_to(meta, (ROW_TILE, dof_count))
        packs[shift][:rows, :] = packed.astype(jnp.bfloat16)
        packs[shift][rows:, :] = meta.astype(jnp.bfloat16)

    fetches[3].wait()
    base = here * (mortar_ref.shape[0]) + first_block
    for column in range(columns):
        block = lax.div(cell_ref[column], dof_count) - base
        dof = lax.rem(cell_ref[column], dof_count)

        @pl.when((block >= 0) & (block < blocks_own))
        def _():
            slab = slice(column // ROW_TILE * ROW_TILE, (column // ROW_TILE + 1) * ROW_TILE)
            shape = (ROW_TILE, dof_count)
            at_well = (lax.broadcasted_iota(jnp.int32, shape, 0) == column % ROW_TILE) & (
                lax.broadcasted_iota(jnp.int32, shape, 1) == dof
            )
            well = jnp.where(at_well, rate_ref[column], 0.0)
            pumped_ref[block, slab, :] = (pumped_ref[block, slab, :].astype(jnp.float32) + well).astype(
                jnp.bfloat16
            )


def apply_kernel(order, groups, tiles, *refs):
    subdomains = len(order)
    pumped_ref, projection_ref, own_ref = refs[:3]
    bases, refs = refs[3 : 3 + 4 * len(groups)], refs[3 + 4 * len(groups) :]
    packs, refs = refs[: 2 * subdomains], refs[2 * subdomains :]
    result_ref, weight_ref, basis_ref, scaled_ref, out_ref, sems = refs
    blocks_own, columns, dof_count = pumped_ref.shape
    face_id = lax.axis_index("face")

    def put(shift, array):
        if not isinstance(shift, int):
            shift = pl.multiple_of(shift * dof_count, dof_count)
        else:
            shift = shift * dof_count
        basis_ref[pl.ds(shift, dof_count), :] = array[0]

    put(0, own_ref)
    for at, (a, b, c) in enumerate(groups):
        first, first_swapped, second, second_swapped = bases[4 * at : 4 * at + 4]
        put(jnp.where(face_id == 0, a, b), first)
        put(jnp.where(face_id == 0, b, a), first_swapped)
        if c < subdomains:
            put(jnp.where(face_id == 0, subdomains, c), second)
            put(jnp.where(face_id == 0, c, subdomains), second_swapped)

    rows = packs[0].shape[0] - ROW_TILE
    block_ids = face_id * blocks_own + lax.broadcasted_iota(jnp.int32, (blocks_own, rows), 0)
    for at, s in enumerate(order):
        total = None
        for pack in packs[2 * at : 2 * at + 2]:
            slots = pack[rows:, :].astype(jnp.int32)[:1, :rows]
            part = jnp.dot(
                (slots == block_ids).astype(jnp.bfloat16), pack[:rows, :], preferred_element_type=jnp.float32
            )
            total = part if total is None else total + part
        weight_ref[s] = total

    tile_blocks = blocks_own // tiles
    copies = []
    for tile in range(tiles):
        at = slice(tile * tile_blocks, (tile + 1) * tile_blocks)
        values = pumped_ref[at].astype(jnp.float32)
        for s in range(subdomains):
            scaled = (values * weight_ref[s, at][:, None, :]).astype(jnp.bfloat16)
            scaled_ref[tile % 2, :, s * dof_count : (s + 1) * dof_count] = scaled.reshape(
                tile_blocks * columns, dof_count
            )
        total = jnp.dot(
            scaled_ref[tile % 2],
            basis_ref[: subdomains * dof_count, :],
            preferred_element_type=jnp.float32,
        )
        result = jnp.dot(
            total.astype(jnp.bfloat16), projection_ref[...], preferred_element_type=jnp.float32
        )
        out_ref[at] = result.reshape(tile_blocks, columns, dof_count)
        copies.append(pltpu.make_async_copy(out_ref.at[at], result_ref.at[at], sems.at[tile]))
        copies[-1].start()
    for copy in copies:
        copy.wait()


def on_device(
    mortar_in, pump_rate, well_cell, face_owner, face_slot, face_scale, section, basis, projection
):
    blocks_dev, cols_dev, dof_count = mortar_in.shape
    faces_dev = face_slot.shape[0]
    subdomains, halves = lax.axis_size("sub"), lax.axis_size("face")
    blocks_own = blocks_dev // halves
    capacity = max(2, 2 * faces_dev // subdomains)
    pack_rows = -(-capacity // ROW_TILE) * ROW_TILE + ROW_TILE

    *packs, pumped = pl.pallas_call(
        functools.partial(prepare_kernel, subdomains),
        out_shape=[jax.ShapeDtypeStruct((pack_rows, dof_count), jnp.bfloat16)] * subdomains
        + [jax.ShapeDtypeStruct((blocks_own, cols_dev, dof_count), jnp.bfloat16)],
        in_specs=[HBM] * 4 + [SMEM] * 3,
        out_specs=[VMEM] * (subdomains + 1),
        scratch_shapes=[
            pltpu.VMEM((1, faces_dev), jnp.int32),
            pltpu.VMEM((1, faces_dev), jnp.int32),
            pltpu.VMEM((faces_dev, dof_count), jnp.bfloat16),
            pltpu.SemaphoreType.DMA((4,)),
        ],
        compiler_params=pltpu.CompilerParams(vmem_limit_bytes=PREPARE_VMEM * MIB),
        cost_estimate=pl.CostEstimate(flops=4_000_000_000, bytes_accessed=8 * MIB, transcendentals=0),
        name="prepare",
    )(
        mortar_in,
        face_owner.reshape(1, faces_dev),
        face_slot.reshape(1, faces_dev),
        face_scale,
        pump_rate,
        well_cell,
        section,
    )

    def flat(sub, face):
        return (sub % subdomains) * halves + face

    swap = [(i, i ^ 1) for i in range(halves)]
    shifts = list(range(1, subdomains))
    if len(shifts) > 1:
        shifts[0], shifts[1] = shifts[1], shifts[0]
    groups = [tuple(shifts[i : i + 3]) for i in range(0, len(shifts), 3)]
    groups = [g + (subdomains,) * (3 - len(g)) for g in groups]
    moved = []
    for a, b, c in groups:
        for send in [(0, a), (1, b)], [(1, c)]:
            pairs = [
                (flat(s, face), flat(s + shift, face))
                for s in range(subdomains)
                for face, shift in send
                if shift < subdomains
            ]
            moved.append(lax.ppermute(basis, ("sub", "face"), pairs) if pairs else basis)
    weights = [packs[0]]
    for shift in shifts:
        ring = [(i, (i + shift) % subdomains) for i in range(subdomains)]
        weights.append(lax.ppermute(packs[shift], "sub", ring))
    own_swapped = lax.ppermute(packs[0], "face", swap)
    moved, weights = lax.optimization_barrier((moved, weights))
    bases, pairs = [], [packs[0], own_swapped]
    for array in moved:
        bases += [array, lax.ppermute(array, "face", swap)]
    for array in weights[1:]:
        pairs += [array, lax.ppermute(array, "face", swap)]
    order = [0] + shifts

    tiles = 4
    operands = [pumped, projection, basis, *bases, *pairs]
    return pl.pallas_call(
        functools.partial(apply_kernel, order, groups, tiles),
        out_shape=jax.ShapeDtypeStruct((blocks_own, cols_dev, dof_count), jnp.float32),
        in_specs=[VMEM] * len(operands),
        out_specs=HBM,
        scratch_shapes=[
            pltpu.VMEM((subdomains, blocks_own, dof_count), jnp.float32),
            pltpu.VMEM(((subdomains + 1) * dof_count, dof_count), jnp.bfloat16),
            pltpu.VMEM((2, blocks_own // tiles * cols_dev, subdomains * dof_count), jnp.bfloat16),
            pltpu.VMEM((blocks_own, cols_dev, dof_count), jnp.float32),
            pltpu.SemaphoreType.DMA((tiles,)),
        ],
        compiler_params=pltpu.CompilerParams(vmem_limit_bytes=48 * MIB),
        name="apply_blocks",
    )(*operands)


def solution(mesh):
    in_specs = (
        P(("groups", "sub"), "rhs", None),
        P(("groups", "rhs")),
        P(("groups", "rhs")),
        P(("groups", "sub", "face"), None),
        P(("groups", "sub", "face")),
        P(("groups", "sub", "face"), None),
        P(("groups", "sub")),
        P(("groups", "sub"), None, None),
        P(),
    )
    out_specs = P(("groups", "sub", "face"), "rhs", None)
    return jax.shard_map(
        on_device, mesh=mesh, in_specs=in_specs, out_specs=out_specs, check_vma=False
    )
```

```python
import functools

import jax
import jax.numpy as jnp
from jax import lax
from jax.experimental import pallas as pl
from jax.experimental.pallas import tpu as pltpu
from jax.sharding import PartitionSpec as P

ROW_TILE = 16
VMEM = pl.BlockSpec(memory_space=pltpu.VMEM)
HBM = pl.BlockSpec(memory_space=pltpu.HBM)
SMEM = pl.BlockSpec(memory_space=pltpu.SMEM)
MIB = 1024 * 1024


def pack_kernel(owner_ref, slot_ref, scale_ref, section_ref, packs_ref):
    subdomains, rows, dof_count = packs_ref.shape
    rows -= ROW_TILE
    faces = owner_ref.shape[1]
    sign = (1 - 2 * section_ref[0]).astype(jnp.float32)
    named = lax.broadcasted_iota(jnp.int32, (subdomains, faces), 0) == owner_ref[...]
    earlier = lax.broadcasted_iota(jnp.int32, (faces, faces), 0) < lax.broadcasted_iota(
        jnp.int32, (faces, faces), 1
    )
    rank = jnp.dot(
        named.astype(jnp.bfloat16), earlier.astype(jnp.bfloat16), preferred_element_type=jnp.float32
    )
    place = jnp.where(named, rank.astype(jnp.int32), -1)
    slots = slot_ref[...].astype(jnp.bfloat16)
    for owner in range(subdomains):
        hit = place[owner : owner + 1, :] == lax.broadcasted_iota(jnp.int32, (rows, faces), 0)
        hit = hit.astype(jnp.bfloat16)
        packed = jnp.dot(hit, scale_ref[...], preferred_element_type=jnp.float32) * sign
        listed = lax.dot_general(
            slots, hit, (((1,), (1,)), ((), ())), preferred_element_type=jnp.float32
        )
        meta = jnp.concatenate([listed, jnp.zeros((1, dof_count - rows), jnp.float32)], axis=1)
        meta = jnp.broadcast_to(meta, (ROW_TILE, dof_count))
        packs_ref[owner, :rows, :] = packed.astype(jnp.bfloat16)
        packs_ref[owner, rows:, :] = meta.astype(jnp.bfloat16)


def apply_kernel(groups, tiles, *refs):
    pumped_ref, projection_ref, own_ref = refs[:3]
    bases, refs = refs[3 : 3 + 4 * len(groups)], refs[3 + 4 * len(groups) :]
    packs, (result_ref, weight_ref, basis_ref, scaled_ref, out_ref, sems) = refs[:2], refs[2:]
    blocks_own, columns, dof_count = pumped_ref.shape
    subdomains = weight_ref.shape[0]
    face_id = lax.axis_index("face")
    sub_id = lax.axis_index("sub")

    def put(shift, array):
        source = jnp.where(shift < subdomains, lax.rem(sub_id + subdomains - shift, subdomains), subdomains)
        basis_ref[pl.ds(pl.multiple_of(source * dof_count, dof_count), dof_count), :] = array[0]

    put(jnp.int32(0), own_ref)
    for at, (a, b, c) in enumerate(groups):
        first, first_swapped, second, second_swapped = bases[4 * at : 4 * at + 4]
        put(jnp.where(face_id == 0, a, b), first)
        put(jnp.where(face_id == 0, b, a), first_swapped)
        if c < subdomains:
            put(jnp.where(face_id == 0, subdomains, c), second)
            put(jnp.where(face_id == 0, c, subdomains), second_swapped)

    rows = packs[0].shape[1] - ROW_TILE
    block_ids = face_id * blocks_own + lax.broadcasted_iota(jnp.int32, (blocks_own, rows), 0)
    for s in range(subdomains):
        total = None
        for pack in packs:
            slots = pack[s, rows:, :].astype(jnp.int32)[:1, :rows]
            part = jnp.dot(
                (slots == block_ids).astype(jnp.bfloat16), pack[s, :rows, :], preferred_element_type=jnp.float32
            )
            total = part if total is None else total + part
        weight_ref[s] = total

    tile_blocks = blocks_own // tiles
    copies = []
    for tile in range(tiles):
        at = slice(tile * tile_blocks, (tile + 1) * tile_blocks)
        values = pumped_ref[at].astype(jnp.float32)
        for s in range(subdomains):
            scaled = (values * weight_ref[s, at][:, None, :]).astype(jnp.bfloat16)
            scaled_ref[tile % 2, :, s * dof_count : (s + 1) * dof_count] = scaled.reshape(
                tile_blocks * columns, dof_count
            )
        total = jnp.dot(
            scaled_ref[tile % 2],
            basis_ref[: subdomains * dof_count, :],
            preferred_element_type=jnp.float32,
        )
        result = jnp.dot(
            total.astype(jnp.bfloat16), projection_ref[...], preferred_element_type=jnp.float32
        )
        out_ref[at] = result.reshape(tile_blocks, columns, dof_count)
        copies.append(pltpu.make_async_copy(out_ref.at[at], result_ref.at[at], sems.at[tile]))
        copies[-1].start()
    for copy in copies:
        copy.wait()


def on_device(
    mortar_in, pump_rate, well_cell, face_owner, face_slot, face_scale, section, basis, projection
):
    blocks_dev, cols_dev, dof_count = mortar_in.shape
    faces_dev = face_slot.shape[0]
    subdomains, halves = lax.axis_size("sub"), lax.axis_size("face")
    blocks_own = blocks_dev // halves
    capacity = max(2, 2 * faces_dev // subdomains)
    pack_rows = -(-capacity // ROW_TILE) * ROW_TILE + ROW_TILE

    packs = pl.pallas_call(
        pack_kernel,
        out_shape=jax.ShapeDtypeStruct((subdomains, pack_rows, dof_count), jnp.bfloat16),
        in_specs=[VMEM, VMEM, VMEM, SMEM],
        out_specs=VMEM,
        cost_estimate=pl.CostEstimate(flops=4_000_000_000, bytes_accessed=8 * MIB, transcendentals=0),
        name="pack_weights",
    )(face_owner.reshape(1, faces_dev), face_slot.reshape(1, faces_dev), face_scale, section)

    first_block = lax.axis_index("face") * blocks_own
    mine = lax.dynamic_slice_in_dim(mortar_in, first_block, blocks_own, 0)
    block_ids = lax.axis_index("sub") * blocks_dev + first_block + jnp.arange(blocks_own, dtype=jnp.int32)
    cell = block_ids[:, None, None] * dof_count + jnp.arange(dof_count, dtype=jnp.int32)[None, None, :]
    wells = jnp.where(cell == well_cell[None, :, None], pump_rate[None, :, None], 0.0)
    pumped = (mine.astype(jnp.float32) + wells).astype(jnp.bfloat16)

    def flat(sub, face):
        return (sub % subdomains) * halves + face

    swap = [(i, i ^ 1) for i in range(halves)]
    shifts = list(range(1, subdomains))
    if len(shifts) > 1:
        shifts[0], shifts[1] = shifts[1], shifts[0]
    groups = [tuple(shifts[i : i + 3]) for i in range(0, len(shifts), 3)]
    groups = [g + (subdomains,) * (3 - len(g)) for g in groups]
    moved = []
    for a, b, c in groups:
        for send in [(0, a), (1, b)], [(1, c)]:
            pairs = [
                (flat(s, face), flat(s + shift, face))
                for s in range(subdomains)
                for face, shift in send
                if shift < subdomains
            ]
            moved.append(lax.ppermute(basis, ("sub", "face"), pairs) if pairs else basis)
    weights = lax.all_to_all(packs, "sub", split_axis=0, concat_axis=0, tiled=True)
    moved, pumped = lax.optimization_barrier((moved, pumped))
    bases = []
    for array in moved:
        bases += [array, lax.ppermute(array, "face", swap)]

    tiles = 4
    operands = [pumped, projection, basis, *bases, weights, lax.ppermute(weights, "face", swap)]
    return pl.pallas_call(
        functools.partial(apply_kernel, groups, tiles),
        out_shape=jax.ShapeDtypeStruct((blocks_own, cols_dev, dof_count), jnp.float32),
        in_specs=[VMEM] * len(operands),
        out_specs=HBM,
        scratch_shapes=[
            pltpu.VMEM((subdomains, blocks_own, dof_count), jnp.float32),
            pltpu.VMEM(((subdomains + 1) * dof_count, dof_count), jnp.bfloat16),
            pltpu.VMEM((2, blocks_own // tiles * cols_dev, subdomains * dof_count), jnp.bfloat16),
            pltpu.VMEM((blocks_own, cols_dev, dof_count), jnp.float32),
            pltpu.SemaphoreType.DMA((tiles,)),
        ],
        compiler_params=pltpu.CompilerParams(vmem_limit_bytes=48 * MIB),
        name="apply_blocks",
    )(*operands)


def solution(mesh):
    in_specs = (
        P(("groups", "sub"), "rhs", None),
        P(("groups", "rhs")),
        P(("groups", "rhs")),
        P(("groups", "sub", "face"), None),
        P(("groups", "sub", "face")),
        P(("groups", "sub", "face"), None),
        P(("groups", "sub")),
        P(("groups", "sub"), None, None),
        P(),
    )
    out_specs = P(("groups", "sub", "face"), "rhs", None)
    return jax.shard_map(
        on_device, mesh=mesh, in_specs=in_specs, out_specs=out_specs, check_vma=False
    )
```

```python
import functools

import jax
import jax.numpy as jnp
from jax import lax
from jax.experimental import pallas as pl
from jax.experimental.pallas import tpu as pltpu
from jax.sharding import PartitionSpec as P

ROW_TILE = 16
VMEM = pl.BlockSpec(memory_space=pltpu.VMEM)
HBM = pl.BlockSpec(memory_space=pltpu.HBM)
SMEM = pl.BlockSpec(memory_space=pltpu.SMEM)
MIB = 1024 * 1024
TILES = 4


def pack_kernel(owner_ref, slot_ref, scale_ref, section_ref, *packs):
    subdomains = len(packs)
    rows, dof_count = packs[0].shape
    rows -= ROW_TILE
    faces = owner_ref.shape[1]
    sign = (1 - 2 * section_ref[...]).astype(jnp.float32)
    shifts = lax.broadcasted_iota(jnp.int32, (subdomains, faces), 0)
    named = lax.rem(lax.axis_index("sub") + shifts, subdomains) == owner_ref[...]
    earlier = lax.broadcasted_iota(jnp.int32, (faces, faces), 0) < lax.broadcasted_iota(
        jnp.int32, (faces, faces), 1
    )
    rank = jnp.dot(
        named.astype(jnp.bfloat16), earlier.astype(jnp.bfloat16), preferred_element_type=jnp.float32
    )
    place = jnp.where(named, rank.astype(jnp.int32), -1)
    slots = slot_ref[...].astype(jnp.bfloat16)
    for shift, pack_ref in enumerate(packs):
        hit = place[shift : shift + 1, :] == lax.broadcasted_iota(jnp.int32, (rows, faces), 0)
        hit = hit.astype(jnp.bfloat16)
        packed = jnp.dot(hit, scale_ref[...], preferred_element_type=jnp.float32) * sign
        listed = lax.dot_general(
            slots, hit, (((1,), (1,)), ((), ())), preferred_element_type=jnp.float32
        )
        meta = jnp.concatenate([listed, jnp.zeros((1, dof_count - rows), jnp.float32)], axis=1)
        meta = jnp.broadcast_to(meta, (ROW_TILE, dof_count))
        pack_ref[:rows, :] = packed.astype(jnp.bfloat16)
        pack_ref[rows:, :] = meta.astype(jnp.bfloat16)


def block_weights(packs, blocks_own):
    rows = packs[0].shape[0] - ROW_TILE
    first = lax.axis_index("face") * blocks_own
    block_ids = first + lax.broadcasted_iota(jnp.int32, (blocks_own, rows), 0)
    total = None
    for pack in packs:
        slots = pack[rows:, :].astype(jnp.int32)[:1, :rows]
        hit = (slots == block_ids).astype(jnp.bfloat16)
        part = jnp.dot(hit, pack[:rows, :], preferred_element_type=jnp.float32)
        total = part if total is None else total + part
    return total


def own_kernel(mortar_ref, rate_ref, cell_ref, basis_ref, pack_ref, swapped_ref, pumped_ref, sum_ref, weight_ref, sem):
    blocks_own, columns, dof_count = pumped_ref.shape
    first_block = lax.axis_index("face") * blocks_own
    fetch = pltpu.make_async_copy(mortar_ref.at[pl.ds(first_block, blocks_own)], pumped_ref, sem)
    fetch.start()
    weight_ref[...] = block_weights((pack_ref, swapped_ref), blocks_own)
    fetch.wait()

    base = lax.axis_index("sub") * mortar_ref.shape[0] + first_block
    for column in range(columns):
        block = lax.div(cell_ref[column], dof_count) - base
        dof = lax.rem(cell_ref[column], dof_count)

        @pl.when((block >= 0) & (block < blocks_own))
        def _():
            slab = slice(column // ROW_TILE * ROW_TILE, (column // ROW_TILE + 1) * ROW_TILE)
            shape = (ROW_TILE, dof_count)
            at_well = (lax.broadcasted_iota(jnp.int32, shape, 0) == column % ROW_TILE) & (
                lax.broadcasted_iota(jnp.int32, shape, 1) == dof
            )
            well = jnp.where(at_well, rate_ref[column], 0.0)
            pumped_ref[block, slab, :] = (pumped_ref[block, slab, :].astype(jnp.float32) + well).astype(
                jnp.bfloat16
            )

    tile_blocks = blocks_own // TILES
    for tile in range(TILES):
        at = slice(tile * tile_blocks, (tile + 1) * tile_blocks)
        scaled = (pumped_ref[at].astype(jnp.float32) * weight_ref[at][:, None, :]).astype(jnp.bfloat16)
        flux = jnp.dot(
            scaled.reshape(tile_blocks * columns, dof_count), basis_ref[0], preferred_element_type=jnp.float32
        )
        sum_ref[at] = flux.reshape(tile_blocks, columns, dof_count)


def apply_kernel(groups, *refs):
    pumped_ref, sum_ref, projection_ref = refs[:3]
    bases, refs = refs[3 : 3 + 4 * len(groups)], refs[3 + 4 * len(groups) :]
    packs, (result_ref, weight_ref, basis_ref, scaled_ref, out_ref, sems) = refs[:-6], refs[-6:]
    blocks_own, columns, dof_count = pumped_ref.shape
    others = weight_ref.shape[0]
    lane = 2 * lax.rem(lax.axis_index("rhs"), 2) + lax.axis_index("face")

    def put(array, *by_lane):
        shift = jnp.int32(by_lane[3])
        for which in range(3):
            shift = jnp.where(lane == which, by_lane[which], shift)
        at = pl.multiple_of((shift - 1) * dof_count, dof_count)
        basis_ref[pl.ds(at, dof_count), :] = array[0]

    spare = others + 1
    for at, (a, b, c) in enumerate(groups):
        first, first_swapped, second, second_swapped = bases[4 * at : 4 * at + 4]
        put(first, a, spare, b, c)
        put(second, b, c, a, spare)
        put(first_swapped, spare, a, c, b)
        put(second_swapped, c, b, spare, a)
    for other in range(others):
        weight_ref[other] = block_weights(packs[2 * other : 2 * other + 2], blocks_own)

    tile_blocks = blocks_own // TILES
    copies = []
    for tile in range(TILES):
        at = slice(tile * tile_blocks, (tile + 1) * tile_blocks)
        values = pumped_ref[at].astype(jnp.float32)
        for other in range(others):
            scaled = (values * weight_ref[other, at][:, None, :]).astype(jnp.bfloat16)
            scaled_ref[tile % 2, :, other * dof_count : (other + 1) * dof_count] = scaled.reshape(
                tile_blocks * columns, dof_count
            )
        total = jnp.dot(
            scaled_ref[tile % 2], basis_ref[: others * dof_count, :], preferred_element_type=jnp.float32
        )
        total = total + sum_ref[at].reshape(tile_blocks * columns, dof_count)
        result = jnp.dot(
            total.astype(jnp.bfloat16), projection_ref[...], preferred_element_type=jnp.float32
        )
        out_ref[at] = result.reshape(tile_blocks, columns, dof_count)
        copies.append(pltpu.make_async_copy(out_ref.at[at], result_ref.at[at], sems.at[tile]))
        copies[-1].start()
    for copy in copies:
        copy.wait()


def on_device(
    mortar_in, pump_rate, well_cell, face_owner, face_slot, face_scale, section, basis, projection
):
    blocks_dev, cols_dev, dof_count = mortar_in.shape
    faces_dev = face_slot.shape[0]
    subdomains, rights, halves = lax.axis_size("sub"), lax.axis_size("rhs"), lax.axis_size("face")
    others = subdomains - 1
    blocks_own = blocks_dev // halves
    capacity = max(2, 2 * faces_dev // subdomains)
    pack_rows = -(-capacity // ROW_TILE) * ROW_TILE + ROW_TILE
    block_shape = (blocks_own, cols_dev, dof_count)

    def flat(sub, right, face):
        return ((sub % subdomains) * rights + right) * halves + face

    cells = [(s, r) for s in range(subdomains) for r in range(rights)]
    cross = [(i, i ^ 1) for i in range(rights)]
    swap = [(i, i ^ 1) for i in range(halves)]
    shifts = list(range(1, subdomains))
    if len(shifts) > 1:
        shifts[0], shifts[1] = shifts[1], shifts[0]
    groups = [tuple(shifts[i : i + 3]) for i in range(0, len(shifts), 3)]
    groups = [g + (subdomains,) * (3 - len(g)) for g in groups]
    firsts = []
    for a, b, c in groups:
        pairs = []
        for s, r in cells:
            for face, shift in ((0, b), (1, c)) if r % 2 else ((0, a),):
                if shift < subdomains:
                    pairs.append((flat(s, r, face), flat(s + shift, r, face)))
        firsts.append(lax.ppermute(basis, ("sub", "rhs", "face"), pairs))

    packs = pl.pallas_call(
        pack_kernel,
        out_shape=[jax.ShapeDtypeStruct((pack_rows, dof_count), jnp.bfloat16)] * subdomains,
        in_specs=[VMEM] * 4,
        out_specs=[VMEM] * subdomains,
        cost_estimate=pl.CostEstimate(flops=4_000_000_000, bytes_accessed=8 * MIB, transcendentals=0),
        name="pack_weights",
    )(
        face_owner.reshape(1, faces_dev),
        face_slot.reshape(1, faces_dev),
        face_scale,
        section.reshape(1, 1),
    )
    arrived = []
    for shift in range(1, subdomains):
        ring = [(i, (i + shift) % subdomains) for i in range(subdomains)]
        arrived.append(lax.ppermute(packs[shift], "sub", ring))
    own_swapped = lax.ppermute(packs[0], "face", swap)

    firsts, own_pack = lax.optimization_barrier((firsts, packs[0]))
    pumped, own_sum = pl.pallas_call(
        own_kernel,
        out_shape=[
            jax.ShapeDtypeStruct(block_shape, jnp.bfloat16),
            jax.ShapeDtypeStruct(block_shape, jnp.float32),
        ],
        in_specs=[HBM, SMEM, SMEM, VMEM, VMEM, VMEM],
        out_specs=[VMEM, VMEM],
        scratch_shapes=[pltpu.VMEM((blocks_own, dof_count), jnp.float32), pltpu.SemaphoreType.DMA(())],
        compiler_params=pltpu.CompilerParams(vmem_limit_bytes=32 * MIB),
        cost_estimate=pl.CostEstimate(flops=2_000_000_000, bytes_accessed=8 * MIB, transcendentals=0),
        name="own_blocks",
    )(mortar_in, pump_rate, well_cell, basis, own_pack, own_swapped)

    arrived, pumped = lax.optimization_barrier((arrived, pumped))
    weights = []
    for array in arrived:
        weights += [array, lax.ppermute(array, "face", swap)]

    bases = []
    for first in firsts:
        second = lax.ppermute(first, "rhs", cross)
        bases += [first, lax.ppermute(first, "face", swap), second, lax.ppermute(second, "face", swap)]

    operands = [pumped, own_sum, projection, *bases, *weights]
    return pl.pallas_call(
        functools.partial(apply_kernel, groups),
        out_shape=jax.ShapeDtypeStruct(block_shape, jnp.float32),
        in_specs=[VMEM] * len(operands),
        out_specs=HBM,
        scratch_shapes=[
            pltpu.VMEM((others, blocks_own, dof_count), jnp.float32),
            pltpu.VMEM(((others + 1) * dof_count, dof_count), jnp.bfloat16),
            pltpu.VMEM((2, blocks_own // TILES * cols_dev, others * dof_count), jnp.bfloat16),
            pltpu.VMEM(block_shape, jnp.float32),
            pltpu.SemaphoreType.DMA((TILES,)),
        ],
        compiler_params=pltpu.CompilerParams(vmem_limit_bytes=48 * MIB),
        name="apply_blocks",
    )(*operands)


def solution(mesh):
    in_specs = (
        P(("groups", "sub"), "rhs", None),
        P(("groups", "rhs")),
        P(("groups", "rhs")),
        P(("groups", "sub", "face"), None),
        P(("groups", "sub", "face")),
        P(("groups", "sub", "face"), None),
        P(("groups", "sub")),
        P(("groups", "sub"), None, None),
        P(),
    )
    out_specs = P(("groups", "sub", "face"), "rhs", None)
    return jax.shard_map(
        on_device, mesh=mesh, in_specs=in_specs, out_specs=out_specs, check_vma=False
    )
```

```python
import functools

import jax
import jax.numpy as jnp
from jax import lax
from jax.experimental import pallas as pl
from jax.experimental.pallas import tpu as pltpu
from jax.sharding import PartitionSpec as P

ROW_TILE = 16
VMEM = pl.BlockSpec(memory_space=pltpu.VMEM)
HBM = pl.BlockSpec(memory_space=pltpu.HBM)
SMEM = pl.BlockSpec(memory_space=pltpu.SMEM)
MIB = 1024 * 1024
TILES = 4


def pack_kernel(owner_ref, slot_ref, scale_ref, section_any, packs_ref, own_ref, section_ref, sem):
    fetch = pltpu.make_async_copy(section_any, section_ref, sem)
    fetch.start()
    subdomains, rows, dof_count = packs_ref.shape
    rows -= ROW_TILE
    faces = owner_ref.shape[1]
    named = lax.broadcasted_iota(jnp.int32, (subdomains, faces), 0) == owner_ref[...]
    earlier = lax.broadcasted_iota(jnp.int32, (faces, faces), 0) < lax.broadcasted_iota(
        jnp.int32, (faces, faces), 1
    )
    rank = jnp.dot(
        named.astype(jnp.bfloat16), earlier.astype(jnp.bfloat16), preferred_element_type=jnp.float32
    )
    place = jnp.where(named, rank.astype(jnp.int32), -1)
    slots = slot_ref[...].astype(jnp.bfloat16)
    fetch.wait()
    sign = (1 - 2 * section_ref[0]).astype(jnp.float32)
    for owner in range(subdomains):
        hit = place[owner : owner + 1, :] == lax.broadcasted_iota(jnp.int32, (rows, faces), 0)
        hit = hit.astype(jnp.bfloat16)
        packed = jnp.dot(hit, scale_ref[...], preferred_element_type=jnp.float32) * sign
        listed = lax.dot_general(
            slots, hit, (((1,), (1,)), ((), ())), preferred_element_type=jnp.float32
        )
        meta = jnp.concatenate([listed, jnp.zeros((1, dof_count - rows), jnp.float32)], axis=1)
        meta = jnp.broadcast_to(meta, (ROW_TILE, dof_count))
        packs_ref[owner, :rows, :] = packed.astype(jnp.bfloat16)
        packs_ref[owner, rows:, :] = meta.astype(jnp.bfloat16)
    own_ref[...] = packs_ref[lax.axis_index("sub")]


def block_weights(packs, blocks_own):
    rows = packs[0].shape[0] - ROW_TILE
    first = lax.axis_index("face") * blocks_own
    block_ids = first + lax.broadcasted_iota(jnp.int32, (blocks_own, rows), 0)
    total = None
    for pack in packs:
        slots = pack[rows:, :].astype(jnp.int32)[:1, :rows]
        hit = (slots == block_ids).astype(jnp.bfloat16)
        part = jnp.dot(hit, pack[:rows, :], preferred_element_type=jnp.float32)
        total = part if total is None else total + part
    return total


def own_kernel(mortar_ref, rate_ref, cell_ref, basis_ref, pack_ref, swapped_ref, pumped_ref, sum_ref, weight_ref, sem):
    blocks_own, columns, dof_count = pumped_ref.shape
    first_block = lax.axis_index("face") * blocks_own
    fetch = pltpu.make_async_copy(mortar_ref.at[pl.ds(first_block, blocks_own)], pumped_ref, sem)
    fetch.start()
    weight_ref[...] = block_weights((pack_ref, swapped_ref), blocks_own)
    fetch.wait()

    base = lax.axis_index("sub") * mortar_ref.shape[0] + first_block
    for column in range(columns):
        block = lax.div(cell_ref[column], dof_count) - base
        dof = lax.rem(cell_ref[column], dof_count)

        @pl.when((block >= 0) & (block < blocks_own))
        def _():
            slab = slice(column // ROW_TILE * ROW_TILE, (column // ROW_TILE + 1) * ROW_TILE)
            shape = (ROW_TILE, dof_count)
            at_well = (lax.broadcasted_iota(jnp.int32, shape, 0) == column % ROW_TILE) & (
                lax.broadcasted_iota(jnp.int32, shape, 1) == dof
            )
            well = jnp.where(at_well, rate_ref[column], 0.0)
            pumped_ref[block, slab, :] = (pumped_ref[block, slab, :].astype(jnp.float32) + well).astype(
                jnp.bfloat16
            )

    tile_blocks = blocks_own // TILES
    for tile in range(TILES):
        at = slice(tile * tile_blocks, (tile + 1) * tile_blocks)
        scaled = (pumped_ref[at].astype(jnp.float32) * weight_ref[at][:, None, :]).astype(jnp.bfloat16)
        flux = jnp.dot(
            scaled.reshape(tile_blocks * columns, dof_count), basis_ref[0], preferred_element_type=jnp.float32
        )
        sum_ref[at] = flux.reshape(tile_blocks, columns, dof_count)


def apply_kernel(groups, *refs):
    pumped_ref, sum_ref, projection_ref = refs[:3]
    bases, refs = refs[3 : 3 + 4 * len(groups)], refs[3 + 4 * len(groups) :]
    arrived_ref, swapped_ref, result_ref, weight_ref, basis_ref, scaled_ref, out_ref, sems = refs
    blocks_own, columns, dof_count = pumped_ref.shape
    others = weight_ref.shape[0]
    lane = 2 * lax.rem(lax.axis_index("rhs"), 2) + lax.axis_index("face")

    def put(array, *by_lane):
        shift = jnp.int32(by_lane[3])
        for which in range(3):
            shift = jnp.where(lane == which, by_lane[which], shift)
        at = pl.multiple_of((shift - 1) * dof_count, dof_count)
        basis_ref[pl.ds(at, dof_count), :] = array[0]

    spare = others + 1
    for at, (a, b, c) in enumerate(groups):
        first, first_swapped, second, second_swapped = bases[4 * at : 4 * at + 4]
        put(first, a, spare, b, c)
        put(second, b, c, a, spare)
        put(first_swapped, spare, a, c, b)
        put(second_swapped, c, b, spare, a)
    for other in range(others):
        source = lax.rem(lax.axis_index("sub") + others - other, others + 1)
        weight_ref[other] = block_weights((arrived_ref.at[source], swapped_ref.at[source]), blocks_own)

    tile_blocks = blocks_own // TILES
    copies = []
    for tile in range(TILES):
        at = slice(tile * tile_blocks, (tile + 1) * tile_blocks)
        values = pumped_ref[at].astype(jnp.float32)
        for other in range(others):
            scaled = (values * weight_ref[other, at][:, None, :]).astype(jnp.bfloat16)
            scaled_ref[tile % 2, :, other * dof_count : (other + 1) * dof_count] = scaled.reshape(
                tile_blocks * columns, dof_count
            )
        total = jnp.dot(
            scaled_ref[tile % 2], basis_ref[: others * dof_count, :], preferred_element_type=jnp.float32
        )
        total = total + sum_ref[at].reshape(tile_blocks * columns, dof_count)
        result = jnp.dot(
            total.astype(jnp.bfloat16), projection_ref[...], preferred_element_type=jnp.float32
        )
        out_ref[at] = result.reshape(tile_blocks, columns, dof_count)
        copies.append(pltpu.make_async_copy(out_ref.at[at], result_ref.at[at], sems.at[tile]))
        copies[-1].start()
    for copy in copies:
        copy.wait()


def on_device(
    mortar_in, pump_rate, well_cell, face_owner, face_slot, face_scale, section, basis, projection
):
    blocks_dev, cols_dev, dof_count = mortar_in.shape
    faces_dev = face_slot.shape[0]
    subdomains, rights, halves = lax.axis_size("sub"), lax.axis_size("rhs"), lax.axis_size("face")
    others = subdomains - 1
    blocks_own = blocks_dev // halves
    capacity = max(2, 2 * faces_dev // subdomains)
    pack_rows = -(-capacity // ROW_TILE) * ROW_TILE + ROW_TILE
    block_shape = (blocks_own, cols_dev, dof_count)

    def flat(sub, right, face):
        return ((sub % subdomains) * rights + right) * halves + face

    cells = [(s, r) for s in range(subdomains) for r in range(rights)]
    cross = [(i, i ^ 1) for i in range(rights)]
    swap = [(i, i ^ 1) for i in range(halves)]
    shifts = list(range(1, subdomains))
    if len(shifts) > 1:
        shifts[0], shifts[1] = shifts[1], shifts[0]
    groups = [tuple(shifts[i : i + 3]) for i in range(0, len(shifts), 3)]
    groups = [g + (subdomains,) * (3 - len(g)) for g in groups]
    firsts = []
    for a, b, c in groups:
        pairs = []
        for s, r in cells:
            for face, shift in ((0, b), (1, c)) if r % 2 else ((0, a), (1, subdomains)):
                pairs.append((flat(s, r, face), flat(s + shift, r, face)))
        firsts.append(lax.ppermute(basis, ("sub", "rhs", "face"), pairs))

    packs, own_pack = pl.pallas_call(
        pack_kernel,
        out_shape=[
            jax.ShapeDtypeStruct((subdomains, pack_rows, dof_count), jnp.bfloat16),
            jax.ShapeDtypeStruct((pack_rows, dof_count), jnp.bfloat16),
        ],
        in_specs=[VMEM, VMEM, VMEM, HBM],
        out_specs=[VMEM, VMEM],
        scratch_shapes=[pltpu.SMEM((1,), jnp.int32), pltpu.SemaphoreType.DMA(())],
        cost_estimate=pl.CostEstimate(flops=4_000_000_000, bytes_accessed=8 * MIB, transcendentals=0),
        name="pack_weights",
    )(face_owner.reshape(1, faces_dev), face_slot.reshape(1, faces_dev), face_scale, section)
    arrived = lax.all_to_all(packs, "sub", split_axis=0, concat_axis=0, tiled=True)
    own_swapped = lax.ppermute(own_pack, "face", swap)

    firsts, own_pack = lax.optimization_barrier((firsts, own_pack))
    pumped, own_sum = pl.pallas_call(
        own_kernel,
        out_shape=[
            jax.ShapeDtypeStruct(block_shape, jnp.bfloat16),
            jax.ShapeDtypeStruct(block_shape, jnp.float32),
        ],
        in_specs=[HBM, SMEM, SMEM, VMEM, VMEM, VMEM],
        out_specs=[VMEM, VMEM],
        scratch_shapes=[pltpu.VMEM((blocks_own, dof_count), jnp.float32), pltpu.SemaphoreType.DMA(())],
        compiler_params=pltpu.CompilerParams(vmem_limit_bytes=32 * MIB),
        cost_estimate=pl.CostEstimate(flops=2_000_000_000, bytes_accessed=8 * MIB, transcendentals=0),
        name="own_blocks",
    )(mortar_in, pump_rate, well_cell, basis, own_pack, own_swapped)

    arrived, pumped = lax.optimization_barrier((arrived, pumped))
    swapped = lax.ppermute(arrived, "face", swap)

    bases = []
    for first in firsts:
        second = lax.ppermute(first, "rhs", cross)
        bases += [first, lax.ppermute(first, "face", swap), second, lax.ppermute(second, "face", swap)]

    operands = [pumped, own_sum, projection, *bases, arrived, swapped]
    return pl.pallas_call(
        functools.partial(apply_kernel, groups),
        out_shape=jax.ShapeDtypeStruct(block_shape, jnp.float32),
        in_specs=[VMEM] * len(operands),
        out_specs=HBM,
        scratch_shapes=[
            pltpu.VMEM((others, blocks_own, dof_count), jnp.float32),
            pltpu.VMEM(((others + 1) * dof_count, dof_count), jnp.bfloat16),
            pltpu.VMEM((2, blocks_own // TILES * cols_dev, others * dof_count), jnp.bfloat16),
            pltpu.VMEM(block_shape, jnp.float32),
            pltpu.SemaphoreType.DMA((TILES,)),
        ],
        compiler_params=pltpu.CompilerParams(vmem_limit_bytes=48 * MIB),
        name="apply_blocks",
    )(*operands)


def solution(mesh):
    in_specs = (
        P(("groups", "sub"), "rhs", None),
        P(("groups", "rhs")),
        P(("groups", "rhs")),
        P(("groups", "sub", "face"), None),
        P(("groups", "sub", "face")),
        P(("groups", "sub", "face"), None),
        P(("groups", "sub")),
        P(("groups", "sub"), None, None),
        P(),
    )
    out_specs = P(("groups", "sub", "face"), "rhs", None)
    return jax.shard_map(
        on_device, mesh=mesh, in_specs=in_specs, out_specs=out_specs, check_vma=False
    )
```

```python
import functools

import jax
import jax.numpy as jnp
from jax import lax
from jax.experimental import pallas as pl
from jax.experimental.pallas import tpu as pltpu
from jax.sharding import PartitionSpec as P

ROW_TILE = 16
VMEM = pl.BlockSpec(memory_space=pltpu.VMEM)
HBM = pl.BlockSpec(memory_space=pltpu.HBM)
SMEM = pl.BlockSpec(memory_space=pltpu.SMEM)
MIB = 1024 * 1024
TILES = 4


def pack_kernel(owner_ref, slot_ref, scale_ref, section_ref, *packs):
    subdomains = len(packs)
    rows, dof_count = packs[0].shape
    rows -= ROW_TILE
    faces = owner_ref.shape[1]
    sign = (1 - 2 * section_ref[0]).astype(jnp.float32)
    partners = lax.broadcasted_iota(jnp.int32, (subdomains, faces), 0)
    named = (lax.axis_index("sub") ^ partners) == owner_ref[...]
    earlier = lax.broadcasted_iota(jnp.int32, (faces, faces), 0) < lax.broadcasted_iota(
        jnp.int32, (faces, faces), 1
    )
    rank = jnp.dot(
        named.astype(jnp.bfloat16), earlier.astype(jnp.bfloat16), preferred_element_type=jnp.float32
    )
    place = jnp.where(named, rank.astype(jnp.int32), -1)
    slots = slot_ref[...].astype(jnp.bfloat16)
    for partner, pack_ref in enumerate(packs):
        hit = place[partner : partner + 1, :] == lax.broadcasted_iota(jnp.int32, (rows, faces), 0)
        hit = hit.astype(jnp.bfloat16)
        packed = jnp.dot(hit, scale_ref[...], preferred_element_type=jnp.float32) * sign
        listed = lax.dot_general(
            slots, hit, (((1,), (1,)), ((), ())), preferred_element_type=jnp.float32
        )
        meta = jnp.concatenate([listed, jnp.zeros((1, dof_count - rows), jnp.float32)], axis=1)
        meta = jnp.broadcast_to(meta, (ROW_TILE, dof_count))
        pack_ref[:rows, :] = packed.astype(jnp.bfloat16)
        pack_ref[rows:, :] = meta.astype(jnp.bfloat16)


def block_weights(packs, blocks_own):
    rows = packs[0].shape[0] - ROW_TILE
    first = lax.axis_index("face") * blocks_own
    block_ids = first + lax.broadcasted_iota(jnp.int32, (blocks_own, rows), 0)
    total = None
    for pack in packs:
        slots = pack[rows:, :].astype(jnp.int32)[:1, :rows]
        hit = (slots == block_ids).astype(jnp.bfloat16)
        part = jnp.dot(hit, pack[:rows, :], preferred_element_type=jnp.float32)
        total = part if total is None else total + part
    return total


def apply_kernel(groups, *refs):
    pumped_ref, projection_ref, own_ref = refs[:3]
    bases, refs = refs[3 : 3 + 4 * len(groups)], refs[3 + 4 * len(groups) :]
    packs, (result_ref, weight_ref, basis_ref, scaled_ref, out_ref, sems) = refs[:-6], refs[-6:]
    blocks_own, columns, dof_count = pumped_ref.shape
    subdomains = weight_ref.shape[0]
    lane = 2 * lax.rem(lax.axis_index("rhs"), 2) + lax.axis_index("face")

    def put(array, *by_lane):
        partner = jnp.int32(by_lane[3])
        for which in range(3):
            partner = jnp.where(lane == which, by_lane[which], partner)
        basis_ref[pl.ds(pl.multiple_of(partner * dof_count, dof_count), dof_count), :] = array[0]

    basis_ref[:dof_count, :] = own_ref[0]
    for at, (a, b, c) in enumerate(groups):
        first, first_swapped, second, second_swapped = bases[4 * at : 4 * at + 4]
        put(first, a, c, b, c)
        put(second, c, b, c, a)
        put(first_swapped, c, a, c, b)
        put(second_swapped, b, c, a, c)
    for partner in range(subdomains):
        weight_ref[partner] = block_weights(packs[2 * partner : 2 * partner + 2], blocks_own)

    tile_blocks = blocks_own // TILES
    copies = []
    for tile in range(TILES):
        at = slice(tile * tile_blocks, (tile + 1) * tile_blocks)
        values = pumped_ref[at].astype(jnp.float32)
        for partner in range(subdomains):
            scaled = (values * weight_ref[partner, at][:, None, :]).astype(jnp.bfloat16)
            scaled_ref[tile % 2, :, partner * dof_count : (partner + 1) * dof_count] = scaled.reshape(
                tile_blocks * columns, dof_count
            )
        total = jnp.dot(scaled_ref[tile % 2], basis_ref[...], preferred_element_type=jnp.float32)
        result = jnp.dot(
            total.astype(jnp.bfloat16), projection_ref[...], preferred_element_type=jnp.float32
        )
        out_ref[at] = result.reshape(tile_blocks, columns, dof_count)
        copies.append(pltpu.make_async_copy(out_ref.at[at], result_ref.at[at], sems.at[tile]))
        copies[-1].start()
    for copy in copies:
        copy.wait()


def on_device(
    mortar_in, pump_rate, well_cell, face_owner, face_slot, face_scale, section, basis, projection
):
    blocks_dev, cols_dev, dof_count = mortar_in.shape
    faces_dev = face_slot.shape[0]
    subdomains, rights, halves = lax.axis_size("sub"), lax.axis_size("rhs"), lax.axis_size("face")
    blocks_own = blocks_dev // halves
    capacity = max(2, 2 * faces_dev // subdomains)
    pack_rows = -(-capacity // ROW_TILE) * ROW_TILE + ROW_TILE
    block_shape = (blocks_own, cols_dev, dof_count)

    def flat(sub, right, face):
        return (sub * rights + right) * halves + face

    partners = list(range(1, subdomains))
    groups = [partners[i : i + 3] for i in range(0, len(partners), 3)]
    groups = [(g[1], g[2], g[0]) if len(g) == 3 else (g[0], g[-1], g[0]) for g in groups]
    firsts = []
    for a, b, c in groups:
        pairs = [
            (flat(s, r, face), flat(s ^ (c if face else b if r % 2 else a), r, face))
            for s in range(subdomains)
            for r in range(rights)
            for face in range(halves)
        ]
        firsts.append(lax.ppermute(basis, ("sub", "rhs", "face"), pairs))

    packs = pl.pallas_call(
        pack_kernel,
        out_shape=[jax.ShapeDtypeStruct((pack_rows, dof_count), jnp.bfloat16)] * subdomains,
        in_specs=[VMEM, VMEM, VMEM, SMEM],
        out_specs=[VMEM] * subdomains,
        cost_estimate=pl.CostEstimate(flops=4_000_000_000, bytes_accessed=8 * MIB, transcendentals=0),
        name="pack_weights",
    )(face_owner.reshape(1, faces_dev), face_slot.reshape(1, faces_dev), face_scale, section)
    swap = [(i, i ^ 1) for i in range(halves)]
    weights = []
    for partner, pack in enumerate(packs):
        if partner:
            here = lax.ppermute(pack, "sub", [(i, i ^ partner) for i in range(subdomains)])
            weights += [here, lax.ppermute(here, "face", swap)]
        else:
            here = lax.ppermute(pack, "rhs", [(i, i ^ 1) for i in range(rights)])
            weights += [here, lax.ppermute(pack, "face", swap)]

    first_block = lax.axis_index("face") * blocks_own
    mine = lax.dynamic_slice_in_dim(mortar_in, first_block, blocks_own, 0)
    block_ids = lax.axis_index("sub") * blocks_dev + first_block + jnp.arange(blocks_own, dtype=jnp.int32)
    cell = block_ids[:, None, None] * dof_count + jnp.arange(dof_count, dtype=jnp.int32)[None, None, :]
    wells = jnp.where(cell == well_cell[None, :, None], pump_rate[None, :, None], 0.0)
    pumped = (mine.astype(jnp.float32) + wells).astype(jnp.bfloat16)

    pairs = [
        (r * halves + face, r * halves if face else (r ^ 1) * halves + 1)
        for r in range(rights)
        for face in range(halves)
    ]
    bases = []
    for first in firsts:
        second = lax.ppermute(first, ("rhs", "face"), pairs)
        bases += [first, lax.ppermute(first, "face", swap), second, lax.ppermute(second, "face", swap)]

    operands = [pumped, projection, basis, *bases, *weights]
    return pl.pallas_call(
        functools.partial(apply_kernel, groups),
        out_shape=jax.ShapeDtypeStruct(block_shape, jnp.float32),
        in_specs=[VMEM] * len(operands),
        out_specs=HBM,
        scratch_shapes=[
            pltpu.VMEM((subdomains, blocks_own, dof_count), jnp.float32),
            pltpu.VMEM((subdomains * dof_count, dof_count), jnp.bfloat16),
            pltpu.VMEM((2, blocks_own // TILES * cols_dev, subdomains * dof_count), jnp.bfloat16),
            pltpu.VMEM(block_shape, jnp.float32),
            pltpu.SemaphoreType.DMA((TILES,)),
        ],
        compiler_params=pltpu.CompilerParams(vmem_limit_bytes=48 * MIB),
        name="apply_blocks",
    )(*operands)


def solution(mesh):
    in_specs = (
        P(("groups", "sub"), "rhs", None),
        P(("groups", "rhs")),
        P(("groups", "rhs")),
        P(("groups", "sub", "face"), None),
        P(("groups", "sub", "face")),
        P(("groups", "sub", "face"), None),
        P(("groups", "sub")),
        P(("groups", "sub"), None, None),
        P(),
    )
    out_specs = P(("groups", "sub", "face"), "rhs", None)
    return jax.shard_map(
        on_device, mesh=mesh, in_specs=in_specs, out_specs=out_specs, check_vma=False
    )
```

```python
import functools

import jax
import jax.numpy as jnp
from jax import lax
from jax.experimental import pallas as pl
from jax.experimental.pallas import tpu as pltpu
from jax.sharding import PartitionSpec as P

ROW_TILE = 16
VMEM = pl.BlockSpec(memory_space=pltpu.VMEM)
HBM = pl.BlockSpec(memory_space=pltpu.HBM)
SMEM = pl.BlockSpec(memory_space=pltpu.SMEM)
MIB = 1024 * 1024
TILES = 4


def pack_kernel(owner_ref, slot_ref, scale_ref, section_ref, basis_ref, *packs):
    subdomains = len(packs)
    rows, dof_count = packs[0].shape
    rows -= ROW_TILE
    faces = owner_ref.shape[1]
    half_rows = dof_count // 2
    half = pl.multiple_of(lax.axis_index("face") * half_rows, half_rows)
    sign = (1 - 2 * section_ref[...].reshape(1, 1)).astype(jnp.float32)
    partners = lax.broadcasted_iota(jnp.int32, (subdomains, faces), 0)
    named = (lax.axis_index("sub") ^ partners) == owner_ref[...]
    earlier = lax.broadcasted_iota(jnp.int32, (faces, faces), 0) < lax.broadcasted_iota(
        jnp.int32, (faces, faces), 1
    )
    rank = jnp.dot(
        named.astype(jnp.bfloat16), earlier.astype(jnp.bfloat16), preferred_element_type=jnp.float32
    )
    place = jnp.where(named, rank.astype(jnp.int32), -1)
    slots = slot_ref[...].astype(jnp.bfloat16)
    for partner, pack_ref in enumerate(packs):
        hit = place[partner : partner + 1, :] == lax.broadcasted_iota(jnp.int32, (rows, faces), 0)
        hit = hit.astype(jnp.bfloat16)
        packed = jnp.dot(hit, scale_ref[...], preferred_element_type=jnp.float32) * sign
        listed = lax.dot_general(
            slots, hit, (((1,), (1,)), ((), ())), preferred_element_type=jnp.float32
        )
        meta = jnp.concatenate([listed, jnp.zeros((1, dof_count - rows), jnp.float32)], axis=1)
        meta = jnp.broadcast_to(meta, (ROW_TILE, dof_count))
        pack_ref[:rows, :] = packed.astype(jnp.bfloat16)
        pack_ref[rows : rows + ROW_TILE, :] = meta.astype(jnp.bfloat16)
        if partner:
            pack_ref[rows + ROW_TILE :, :] = basis_ref[0, pl.ds(half, half_rows), :]


def block_weights(packs, rows, blocks_own):
    first = lax.axis_index("face") * blocks_own
    block_ids = first + lax.broadcasted_iota(jnp.int32, (blocks_own, rows), 0)
    total = None
    for pack in packs:
        slots = pack[rows : rows + ROW_TILE, :].astype(jnp.int32)[:1, :rows]
        hit = (slots == block_ids).astype(jnp.bfloat16)
        part = jnp.dot(hit, pack[:rows, :], preferred_element_type=jnp.float32)
        total = part if total is None else total + part
    return total


def own_kernel(mortar_ref, rate_ref, cell_ref, basis_ref, pack_ref, swapped_ref, pumped_ref, sum_ref, weight_ref, sem):
    blocks_own, columns, dof_count = pumped_ref.shape
    first_block = lax.axis_index("face") * blocks_own
    fetch = pltpu.make_async_copy(mortar_ref.at[pl.ds(first_block, blocks_own)], pumped_ref, sem)
    fetch.start()
    weight_ref[...] = block_weights((pack_ref, swapped_ref), pack_ref.shape[0] - ROW_TILE, blocks_own)
    fetch.wait()

    base = lax.axis_index("sub") * mortar_ref.shape[0] + first_block
    for column in range(columns):
        block = lax.div(cell_ref[column], dof_count) - base
        dof = lax.rem(cell_ref[column], dof_count)

        @pl.when((block >= 0) & (block < blocks_own))
        def _():
            slab = slice(column // ROW_TILE * ROW_TILE, (column // ROW_TILE + 1) * ROW_TILE)
            shape = (ROW_TILE, dof_count)
            at_well = (lax.broadcasted_iota(jnp.int32, shape, 0) == column % ROW_TILE) & (
                lax.broadcasted_iota(jnp.int32, shape, 1) == dof
            )
            well = jnp.where(at_well, rate_ref[column], 0.0)
            pumped_ref[block, slab, :] = (pumped_ref[block, slab, :].astype(jnp.float32) + well).astype(
                jnp.bfloat16
            )

    tile_blocks = blocks_own // TILES
    for tile in range(TILES):
        at = slice(tile * tile_blocks, (tile + 1) * tile_blocks)
        scaled = (pumped_ref[at].astype(jnp.float32) * weight_ref[at][:, None, :]).astype(jnp.bfloat16)
        flux = jnp.dot(
            scaled.reshape(tile_blocks * columns, dof_count), basis_ref[0], preferred_element_type=jnp.float32
        )
        sum_ref[at] = flux.reshape(tile_blocks, columns, dof_count)


def stage_kernel(count, last, pumped_ref, sum_ref, *refs):
    packs, refs = refs[: 2 * count], refs[2 * count :]
    if last:
        projection_ref, result_ref, weight_ref, basis_ref, scaled_ref, out_ref, sems = refs
    else:
        out_ref, weight_ref, basis_ref, scaled_ref = refs
    blocks_own, columns, dof_count = pumped_ref.shape
    half_rows = dof_count // 2
    rows = packs[0].shape[0] - ROW_TILE - half_rows
    for at in range(count):
        pair = packs[2 * at : 2 * at + 2]
        weight_ref[at] = block_weights(pair, rows, blocks_own)
        for which, pack in enumerate(pair):
            half = lax.axis_index("face") ^ which
            start = pl.multiple_of(at * dof_count + half * half_rows, half_rows)
            basis_ref[pl.ds(start, half_rows), :] = pack[rows + ROW_TILE :, :]

    tile_blocks = blocks_own // TILES
    copies = []
    for tile in range(TILES):
        at = slice(tile * tile_blocks, (tile + 1) * tile_blocks)
        values = pumped_ref[at].astype(jnp.float32)
        for other in range(count):
            scaled = (values * weight_ref[other, at][:, None, :]).astype(jnp.bfloat16)
            scaled_ref[tile % 2, :, other * dof_count : (other + 1) * dof_count] = scaled.reshape(
                tile_blocks * columns, dof_count
            )
        total = jnp.dot(scaled_ref[tile % 2], basis_ref[...], preferred_element_type=jnp.float32)
        total = total + sum_ref[at].reshape(tile_blocks * columns, dof_count)
        if last:
            total = jnp.dot(
                total.astype(jnp.bfloat16), projection_ref[...], preferred_element_type=jnp.float32
            )
        out_ref[at] = total.reshape(tile_blocks, columns, dof_count)
        if last:
            copies.append(pltpu.make_async_copy(out_ref.at[at], result_ref.at[at], sems.at[tile]))
            copies[-1].start()
    for copy in copies:
        copy.wait()


def on_device(
    mortar_in, pump_rate, well_cell, face_owner, face_slot, face_scale, section, basis, projection
):
    blocks_dev, cols_dev, dof_count = mortar_in.shape
    faces_dev = face_slot.shape[0]
    subdomains, halves = lax.axis_size("sub"), lax.axis_size("face")
    blocks_own = blocks_dev // halves
    capacity = max(2, 2 * faces_dev // subdomains)
    pack_rows = -(-capacity // ROW_TILE) * ROW_TILE + ROW_TILE
    block_shape = (blocks_own, cols_dev, dof_count)
    pack_shapes = [(pack_rows, dof_count)] + [(pack_rows + dof_count // halves, dof_count)] * (subdomains - 1)

    packs = pl.pallas_call(
        pack_kernel,
        out_shape=[jax.ShapeDtypeStruct(shape, jnp.bfloat16) for shape in pack_shapes],
        in_specs=[VMEM] * 5,
        out_specs=[VMEM] * subdomains,
        name="pack_weights",
    )(face_owner.reshape(1, faces_dev), face_slot.reshape(1, faces_dev), face_scale, section, basis)

    swap = [(i, i ^ 1) for i in range(halves)]
    partners = sorted(range(1, subdomains), key=lambda p: (p < subdomains // 2, p))
    arrived = {p: lax.ppermute(packs[p], "sub", [(i, i ^ p) for i in range(subdomains)]) for p in partners}
    own_swapped = lax.ppermute(packs[0], "face", swap)

    pumped, total = pl.pallas_call(
        own_kernel,
        out_shape=[
            jax.ShapeDtypeStruct(block_shape, jnp.bfloat16),
            jax.ShapeDtypeStruct(block_shape, jnp.float32),
        ],
        in_specs=[HBM, SMEM, SMEM, VMEM, VMEM, VMEM],
        out_specs=[VMEM, VMEM],
        scratch_shapes=[pltpu.VMEM((blocks_own, dof_count), jnp.float32), pltpu.SemaphoreType.DMA(())],
        compiler_params=pltpu.CompilerParams(vmem_limit_bytes=32 * MIB),
        cost_estimate=pl.CostEstimate(flops=2_000_000_000, bytes_accessed=8 * MIB, transcendentals=0),
        name="own_blocks",
    )(mortar_in, pump_rate, well_cell, basis, packs[0], own_swapped)

    for stage in (partners,):
        arrays, total = lax.optimization_barrier(([arrived[p] for p in stage], total))
        pairs = []
        for array in arrays:
            pairs += [array, lax.ppermute(array, "face", swap)]
        last = stage[-1] == partners[-1]
        count = len(stage)
        scratch = [
            pltpu.VMEM((count, blocks_own, dof_count), jnp.float32),
            pltpu.VMEM((count * dof_count, dof_count), jnp.bfloat16),
            pltpu.VMEM((2, blocks_own // TILES * cols_dev, count * dof_count), jnp.bfloat16),
        ]
        if last:
            scratch += [pltpu.VMEM(block_shape, jnp.float32), pltpu.SemaphoreType.DMA((TILES,))]
        operands = [pumped, total, *pairs] + ([projection] if last else [])
        total = pl.pallas_call(
            functools.partial(stage_kernel, count, last),
            out_shape=jax.ShapeDtypeStruct(block_shape, jnp.float32),
            in_specs=[VMEM] * len(operands),
            out_specs=HBM if last else VMEM,
            scratch_shapes=scratch,
            input_output_aliases={} if last else {1: 0},
            compiler_params=pltpu.CompilerParams(vmem_limit_bytes=40 * MIB),
            cost_estimate=pl.CostEstimate(flops=2_000_000_000, bytes_accessed=8 * MIB, transcendentals=0),
            name="last_stage" if last else "stage",
        )(*operands)
    return total


def solution(mesh):
    in_specs = (
        P(("groups", "sub"), "rhs", None),
        P(("groups", "rhs")),
        P(("groups", "rhs")),
        P(("groups", "sub", "face"), None),
        P(("groups", "sub", "face")),
        P(("groups", "sub", "face"), None),
        P(("groups", "sub")),
        P(("groups", "sub"), None, None),
        P(),
    )
    out_specs = P(("groups", "sub", "face"), "rhs", None)
    return jax.shard_map(
        on_device, mesh=mesh, in_specs=in_specs, out_specs=out_specs, check_vma=False
    )
```

```python
import functools

import jax
import jax.numpy as jnp
from jax import lax
from jax.experimental import pallas as pl
from jax.experimental.pallas import tpu as pltpu
from jax.sharding import PartitionSpec as P

ROW_TILE = 16
VMEM = pl.BlockSpec(memory_space=pltpu.VMEM)
HBM = pl.BlockSpec(memory_space=pltpu.HBM)
SMEM = pl.BlockSpec(memory_space=pltpu.SMEM)
MIB = 1024 * 1024
TILES = 4
WORK = pl.CostEstimate(flops=4_000_000_000, bytes_accessed=8 * MIB, transcendentals=0)


def pack_kernel(owner_ref, slot_ref, scale_ref, section_ref, *packs):
    subdomains = len(packs)
    rows, dof_count = packs[0].shape
    rows -= ROW_TILE
    faces = owner_ref.shape[1]
    sign = (1 - 2 * section_ref[0]).astype(jnp.float32)
    partners = lax.broadcasted_iota(jnp.int32, (subdomains, faces), 0)
    named = (lax.axis_index("sub") ^ partners) == owner_ref[...]
    earlier = lax.broadcasted_iota(jnp.int32, (faces, faces), 0) < lax.broadcasted_iota(
        jnp.int32, (faces, faces), 1
    )
    rank = jnp.dot(
        named.astype(jnp.bfloat16), earlier.astype(jnp.bfloat16), preferred_element_type=jnp.float32
    )
    place = jnp.where(named, rank, -1.0)
    at = lax.broadcasted_iota(jnp.int32, (rows, faces), 0).astype(jnp.float32)
    hit = jnp.concatenate([place[p : p + 1, :] == at for p in range(subdomains)], axis=0)
    hit = hit.astype(jnp.bfloat16)
    packed = jnp.dot(hit, scale_ref[...], preferred_element_type=jnp.float32) * sign
    listed = lax.dot_general(
        slot_ref[...].astype(jnp.bfloat16), hit, (((1,), (1,)), ((), ())), preferred_element_type=jnp.float32
    )
    packed = packed.astype(jnp.bfloat16)
    for p, pack_ref in enumerate(packs):
        pack_ref[:rows, :] = packed[p * rows : (p + 1) * rows, :]
        meta = jnp.concatenate(
            [listed[:, p * rows : (p + 1) * rows], jnp.zeros((1, dof_count - rows), jnp.float32)], axis=1
        )
        pack_ref[rows:, :] = jnp.broadcast_to(meta, (ROW_TILE, dof_count)).astype(jnp.bfloat16)


def block_weights(packs, rows, blocks_own):
    first = lax.axis_index("face") * blocks_own
    block_ids = first + lax.broadcasted_iota(jnp.int32, (blocks_own, rows), 0)
    total = None
    for pack in packs:
        slots = pack[rows : rows + ROW_TILE, :].astype(jnp.int32)[:1, :rows]
        hit = (slots == block_ids).astype(jnp.bfloat16)
        part = jnp.dot(hit, pack[:rows, :], preferred_element_type=jnp.float32)
        total = part if total is None else total + part
    return total


def pump_kernel(mortar_ref, rate_ref, cell_ref, pumped_ref, sem):
    blocks_own, columns, dof_count = pumped_ref.shape
    first_block = lax.axis_index("face") * blocks_own
    fetch = pltpu.make_async_copy(mortar_ref.at[pl.ds(first_block, blocks_own)], pumped_ref, sem)
    fetch.start()
    fetch.wait()
    base = lax.axis_index("sub") * mortar_ref.shape[0] + first_block
    for column in range(columns):
        block = lax.div(cell_ref[column], dof_count) - base
        dof = lax.rem(cell_ref[column], dof_count)

        @pl.when((block >= 0) & (block < blocks_own))
        def _():
            slab = slice(column // ROW_TILE * ROW_TILE, (column // ROW_TILE + 1) * ROW_TILE)
            shape = (ROW_TILE, dof_count)
            at_well = (lax.broadcasted_iota(jnp.int32, shape, 0) == column % ROW_TILE) & (
                lax.broadcasted_iota(jnp.int32, shape, 1) == dof
            )
            well = jnp.where(at_well, rate_ref[column], 0.0)
            pumped_ref[block, slab, :] = (pumped_ref[block, slab, :].astype(jnp.float32) + well).astype(
                jnp.bfloat16
            )


def own_kernel(pumped_ref, basis_ref, pack_ref, swapped_ref, sum_ref, weight_ref):
    blocks_own, columns, dof_count = pumped_ref.shape
    weight_ref[...] = block_weights((pack_ref, swapped_ref), pack_ref.shape[0] - ROW_TILE, blocks_own)
    tile_blocks = blocks_own // TILES
    for tile in range(TILES):
        at = slice(tile * tile_blocks, (tile + 1) * tile_blocks)
        scaled = (pumped_ref[at].astype(jnp.float32) * weight_ref[at][:, None, :]).astype(jnp.bfloat16)
        flux = jnp.dot(
            scaled.reshape(tile_blocks * columns, dof_count), basis_ref[0], preferred_element_type=jnp.float32
        )
        sum_ref[at] = flux.reshape(tile_blocks, columns, dof_count)


def last_kernel(groups, order, pumped_ref, sum_ref, projection_ref, *refs):
    bases, refs = refs[: 4 * len(groups)], refs[4 * len(groups) :]
    packs, (result_ref, weight_ref, basis_ref, scaled_ref, out_ref, sems) = refs[:-6], refs[-6:]
    blocks_own, columns, dof_count = pumped_ref.shape
    others = len(order)
    lane = 2 * lax.rem(lax.axis_index("rhs"), 2) + lax.axis_index("face")

    def put(array, *by_lane):
        partner = jnp.int32(by_lane[3])
        for which in range(3):
            partner = jnp.where(lane == which, by_lane[which], partner)
        start = pl.multiple_of((partner - 1) * dof_count, dof_count)
        basis_ref[pl.ds(start, dof_count), :] = array[0]

    for at, (a, b, c) in enumerate(groups):
        first, first_swapped, second, second_swapped = bases[4 * at : 4 * at + 4]
        put(first, a, c, b, c)
        put(second, c, b, c, a)
        put(first_swapped, c, a, c, b)
        put(second_swapped, b, c, a, c)
    for at, partner in enumerate(order):
        pair = packs[2 * at : 2 * at + 2]
        weight_ref[partner - 1] = block_weights(pair, pair[0].shape[0] - ROW_TILE, blocks_own)

    tile_blocks = blocks_own // TILES
    copies = []
    for tile in range(TILES):
        at = slice(tile * tile_blocks, (tile + 1) * tile_blocks)
        values = pumped_ref[at].astype(jnp.float32)
        for other in range(others):
            scaled = (values * weight_ref[other, at][:, None, :]).astype(jnp.bfloat16)
            scaled_ref[tile % 2, :, other * dof_count : (other + 1) * dof_count] = scaled.reshape(
                tile_blocks * columns, dof_count
            )
        total = jnp.dot(scaled_ref[tile % 2], basis_ref[...], preferred_element_type=jnp.float32)
        total = total + sum_ref[at].reshape(tile_blocks * columns, dof_count)
        result = jnp.dot(
            total.astype(jnp.bfloat16), projection_ref[...], preferred_element_type=jnp.float32
        )
        out_ref[at] = result.reshape(tile_blocks, columns, dof_count)
        copies.append(pltpu.make_async_copy(out_ref.at[at], result_ref.at[at], sems.at[tile]))
        copies[-1].start()
    for copy in copies:
        copy.wait()


def on_device(
    mortar_in, pump_rate, well_cell, face_owner, face_slot, face_scale, section, basis, projection
):
    blocks_dev, cols_dev, dof_count = mortar_in.shape
    faces_dev = face_slot.shape[0]
    subdomains, rights, halves = lax.axis_size("sub"), lax.axis_size("rhs"), lax.axis_size("face")
    others = subdomains - 1
    blocks_own = blocks_dev // halves
    capacity = max(2, 2 * faces_dev // subdomains)
    pack_rows = -(-capacity // ROW_TILE) * ROW_TILE + ROW_TILE
    block_shape = (blocks_own, cols_dev, dof_count)
    swap = [(i, i ^ 1) for i in range(halves)]

    def flat(sub, right, face):
        return (sub * rights + right) * halves + face

    partners = sorted(range(1, subdomains), key=lambda p: (p < subdomains // 2, p))
    groups = [partners[i : i + 3] for i in range(0, others, 3)]
    groups = [tuple(g) if len(g) == 3 else (g[0], g[-1], g[0]) for g in groups]
    firsts = []
    for a, b, c in groups:
        pairs = [
            (flat(s, r, face), flat(s ^ (c if face else b if r % 2 else a), r, face))
            for s in range(subdomains)
            for r in range(rights)
            for face in range(halves)
        ]
        firsts.append(lax.ppermute(basis, ("sub", "rhs", "face"), pairs))

    packs = pl.pallas_call(
        pack_kernel,
        out_shape=[jax.ShapeDtypeStruct((pack_rows, dof_count), jnp.bfloat16)] * subdomains,
        in_specs=[VMEM, VMEM, VMEM, SMEM],
        out_specs=[VMEM] * subdomains,
        cost_estimate=WORK,
        name="pack_weights",
    )(face_owner.reshape(1, faces_dev), face_slot.reshape(1, faces_dev), face_scale, section)
    arrived = [lax.ppermute(packs[p], "sub", [(i, i ^ p) for i in range(subdomains)]) for p in partners]
    own_swapped = lax.ppermute(packs[0], "face", swap)

    pairs = [
        (r * halves + face, r * halves if face else (r ^ 1) * halves + 1)
        for r in range(rights)
        for face in range(halves)
    ]
    bases = []
    for first in firsts:
        second = lax.ppermute(first, ("rhs", "face"), pairs)
        bases += [first, lax.ppermute(first, "face", swap), second, lax.ppermute(second, "face", swap)]

    pumped = pl.pallas_call(
        pump_kernel,
        out_shape=jax.ShapeDtypeStruct(block_shape, jnp.bfloat16),
        in_specs=[HBM, SMEM, SMEM],
        out_specs=VMEM,
        scratch_shapes=[pltpu.SemaphoreType.DMA(())],
        compiler_params=pltpu.CompilerParams(vmem_limit_bytes=32 * MIB),
        cost_estimate=WORK,
        name="pump",
    )(mortar_in, pump_rate, well_cell)
    own_sum = pl.pallas_call(
        own_kernel,
        out_shape=jax.ShapeDtypeStruct(block_shape, jnp.float32),
        in_specs=[VMEM] * 4,
        out_specs=VMEM,
        scratch_shapes=[pltpu.VMEM((blocks_own, dof_count), jnp.float32)],
        compiler_params=pltpu.CompilerParams(vmem_limit_bytes=32 * MIB),
        cost_estimate=WORK,
        name="own_blocks",
    )(pumped, basis, packs[0], own_swapped)

    arrived, own_sum = lax.optimization_barrier((arrived, own_sum))
    weights = []
    for array in arrived:
        weights += [array, lax.ppermute(array, "face", swap)]

    operands = [pumped, own_sum, projection, *bases, *weights]
    return pl.pallas_call(
        functools.partial(last_kernel, groups, partners),
        out_shape=jax.ShapeDtypeStruct(block_shape, jnp.float32),
        in_specs=[VMEM] * len(operands),
        out_specs=HBM,
        scratch_shapes=[
            pltpu.VMEM((others, blocks_own, dof_count), jnp.float32),
            pltpu.VMEM((others * dof_count, dof_count), jnp.bfloat16),
            pltpu.VMEM((2, blocks_own // TILES * cols_dev, others * dof_count), jnp.bfloat16),
            pltpu.VMEM(block_shape, jnp.float32),
            pltpu.SemaphoreType.DMA((TILES,)),
        ],
        compiler_params=pltpu.CompilerParams(vmem_limit_bytes=40 * MIB),
        name="last_stage",
    )(*operands)


def solution(mesh):
    in_specs = (
        P(("groups", "sub"), "rhs", None),
        P(("groups", "rhs")),
        P(("groups", "rhs")),
        P(("groups", "sub", "face"), None),
        P(("groups", "sub", "face")),
        P(("groups", "sub", "face"), None),
        P(("groups", "sub")),
        P(("groups", "sub"), None, None),
        P(),
    )
    out_specs = P(("groups", "sub", "face"), "rhs", None)
    return jax.shard_map(
        on_device, mesh=mesh, in_specs=in_specs, out_specs=out_specs, check_vma=False
    )
```

```python
import functools

import jax
import jax.numpy as jnp
from jax import lax
from jax.experimental import pallas as pl
from jax.experimental.pallas import tpu as pltpu
from jax.sharding import PartitionSpec as P

ROW_TILE = 16
VMEM = pl.BlockSpec(memory_space=pltpu.VMEM)
HBM = pl.BlockSpec(memory_space=pltpu.HBM)
SMEM = pl.BlockSpec(memory_space=pltpu.SMEM)
MIB = 1024 * 1024
TILES = 4
LAST_TILES = 8
LIGHT = pl.CostEstimate(flops=1_000_000, bytes_accessed=1024, transcendentals=0)
WORK = pl.CostEstimate(flops=4_000_000_000, bytes_accessed=8 * MIB, transcendentals=0)


def pack_kernel(owner_ref, slot_ref, scale_ref, section_ref, *packs):
    subdomains = len(packs)
    rows, dof_count = packs[0].shape
    rows -= ROW_TILE
    faces = owner_ref.shape[1]
    sign = (1 - 2 * section_ref[0]).astype(jnp.float32)
    partners = lax.broadcasted_iota(jnp.int32, (subdomains, faces), 0)
    named = (lax.axis_index("sub") ^ partners) == owner_ref[...]
    earlier = lax.broadcasted_iota(jnp.int32, (faces, faces), 0) < lax.broadcasted_iota(
        jnp.int32, (faces, faces), 1
    )
    rank = jnp.dot(
        named.astype(jnp.bfloat16), earlier.astype(jnp.bfloat16), preferred_element_type=jnp.float32
    )
    place = jnp.where(named, rank, -1.0)
    at = lax.broadcasted_iota(jnp.int32, (rows, faces), 0).astype(jnp.float32)
    hit = jnp.concatenate([place[p : p + 1, :] == at for p in range(subdomains)], axis=0)
    hit = hit.astype(jnp.bfloat16)
    packed = jnp.dot(hit, scale_ref[...], preferred_element_type=jnp.float32) * sign
    listed = lax.dot_general(
        slot_ref[...].astype(jnp.bfloat16), hit, (((1,), (1,)), ((), ())), preferred_element_type=jnp.float32
    )
    packed = packed.astype(jnp.bfloat16)
    for p, pack_ref in enumerate(packs):
        pack_ref[:rows, :] = packed[p * rows : (p + 1) * rows, :]
        meta = jnp.concatenate(
            [listed[:, p * rows : (p + 1) * rows], jnp.zeros((1, dof_count - rows), jnp.float32)], axis=1
        )
        pack_ref[rows:, :] = jnp.broadcast_to(meta, (ROW_TILE, dof_count)).astype(jnp.bfloat16)


def block_weights(packs, rows, blocks_own):
    first = lax.axis_index("face") * blocks_own
    block_ids = first + lax.broadcasted_iota(jnp.int32, (blocks_own, rows), 0)
    total = None
    for pack in packs:
        slots = pack[rows : rows + ROW_TILE, :].astype(jnp.int32)[:1, :rows]
        hit = (slots == block_ids).astype(jnp.bfloat16)
        part = jnp.dot(hit, pack[:rows, :], preferred_element_type=jnp.float32)
        total = part if total is None else total + part
    return total


def pump_kernel(mortar_ref, rate_ref, cell_ref, pumped_ref, sem):
    blocks_own, columns, dof_count = pumped_ref.shape
    first_block = lax.axis_index("face") * blocks_own
    fetch = pltpu.make_async_copy(mortar_ref.at[pl.ds(first_block, blocks_own)], pumped_ref, sem)
    fetch.start()
    fetch.wait()
    base = lax.axis_index("sub") * mortar_ref.shape[0] + first_block
    for column in range(columns):
        block = lax.div(cell_ref[column], dof_count) - base
        dof = lax.rem(cell_ref[column], dof_count)

        @pl.when((block >= 0) & (block < blocks_own))
        def _():
            slab = slice(column // ROW_TILE * ROW_TILE, (column // ROW_TILE + 1) * ROW_TILE)
            shape = (ROW_TILE, dof_count)
            at_well = (lax.broadcasted_iota(jnp.int32, shape, 0) == column % ROW_TILE) & (
                lax.broadcasted_iota(jnp.int32, shape, 1) == dof
            )
            well = jnp.where(at_well, rate_ref[column], 0.0)
            pumped_ref[block, slab, :] = (pumped_ref[block, slab, :].astype(jnp.float32) + well).astype(
                jnp.bfloat16
            )


def own_kernel(pumped_ref, basis_ref, pack_ref, swapped_ref, sum_ref, weight_ref):
    blocks_own, columns, dof_count = pumped_ref.shape
    weight_ref[...] = block_weights((pack_ref, swapped_ref), pack_ref.shape[0] - ROW_TILE, blocks_own)
    tile_blocks = blocks_own // TILES
    for tile in range(TILES):
        at = slice(tile * tile_blocks, (tile + 1) * tile_blocks)
        scaled = (pumped_ref[at].astype(jnp.float32) * weight_ref[at][:, None, :]).astype(jnp.bfloat16)
        flux = jnp.dot(
            scaled.reshape(tile_blocks * columns, dof_count), basis_ref[0], preferred_element_type=jnp.float32
        )
        sum_ref[at] = flux.reshape(tile_blocks, columns, dof_count)


def on_even(even, odd):
    return jnp.where(lax.rem(lax.axis_index("rhs"), 2) == 0, even, odd)


def stage_kernel(groups, pumped_ref, sum_ref, *refs):
    bases, refs = refs[: 2 * len(groups)], refs[2 * len(groups) :]
    packs, (out_ref, late_ref, weight_ref, basis_ref, scaled_ref) = refs[:-5], refs[-5:]
    blocks_own, columns, dof_count = pumped_ref.shape
    face_id = lax.axis_index("face")
    rows = packs[0].shape[0] - ROW_TILE
    weights = {}

    def weight(partner):
        if partner not in weights:
            weights[partner] = block_weights(packs[2 * partner - 2 : 2 * partner], rows, blocks_own)
        return weights[partner]

    count = late = 0
    for at, (a, b, c) in enumerate(groups):
        first, first_swapped = bases[2 * at : 2 * at + 2]
        spots = [None, None]
        if a != b:
            spots[0] = count
            weight_ref[count] = on_even(weight(a), weight(b))
            late_ref[late] = on_even(weight(b), weight(a))
            count, late = count + 1, late + 1
        if c != a:
            spots[1] = count
            weight_ref[count] = weight(c)
            count += 1
        elif a == b:
            spots = [count, count]
            weight_ref[count] = weight(c)
            count += 1
        spare = weight_ref.shape[0]
        spots = [spare if spot is None else spot for spot in spots]
        for array, core_0, core_1 in ((first, *spots), (first_swapped, *spots[::-1])):
            start = pl.multiple_of(jnp.where(face_id == 0, core_0, core_1) * dof_count, dof_count)
            basis_ref[pl.ds(start, dof_count), :] = array[0]

    tile_blocks = blocks_own // TILES
    for tile in range(TILES):
        at = slice(tile * tile_blocks, (tile + 1) * tile_blocks)
        values = pumped_ref[at].astype(jnp.float32)
        for spot in range(count):
            scaled = (values * weight_ref[spot, at][:, None, :]).astype(jnp.bfloat16)
            scaled_ref[tile % 2, :, spot * dof_count : (spot + 1) * dof_count] = scaled.reshape(
                tile_blocks * columns, dof_count
            )
        total = jnp.dot(
            scaled_ref[tile % 2], basis_ref[: count * dof_count, :], preferred_element_type=jnp.float32
        )
        out_ref[at] = total.reshape(tile_blocks, columns, dof_count) + sum_ref[at]


def last_kernel(pumped_ref, sum_ref, weight_ref, projection_ref, *refs):
    bases, (result_ref, basis_ref, scaled_ref, out_ref, sems) = refs[:-5], refs[-5:]
    blocks_own, columns, dof_count = pumped_ref.shape
    count = weight_ref.shape[0]
    for at in range(count):
        for core, array in ((1, bases[2 * at]), (0, bases[2 * at + 1])):

            @pl.when(lax.axis_index("face") == core)
            def _():
                basis_ref[at * dof_count : (at + 1) * dof_count, :] = array[0]

    tiles = sems.shape[0]
    tile_blocks = blocks_own // tiles
    copies = []
    for tile in range(tiles):
        at = slice(tile * tile_blocks, (tile + 1) * tile_blocks)
        values = pumped_ref[at].astype(jnp.float32)
        for spot in range(count):
            scaled = (values * weight_ref[spot, at][:, None, :]).astype(jnp.bfloat16)
            scaled_ref[tile % 2, :, spot * dof_count : (spot + 1) * dof_count] = scaled.reshape(
                tile_blocks * columns, dof_count
            )
        total = jnp.dot(scaled_ref[tile % 2], basis_ref[...], preferred_element_type=jnp.float32)
        total = total + sum_ref[at].reshape(tile_blocks * columns, dof_count)
        result = jnp.dot(
            total.astype(jnp.bfloat16), projection_ref[...], preferred_element_type=jnp.float32
        )
        out_ref[at] = result.reshape(tile_blocks, columns, dof_count)
        copies.append(pltpu.make_async_copy(out_ref.at[at], result_ref.at[at], sems.at[tile]))
        copies[-1].start()
    for copy in copies:
        copy.wait()


def on_device(
    mortar_in, pump_rate, well_cell, face_owner, face_slot, face_scale, section, basis, projection
):
    blocks_dev, cols_dev, dof_count = mortar_in.shape
    faces_dev = face_slot.shape[0]
    subdomains, rights, halves = lax.axis_size("sub"), lax.axis_size("rhs"), lax.axis_size("face")
    others = subdomains - 1
    blocks_own = blocks_dev // halves
    capacity = max(2, 2 * faces_dev // subdomains)
    pack_rows = -(-capacity // ROW_TILE) * ROW_TILE + ROW_TILE
    block_shape = (blocks_own, cols_dev, dof_count)
    swap = [(i, i ^ 1) for i in range(halves)]

    def flat(sub, right, face):
        return (sub * rights + right) * halves + face

    partners = sorted(range(1, subdomains), key=lambda p: (p < subdomains // 2, p))
    groups = [partners[i : i + 3] for i in range(0, others, 3)]
    groups = [tuple(g) if len(g) == 3 else (g[0], g[-1], g[0]) for g in groups]
    firsts = []
    for a, b, c in groups:
        pairs = [
            (flat(s, r, face), flat(s ^ (c if face else b if r % 2 else a), r, face))
            for s in range(subdomains)
            for r in range(rights)
            for face in range(halves)
        ]
        firsts.append(lax.ppermute(basis, ("sub", "rhs", "face"), pairs))

    packs = pl.pallas_call(
        pack_kernel,
        out_shape=[jax.ShapeDtypeStruct((pack_rows, dof_count), jnp.bfloat16)] * subdomains,
        in_specs=[VMEM, VMEM, VMEM, SMEM],
        out_specs=[VMEM] * subdomains,
        cost_estimate=WORK,
        name="pack_weights",
    )(face_owner.reshape(1, faces_dev), face_slot.reshape(1, faces_dev), face_scale, section)
    arrived = [lax.ppermute(packs[p], "sub", [(i, i ^ p) for i in range(subdomains)]) for p in partners]
    own_swapped = lax.ppermute(packs[0], "face", swap)

    pumped = pl.pallas_call(
        pump_kernel,
        out_shape=jax.ShapeDtypeStruct(block_shape, jnp.bfloat16),
        in_specs=[HBM, SMEM, SMEM],
        out_specs=VMEM,
        scratch_shapes=[pltpu.SemaphoreType.DMA(())],
        compiler_params=pltpu.CompilerParams(vmem_limit_bytes=32 * MIB),
        cost_estimate=LIGHT,
        name="pump",
    )(mortar_in, pump_rate, well_cell)
    own_sum = pl.pallas_call(
        own_kernel,
        out_shape=jax.ShapeDtypeStruct(block_shape, jnp.float32),
        in_specs=[VMEM] * 4,
        out_specs=VMEM,
        scratch_shapes=[pltpu.VMEM((blocks_own, dof_count), jnp.float32)],
        compiler_params=pltpu.CompilerParams(vmem_limit_bytes=32 * MIB),
        cost_estimate=LIGHT,
        name="own_blocks",
    )(pumped, basis, packs[0], own_swapped)

    firsts, arrived, own_sum = lax.optimization_barrier((firsts, arrived, own_sum))
    pairs = [
        (r * halves + face, r * halves if face else (r ^ 1) * halves + 1)
        for r in range(rights)
        for face in range(halves)
    ]
    early, late = [], []
    for (a, b, _), first in zip(groups, firsts):
        early += [first, lax.ppermute(first, "face", swap)]
        if a != b:
            second = lax.ppermute(first, ("rhs", "face"), pairs)
            late += [second, lax.ppermute(second, "face", swap)]
    weights = []
    for partner in range(1, subdomains):
        array = arrived[partners.index(partner)]
        weights += [array, lax.ppermute(array, "face", swap)]

    late_count = len(late) // 2
    count = others - late_count
    operands = [pumped, own_sum, *early, *weights]
    total, late_weight = pl.pallas_call(
        functools.partial(stage_kernel, groups),
        out_shape=[
            jax.ShapeDtypeStruct(block_shape, jnp.float32),
            jax.ShapeDtypeStruct((late_count, blocks_own, dof_count), jnp.float32),
        ],
        in_specs=[VMEM] * len(operands),
        out_specs=[VMEM, VMEM],
        scratch_shapes=[
            pltpu.VMEM((count, blocks_own, dof_count), jnp.float32),
            pltpu.VMEM(((count + 1) * dof_count, dof_count), jnp.bfloat16),
            pltpu.VMEM((2, blocks_own // TILES * cols_dev, count * dof_count), jnp.bfloat16),
        ],
        input_output_aliases={1: 0},
        compiler_params=pltpu.CompilerParams(vmem_limit_bytes=40 * MIB),
        cost_estimate=WORK,
        name="stage",
    )(*operands)

    operands = [pumped, total, late_weight, projection, *late]
    return pl.pallas_call(
        last_kernel,
        out_shape=jax.ShapeDtypeStruct(block_shape, jnp.float32),
        in_specs=[VMEM] * len(operands),
        out_specs=HBM,
        scratch_shapes=[
            pltpu.VMEM((late_count * dof_count, dof_count), jnp.bfloat16),
            pltpu.VMEM((2, blocks_own // LAST_TILES * cols_dev, late_count * dof_count), jnp.bfloat16),
            pltpu.VMEM(block_shape, jnp.float32),
            pltpu.SemaphoreType.DMA((LAST_TILES,)),
        ],
        compiler_params=pltpu.CompilerParams(vmem_limit_bytes=40 * MIB),
        name="last_stage",
    )(*operands)


def solution(mesh):
    in_specs = (
        P(("groups", "sub"), "rhs", None),
        P(("groups", "rhs")),
        P(("groups", "rhs")),
        P(("groups", "sub", "face"), None),
        P(("groups", "sub", "face")),
        P(("groups", "sub", "face"), None),
        P(("groups", "sub")),
        P(("groups", "sub"), None, None),
        P(),
    )
    out_specs = P(("groups", "sub", "face"), "rhs", None)
    return jax.shard_map(
        on_device, mesh=mesh, in_specs=in_specs, out_specs=out_specs, check_vma=False
    )
```

```python
import functools

import jax
import jax.numpy as jnp
from jax import lax
from jax.experimental import pallas as pl
from jax.experimental.pallas import tpu as pltpu
from jax.sharding import PartitionSpec as P

ROW_TILE = 16
VMEM = pl.BlockSpec(memory_space=pltpu.VMEM)
HBM = pl.BlockSpec(memory_space=pltpu.HBM)
SMEM = pl.BlockSpec(memory_space=pltpu.SMEM)
MIB = 1024 * 1024
TILES = 4
LAST_TILES = 8
LIGHT = pl.CostEstimate(flops=1_000_000, bytes_accessed=1024, transcendentals=0)
WORK = pl.CostEstimate(flops=4_000_000_000, bytes_accessed=8 * MIB, transcendentals=0)


def on_even(even, odd):
    return jnp.where(lax.rem(lax.axis_index("rhs"), 2) == 0, even, odd)


def pack_kernel(partners, owner_ref, slot_ref, scale_ref, section_ref, *packs):
    rows, dof_count = packs[0].shape
    rows -= ROW_TILE
    faces = owner_ref.shape[1]
    sign = (1 - 2 * section_ref[0]).astype(jnp.float32)
    here = lax.axis_index("sub")
    owners = jnp.concatenate(
        [jnp.full((1, faces), here ^ on_even(even, odd), jnp.int32) for even, odd in partners], axis=0
    )
    named = owners == owner_ref[...]
    earlier = lax.broadcasted_iota(jnp.int32, (faces, faces), 0) < lax.broadcasted_iota(
        jnp.int32, (faces, faces), 1
    )
    rank = jnp.dot(
        named.astype(jnp.bfloat16), earlier.astype(jnp.bfloat16), preferred_element_type=jnp.float32
    )
    place = jnp.where(named, rank, -1.0)
    at = lax.broadcasted_iota(jnp.int32, (rows, faces), 0).astype(jnp.float32)
    hit = jnp.concatenate([place[p : p + 1, :] == at for p in range(len(packs))], axis=0)
    hit = hit.astype(jnp.bfloat16)
    packed = jnp.dot(hit, scale_ref[...], preferred_element_type=jnp.float32) * sign
    listed = lax.dot_general(
        slot_ref[...].astype(jnp.bfloat16), hit, (((1,), (1,)), ((), ())), preferred_element_type=jnp.float32
    )
    packed = packed.astype(jnp.bfloat16)
    for p, pack_ref in enumerate(packs):
        pack_ref[:rows, :] = packed[p * rows : (p + 1) * rows, :]
        meta = jnp.concatenate(
            [listed[:, p * rows : (p + 1) * rows], jnp.zeros((1, dof_count - rows), jnp.float32)], axis=1
        )
        pack_ref[rows:, :] = jnp.broadcast_to(meta, (ROW_TILE, dof_count)).astype(jnp.bfloat16)


def block_weights(packs, rows, blocks_own):
    first = lax.axis_index("face") * blocks_own
    block_ids = first + lax.broadcasted_iota(jnp.int32, (blocks_own, rows), 0)
    total = None
    for pack in packs:
        slots = pack[rows : rows + ROW_TILE, :].astype(jnp.int32)[:1, :rows]
        hit = (slots == block_ids).astype(jnp.bfloat16)
        part = jnp.dot(hit, pack[:rows, :], preferred_element_type=jnp.float32)
        total = part if total is None else total + part
    return total


def pump_kernel(mortar_ref, rate_ref, cell_ref, pumped_ref, sem):
    blocks_own, columns, dof_count = pumped_ref.shape
    first_block = lax.axis_index("face") * blocks_own
    fetch = pltpu.make_async_copy(mortar_ref.at[pl.ds(first_block, blocks_own)], pumped_ref, sem)
    fetch.start()
    fetch.wait()
    base = lax.axis_index("sub") * mortar_ref.shape[0] + first_block
    for column in range(columns):
        block = lax.div(cell_ref[column], dof_count) - base
        dof = lax.rem(cell_ref[column], dof_count)

        @pl.when((block >= 0) & (block < blocks_own))
        def _():
            slab = slice(column // ROW_TILE * ROW_TILE, (column // ROW_TILE + 1) * ROW_TILE)
            shape = (ROW_TILE, dof_count)
            at_well = (lax.broadcasted_iota(jnp.int32, shape, 0) == column % ROW_TILE) & (
                lax.broadcasted_iota(jnp.int32, shape, 1) == dof
            )
            well = jnp.where(at_well, rate_ref[column], 0.0)
            pumped_ref[block, slab, :] = (pumped_ref[block, slab, :].astype(jnp.float32) + well).astype(
                jnp.bfloat16
            )


def own_kernel(pumped_ref, basis_ref, pack_ref, swapped_ref, sum_ref, weight_ref):
    blocks_own, columns, dof_count = pumped_ref.shape
    weight_ref[...] = block_weights((pack_ref, swapped_ref), pack_ref.shape[0] - ROW_TILE, blocks_own)
    tile_blocks = blocks_own // TILES
    for tile in range(TILES):
        at = slice(tile * tile_blocks, (tile + 1) * tile_blocks)
        scaled = (pumped_ref[at].astype(jnp.float32) * weight_ref[at][:, None, :]).astype(jnp.bfloat16)
        flux = jnp.dot(
            scaled.reshape(tile_blocks * columns, dof_count), basis_ref[0], preferred_element_type=jnp.float32
        )
        sum_ref[at] = flux.reshape(tile_blocks, columns, dof_count)


def stage_kernel(kinds, pumped_ref, sum_ref, *refs):
    bases, refs = refs[: 2 * len(kinds)], refs[2 * len(kinds) :]
    packs, (out_ref, weight_ref, basis_ref, scaled_ref) = refs[:-4], refs[-4:]
    blocks_own, columns, dof_count = pumped_ref.shape
    face_id = lax.axis_index("face")
    rows = packs[0].shape[0] - ROW_TILE
    count = weight_ref.shape[0]
    for spot in range(count):
        weight_ref[spot] = block_weights(packs[2 * spot : 2 * spot + 2], rows, blocks_own)
    spot = 0
    for at, (far, near) in enumerate(kinds):
        spots = []
        for wanted in (far, near):
            spots.append(spot if wanted else count)
            spot += wanted
        for array, core_0, core_1 in ((bases[2 * at], *spots), (bases[2 * at + 1], *spots[::-1])):
            start = pl.multiple_of(jnp.where(face_id == 0, core_0, core_1) * dof_count, dof_count)
            basis_ref[pl.ds(start, dof_count), :] = array[0]

    tile_blocks = blocks_own // TILES
    for tile in range(TILES):
        at = slice(tile * tile_blocks, (tile + 1) * tile_blocks)
        values = pumped_ref[at].astype(jnp.float32)
        for spot in range(count):
            scaled = (values * weight_ref[spot, at][:, None, :]).astype(jnp.bfloat16)
            scaled_ref[tile % 2, :, spot * dof_count : (spot + 1) * dof_count] = scaled.reshape(
                tile_blocks * columns, dof_count
            )
        total = jnp.dot(
            scaled_ref[tile % 2], basis_ref[: count * dof_count, :], preferred_element_type=jnp.float32
        )
        out_ref[at] = total.reshape(tile_blocks, columns, dof_count) + sum_ref[at]


def last_kernel(pumped_ref, sum_ref, projection_ref, *refs):
    arrays, (result_ref, weight_ref, basis_ref, scaled_ref, out_ref, sems) = refs[:-6], refs[-6:]
    blocks_own, columns, dof_count = pumped_ref.shape
    count = weight_ref.shape[0]
    for at in range(count):
        basis, basis_swapped, pack, pack_swapped = arrays[4 * at : 4 * at + 4]
        weight_ref[at] = block_weights((pack, pack_swapped), pack.shape[0] - ROW_TILE, blocks_own)
        for core, array in ((1, basis), (0, basis_swapped)):

            @pl.when(lax.axis_index("face") == core)
            def _():
                basis_ref[at * dof_count : (at + 1) * dof_count, :] = array[0]

    tiles = sems.shape[0]
    tile_blocks = blocks_own // tiles
    copies = []
    for tile in range(tiles):
        at = slice(tile * tile_blocks, (tile + 1) * tile_blocks)
        values = pumped_ref[at].astype(jnp.float32)
        for spot in range(count):
            scaled = (values * weight_ref[spot, at][:, None, :]).astype(jnp.bfloat16)
            scaled_ref[tile % 2, :, spot * dof_count : (spot + 1) * dof_count] = scaled.reshape(
                tile_blocks * columns, dof_count
            )
        total = jnp.dot(scaled_ref[tile % 2], basis_ref[...], preferred_element_type=jnp.float32)
        total = total + sum_ref[at].reshape(tile_blocks * columns, dof_count)
        result = jnp.dot(
            total.astype(jnp.bfloat16), projection_ref[...], preferred_element_type=jnp.float32
        )
        out_ref[at] = result.reshape(tile_blocks, columns, dof_count)
        copies.append(pltpu.make_async_copy(out_ref.at[at], result_ref.at[at], sems.at[tile]))
        copies[-1].start()
    for copy in copies:
        copy.wait()


def on_device(
    mortar_in, pump_rate, well_cell, face_owner, face_slot, face_scale, section, basis, projection
):
    blocks_dev, cols_dev, dof_count = mortar_in.shape
    faces_dev = face_slot.shape[0]
    subdomains, rights, halves = lax.axis_size("sub"), lax.axis_size("rhs"), lax.axis_size("face")
    others = subdomains - 1
    blocks_own = blocks_dev // halves
    capacity = max(2, 2 * faces_dev // subdomains)
    pack_rows = -(-capacity // ROW_TILE) * ROW_TILE + ROW_TILE
    block_shape = (blocks_own, cols_dev, dof_count)
    swap = [(i, i ^ 1) for i in range(halves)]

    def flat(sub, right, face):
        return (sub * rights + right) * halves + face

    partners = sorted(range(1, subdomains), key=lambda p: (p < subdomains // 2, p))
    groups = [partners[i : i + 3] for i in range(0, others, 3)]
    groups = [tuple(g) if len(g) == 3 else (g[0], g[-1], g[0]) for g in groups]
    firsts = []
    for a, b, c in groups:
        pairs = [
            (flat(s, r, face), flat(s ^ (c if face else b if r % 2 else a), r, face))
            for s in range(subdomains)
            for r in range(rights)
            for face in range(halves)
        ]
        firsts.append(lax.ppermute(basis, ("sub", "rhs", "face"), pairs))

    kinds = [(a != b, c != a or a == b) for a, b, c in groups]
    ways = [(0, 0)]
    for (a, b, c), (far, near) in zip(groups, kinds):
        ways += [(a, b)] * far + [(c, c)] * near
    packs = pl.pallas_call(
        functools.partial(pack_kernel, ways),
        out_shape=[jax.ShapeDtypeStruct((pack_rows, dof_count), jnp.bfloat16)] * len(ways),
        in_specs=[VMEM, VMEM, VMEM, SMEM],
        out_specs=[VMEM] * len(ways),
        cost_estimate=WORK,
        name="pack_weights",
    )(face_owner.reshape(1, faces_dev), face_slot.reshape(1, faces_dev), face_scale, section)
    arrived = []
    for (even, odd), pack in zip(ways[1:], packs[1:]):
        pairs = [
            (s * rights + r, (s ^ (odd if r % 2 else even)) * rights + r)
            for s in range(subdomains)
            for r in range(rights)
        ]
        arrived.append(lax.ppermute(pack, ("sub", "rhs"), pairs))
    own_swapped = lax.ppermute(packs[0], "face", swap)

    pumped = pl.pallas_call(
        pump_kernel,
        out_shape=jax.ShapeDtypeStruct(block_shape, jnp.bfloat16),
        in_specs=[HBM, SMEM, SMEM],
        out_specs=VMEM,
        scratch_shapes=[pltpu.SemaphoreType.DMA(())],
        compiler_params=pltpu.CompilerParams(vmem_limit_bytes=32 * MIB),
        cost_estimate=LIGHT,
        name="pump",
    )(mortar_in, pump_rate, well_cell)
    own_sum = pl.pallas_call(
        own_kernel,
        out_shape=jax.ShapeDtypeStruct(block_shape, jnp.float32),
        in_specs=[VMEM] * 4,
        out_specs=VMEM,
        scratch_shapes=[pltpu.VMEM((blocks_own, dof_count), jnp.float32)],
        compiler_params=pltpu.CompilerParams(vmem_limit_bytes=32 * MIB),
        cost_estimate=LIGHT,
        name="own_blocks",
    )(pumped, basis, packs[0], own_swapped)

    firsts, arrived, own_sum = lax.optimization_barrier((firsts, arrived, own_sum))
    pairs = [
        (r * halves + face, r * halves if face else (r ^ 1) * halves + 1)
        for r in range(rights)
        for face in range(halves)
    ]
    cross = [(i, i ^ 1) for i in range(rights)]
    early, late = [], []
    for (far, _), first in zip(kinds, firsts):
        early += [first, lax.ppermute(first, "face", swap)]
        if far:
            second = lax.ppermute(first, ("rhs", "face"), pairs)
            late.append([second, lax.ppermute(second, "face", swap)])
    weights, others_late = [], iter(late)
    for (even, odd), array in zip(ways[1:], arrived):
        weights += [array, lax.ppermute(array, "face", swap)]
        if even != odd:
            second = lax.ppermute(array, "rhs", cross)
            next(others_late).extend([second, lax.ppermute(second, "face", swap)])

    late_count = len(late)
    count = others - late_count
    operands = [pumped, own_sum, *early, *weights]
    total = pl.pallas_call(
        functools.partial(stage_kernel, kinds),
        out_shape=jax.ShapeDtypeStruct(block_shape, jnp.float32),
        in_specs=[VMEM] * len(operands),
        out_specs=VMEM,
        scratch_shapes=[
            pltpu.VMEM((count, blocks_own, dof_count), jnp.float32),
            pltpu.VMEM(((count + 1) * dof_count, dof_count), jnp.bfloat16),
            pltpu.VMEM((2, blocks_own // TILES * cols_dev, count * dof_count), jnp.bfloat16),
        ],
        input_output_aliases={1: 0},
        compiler_params=pltpu.CompilerParams(vmem_limit_bytes=40 * MIB),
        cost_estimate=WORK,
        name="stage",
    )(*operands)

    operands = [pumped, total, projection, *sum(late, [])]
    return pl.pallas_call(
        last_kernel,
        out_shape=jax.ShapeDtypeStruct(block_shape, jnp.float32),
        in_specs=[VMEM] * len(operands),
        out_specs=HBM,
        scratch_shapes=[
            pltpu.VMEM((late_count, blocks_own, dof_count), jnp.float32),
            pltpu.VMEM((late_count * dof_count, dof_count), jnp.bfloat16),
            pltpu.VMEM((2, blocks_own // LAST_TILES * cols_dev, late_count * dof_count), jnp.bfloat16),
            pltpu.VMEM(block_shape, jnp.float32),
            pltpu.SemaphoreType.DMA((LAST_TILES,)),
        ],
        compiler_params=pltpu.CompilerParams(vmem_limit_bytes=40 * MIB),
        name="last_stage",
    )(*operands)


def solution(mesh):
    in_specs = (
        P(("groups", "sub"), "rhs", None),
        P(("groups", "rhs")),
        P(("groups", "rhs")),
        P(("groups", "sub", "face"), None),
        P(("groups", "sub", "face")),
        P(("groups", "sub", "face"), None),
        P(("groups", "sub")),
        P(("groups", "sub"), None, None),
        P(),
    )
    out_specs = P(("groups", "sub", "face"), "rhs", None)
    return jax.shard_map(
        on_device, mesh=mesh, in_specs=in_specs, out_specs=out_specs, check_vma=False
    )
```

```python
import functools

import jax
import jax.numpy as jnp
from jax import lax
from jax.experimental import pallas as pl
from jax.experimental.pallas import tpu as pltpu
from jax.sharding import PartitionSpec as P

ROW_TILE = 16
VMEM = pl.BlockSpec(memory_space=pltpu.VMEM)
HBM = pl.BlockSpec(memory_space=pltpu.HBM)
SMEM = pl.BlockSpec(memory_space=pltpu.SMEM)
MIB = 1024 * 1024
TILES = 4
LAST_TILES = 8
LIGHT = pl.CostEstimate(flops=1_000_000, bytes_accessed=1024, transcendentals=0)
WORK = pl.CostEstimate(flops=4_000_000_000, bytes_accessed=8 * MIB, transcendentals=0)


def on_even(even, odd):
    return jnp.where(lax.rem(lax.axis_index("rhs"), 2) == 0, even, odd)


def pack_kernel(partners, owner_ref, slot_ref, scale_ref, section_ref, *packs):
    rows, dof_count = packs[0].shape
    rows -= ROW_TILE
    faces = owner_ref.shape[1]
    sign = (1 - 2 * section_ref[0]).astype(jnp.float32)
    here = lax.axis_index("sub")
    owners = jnp.concatenate(
        [jnp.full((1, faces), here ^ on_even(even, odd), jnp.int32) for even, odd in partners], axis=0
    )
    named = owners == owner_ref[...]
    earlier = lax.broadcasted_iota(jnp.int32, (faces, faces), 0) < lax.broadcasted_iota(
        jnp.int32, (faces, faces), 1
    )
    rank = jnp.dot(
        named.astype(jnp.bfloat16), earlier.astype(jnp.bfloat16), preferred_element_type=jnp.float32
    )
    place = jnp.where(named, rank, -1.0)
    at = lax.broadcasted_iota(jnp.int32, (rows, faces), 0).astype(jnp.float32)
    hit = jnp.concatenate([place[p : p + 1, :] == at for p in range(len(packs))], axis=0)
    hit = hit.astype(jnp.bfloat16)
    packed = jnp.dot(hit, scale_ref[...], preferred_element_type=jnp.float32) * sign
    listed = lax.dot_general(
        slot_ref[...].astype(jnp.bfloat16), hit, (((1,), (1,)), ((), ())), preferred_element_type=jnp.float32
    )
    packed = packed.astype(jnp.bfloat16)
    for p, pack_ref in enumerate(packs):
        pack_ref[:rows, :] = packed[p * rows : (p + 1) * rows, :]
        meta = jnp.concatenate(
            [listed[:, p * rows : (p + 1) * rows], jnp.zeros((1, dof_count - rows), jnp.float32)], axis=1
        )
        pack_ref[rows:, :] = jnp.broadcast_to(meta, (ROW_TILE, dof_count)).astype(jnp.bfloat16)


def block_weights(packs, rows, blocks_own):
    first = lax.axis_index("face") * blocks_own
    block_ids = first + lax.broadcasted_iota(jnp.int32, (blocks_own, rows), 0)
    total = None
    for pack in packs:
        slots = pack[rows : rows + ROW_TILE, :].astype(jnp.int32)[:1, :rows]
        hit = (slots == block_ids).astype(jnp.bfloat16)
        part = jnp.dot(hit, pack[:rows, :], preferred_element_type=jnp.float32)
        total = part if total is None else total + part
    return total


def pump_kernel(mortar_ref, rate_ref, cell_ref, pumped_ref, sem):
    blocks_own, columns, dof_count = pumped_ref.shape
    first_block = lax.axis_index("face") * blocks_own
    fetch = pltpu.make_async_copy(mortar_ref.at[pl.ds(first_block, blocks_own)], pumped_ref, sem)
    fetch.start()
    fetch.wait()
    base = lax.axis_index("sub") * mortar_ref.shape[0] + first_block
    for column in range(columns):
        block = lax.div(cell_ref[column], dof_count) - base
        dof = lax.rem(cell_ref[column], dof_count)

        @pl.when((block >= 0) & (block < blocks_own))
        def _():
            slab = slice(column // ROW_TILE * ROW_TILE, (column // ROW_TILE + 1) * ROW_TILE)
            shape = (ROW_TILE, dof_count)
            at_well = (lax.broadcasted_iota(jnp.int32, shape, 0) == column % ROW_TILE) & (
                lax.broadcasted_iota(jnp.int32, shape, 1) == dof
            )
            well = jnp.where(at_well, rate_ref[column], 0.0)
            pumped_ref[block, slab, :] = (pumped_ref[block, slab, :].astype(jnp.float32) + well).astype(
                jnp.bfloat16
            )


def own_kernel(pumped_ref, basis_ref, pack_ref, swapped_ref, sum_ref, weight_ref):
    blocks_own, columns, dof_count = pumped_ref.shape
    weight_ref[...] = block_weights((pack_ref, swapped_ref), pack_ref.shape[0] - ROW_TILE, blocks_own)
    tile_blocks = blocks_own // TILES
    for tile in range(TILES):
        at = slice(tile * tile_blocks, (tile + 1) * tile_blocks)
        scaled = (pumped_ref[at].astype(jnp.float32) * weight_ref[at][:, None, :]).astype(jnp.bfloat16)
        flux = jnp.dot(
            scaled.reshape(tile_blocks * columns, dof_count), basis_ref[0], preferred_element_type=jnp.float32
        )
        sum_ref[at] = flux.reshape(tile_blocks, columns, dof_count)


def stage_kernel(kinds, pumped_ref, sum_ref, *refs):
    bases, refs = refs[: 2 * len(kinds)], refs[2 * len(kinds) :]
    packs, (out_ref, weight_ref, basis_ref, scaled_ref) = refs[:-4], refs[-4:]
    blocks_own, columns, dof_count = pumped_ref.shape
    face_id = lax.axis_index("face")
    rows = packs[0].shape[0] - ROW_TILE
    count = weight_ref.shape[0]
    for spot in range(count):
        weight_ref[spot] = block_weights(packs[2 * spot : 2 * spot + 2], rows, blocks_own)
    spot = 0
    for at, (far, near) in enumerate(kinds):
        spots = []
        for wanted in (far, near):
            spots.append(spot if wanted else count)
            spot += wanted
        for array, core_0, core_1 in ((bases[2 * at], *spots), (bases[2 * at + 1], *spots[::-1])):
            start = pl.multiple_of(jnp.where(face_id == 0, core_0, core_1) * dof_count, dof_count)
            basis_ref[pl.ds(start, dof_count), :] = array[0]

    tile_blocks = blocks_own // TILES
    for tile in range(TILES):
        at = slice(tile * tile_blocks, (tile + 1) * tile_blocks)
        values = pumped_ref[at].astype(jnp.float32)
        for spot in range(count):
            scaled = (values * weight_ref[spot, at][:, None, :]).astype(jnp.bfloat16)
            scaled_ref[tile % 2, :, spot * dof_count : (spot + 1) * dof_count] = scaled.reshape(
                tile_blocks * columns, dof_count
            )
        total = jnp.dot(
            scaled_ref[tile % 2], basis_ref[: count * dof_count, :], preferred_element_type=jnp.float32
        )
        out_ref[at] = total.reshape(tile_blocks, columns, dof_count) + sum_ref[at]


def last_kernel(pumped_ref, sum_ref, projection_ref, *refs):
    arrays, (result_ref, weight_ref, basis_ref, scaled_ref, out_ref, sems) = refs[:-6], refs[-6:]
    blocks_own, columns, dof_count = pumped_ref.shape
    count = weight_ref.shape[0]
    for at in range(count):
        basis, basis_swapped, pack, pack_swapped = arrays[4 * at : 4 * at + 4]
        weight_ref[at] = block_weights((pack, pack_swapped), pack.shape[0] - ROW_TILE, blocks_own)
        for core, array in ((1, basis), (0, basis_swapped)):

            @pl.when(lax.axis_index("face") == core)
            def _():
                basis_ref[at * dof_count : (at + 1) * dof_count, :] = array[0]

    tiles = sems.shape[0]
    tile_blocks = blocks_own // tiles
    copies = []
    for tile in range(tiles):
        at = slice(tile * tile_blocks, (tile + 1) * tile_blocks)
        values = pumped_ref[at].astype(jnp.float32)
        for spot in range(count):
            scaled = (values * weight_ref[spot, at][:, None, :]).astype(jnp.bfloat16)
            scaled_ref[tile % 2, :, spot * dof_count : (spot + 1) * dof_count] = scaled.reshape(
                tile_blocks * columns, dof_count
            )
        total = jnp.dot(scaled_ref[tile % 2], basis_ref[...], preferred_element_type=jnp.float32)
        total = total + sum_ref[at].reshape(tile_blocks * columns, dof_count)
        result = jnp.dot(
            total.astype(jnp.bfloat16), projection_ref[...], preferred_element_type=jnp.float32
        )
        out_ref[at] = result.reshape(tile_blocks, columns, dof_count)
        copies.append(pltpu.make_async_copy(out_ref.at[at], result_ref.at[at], sems.at[tile]))
        copies[-1].start()
    for copy in copies:
        copy.wait()


def on_device(
    mortar_in, pump_rate, well_cell, face_owner, face_slot, face_scale, section, basis, projection
):
    blocks_dev, cols_dev, dof_count = mortar_in.shape
    faces_dev = face_slot.shape[0]
    subdomains, rights, halves = lax.axis_size("sub"), lax.axis_size("rhs"), lax.axis_size("face")
    others = subdomains - 1
    blocks_own = blocks_dev // halves
    capacity = max(2, 2 * faces_dev // subdomains)
    pack_rows = -(-capacity // ROW_TILE) * ROW_TILE + ROW_TILE
    block_shape = (blocks_own, cols_dev, dof_count)
    swap = [(i, i ^ 1) for i in range(halves)]

    def flat(sub, right, face):
        return (sub * rights + right) * halves + face

    partners = sorted(range(1, subdomains), key=lambda p: (p < subdomains // 2, p))
    groups = [partners[i : i + 3] for i in range(0, others, 3)]
    groups = [tuple(g) if len(g) == 3 else (g[0], g[-1], g[0]) for g in groups]
    firsts = []
    for a, b, c in groups:
        pairs = [
            (flat(s, r, face), flat(s ^ (c if face else b if r % 2 else a), r, face))
            for s in range(subdomains)
            for r in range(rights)
            for face in range(halves)
        ]
        firsts.append(lax.ppermute(basis, ("sub", "rhs", "face"), pairs))

    kinds = [(a != b, c != a or a == b) for a, b, c in groups]
    ways = [(0, 0)]
    for (a, b, c), (far, near) in zip(groups, kinds):
        ways += [(a, b)] * far + [(c, c)] * near
    packs = pl.pallas_call(
        functools.partial(pack_kernel, ways),
        out_shape=[jax.ShapeDtypeStruct((pack_rows, dof_count), jnp.bfloat16)] * len(ways),
        in_specs=[VMEM, VMEM, VMEM, SMEM],
        out_specs=[VMEM] * len(ways),
        cost_estimate=WORK,
        name="pack_weights",
    )(face_owner.reshape(1, faces_dev), face_slot.reshape(1, faces_dev), face_scale, section)
    arrived = []
    for (even, odd), pack in zip(ways[1:], packs[1:]):
        pairs = [
            (s * rights + r, (s ^ (odd if r % 2 else even)) * rights + r)
            for s in range(subdomains)
            for r in range(rights)
        ]
        arrived.append(lax.ppermute(pack, ("sub", "rhs"), pairs))
    own_swapped = lax.ppermute(packs[0], "face", swap)

    pumped = pl.pallas_call(
        pump_kernel,
        out_shape=jax.ShapeDtypeStruct(block_shape, jnp.bfloat16),
        in_specs=[HBM, SMEM, SMEM],
        out_specs=VMEM,
        scratch_shapes=[pltpu.SemaphoreType.DMA(())],
        compiler_params=pltpu.CompilerParams(vmem_limit_bytes=32 * MIB),
        cost_estimate=LIGHT,
        name="pump",
    )(mortar_in, pump_rate, well_cell)
    own_sum = pl.pallas_call(
        own_kernel,
        out_shape=jax.ShapeDtypeStruct(block_shape, jnp.float32),
        in_specs=[VMEM] * 4,
        out_specs=VMEM,
        scratch_shapes=[pltpu.VMEM((blocks_own, dof_count), jnp.float32)],
        compiler_params=pltpu.CompilerParams(vmem_limit_bytes=32 * MIB),
        cost_estimate=WORK,
        name="own_blocks",
    )(pumped, basis, packs[0], own_swapped)

    pairs = [
        (r * halves + face, r * halves if face else (r ^ 1) * halves + 1)
        for r in range(rights)
        for face in range(halves)
    ]
    cross = [(i, i ^ 1) for i in range(rights)]
    early, late = [], []
    for (far, _), first in zip(kinds, firsts):
        early += [first, lax.ppermute(first, "face", swap)]
        if far:
            second = lax.ppermute(first, ("rhs", "face"), pairs)
            late.append([second, lax.ppermute(second, "face", swap)])
    arrived, own_sum, early = lax.optimization_barrier((arrived, own_sum, early))
    weights, others_late = [], iter(late)
    for (even, odd), array in zip(ways[1:], arrived):
        weights += [array, lax.ppermute(array, "face", swap)]
        if even != odd:
            second = lax.ppermute(array, "rhs", cross)
            next(others_late).extend([second, lax.ppermute(second, "face", swap)])

    late_count = len(late)
    count = others - late_count
    operands = [pumped, own_sum, *early, *weights]
    total = pl.pallas_call(
        functools.partial(stage_kernel, kinds),
        out_shape=jax.ShapeDtypeStruct(block_shape, jnp.float32),
        in_specs=[VMEM] * len(operands),
        out_specs=VMEM,
        scratch_shapes=[
            pltpu.VMEM((count, blocks_own, dof_count), jnp.float32),
            pltpu.VMEM(((count + 1) * dof_count, dof_count), jnp.bfloat16),
            pltpu.VMEM((2, blocks_own // TILES * cols_dev, count * dof_count), jnp.bfloat16),
        ],
        input_output_aliases={1: 0},
        compiler_params=pltpu.CompilerParams(vmem_limit_bytes=40 * MIB),
        cost_estimate=WORK,
        name="stage",
    )(*operands)

    operands = [pumped, total, projection, *sum(late, [])]
    return pl.pallas_call(
        last_kernel,
        out_shape=jax.ShapeDtypeStruct(block_shape, jnp.float32),
        in_specs=[VMEM] * len(operands),
        out_specs=HBM,
        scratch_shapes=[
            pltpu.VMEM((late_count, blocks_own, dof_count), jnp.float32),
            pltpu.VMEM((late_count * dof_count, dof_count), jnp.bfloat16),
            pltpu.VMEM((2, blocks_own // LAST_TILES * cols_dev, late_count * dof_count), jnp.bfloat16),
            pltpu.VMEM(block_shape, jnp.float32),
            pltpu.SemaphoreType.DMA((LAST_TILES,)),
        ],
        compiler_params=pltpu.CompilerParams(vmem_limit_bytes=40 * MIB),
        name="last_stage",
    )(*operands)


def solution(mesh):
    in_specs = (
        P(("groups", "sub"), "rhs", None),
        P(("groups", "rhs")),
        P(("groups", "rhs")),
        P(("groups", "sub", "face"), None),
        P(("groups", "sub", "face")),
        P(("groups", "sub", "face"), None),
        P(("groups", "sub")),
        P(("groups", "sub"), None, None),
        P(),
    )
    out_specs = P(("groups", "sub", "face"), "rhs", None)
    return jax.shard_map(
        on_device, mesh=mesh, in_specs=in_specs, out_specs=out_specs, check_vma=False
    )
```

```python
import functools

import jax
import jax.numpy as jnp
from jax import lax
from jax.experimental import pallas as pl
from jax.experimental.pallas import tpu as pltpu
from jax.sharding import PartitionSpec as P

ROW_TILE = 16
VMEM = pl.BlockSpec(memory_space=pltpu.VMEM)
HBM = pl.BlockSpec(memory_space=pltpu.HBM)
SMEM = pl.BlockSpec(memory_space=pltpu.SMEM)
MIB = 1024 * 1024
TILES = 4
LAST_TILES = 8
LIGHT = pl.CostEstimate(flops=1_000_000, bytes_accessed=1024, transcendentals=0)
WORK = pl.CostEstimate(flops=4_000_000_000, bytes_accessed=8 * MIB, transcendentals=0)


def on_even(even, odd):
    return jnp.where(lax.rem(lax.axis_index("rhs"), 2) == 0, even, odd)


def pack_kernel(partners, owner_ref, slot_ref, scale_ref, section_ref, *packs):
    rows, dof_count = packs[0].shape
    rows -= ROW_TILE
    faces = owner_ref.shape[1]
    sign = (1 - 2 * section_ref[0]).astype(jnp.float32)
    here = lax.axis_index("sub")
    owners = jnp.concatenate(
        [jnp.full((1, faces), here ^ on_even(even, odd), jnp.int32) for even, odd in partners], axis=0
    )
    named = owners == owner_ref[...]
    earlier = lax.broadcasted_iota(jnp.int32, (faces, faces), 0) < lax.broadcasted_iota(
        jnp.int32, (faces, faces), 1
    )
    rank = jnp.dot(
        named.astype(jnp.bfloat16), earlier.astype(jnp.bfloat16), preferred_element_type=jnp.float32
    )
    place = jnp.where(named, rank, -1.0)
    at = lax.broadcasted_iota(jnp.int32, (rows, faces), 0).astype(jnp.float32)
    hit = jnp.concatenate([place[p : p + 1, :] == at for p in range(len(packs))], axis=0)
    hit = hit.astype(jnp.bfloat16)
    packed = jnp.dot(hit, scale_ref[...], preferred_element_type=jnp.float32) * sign
    listed = lax.dot_general(
        slot_ref[...].astype(jnp.bfloat16), hit, (((1,), (1,)), ((), ())), preferred_element_type=jnp.float32
    )
    packed = packed.astype(jnp.bfloat16)
    for p, pack_ref in enumerate(packs):
        pack_ref[:rows, :] = packed[p * rows : (p + 1) * rows, :]
        meta = jnp.concatenate(
            [listed[:, p * rows : (p + 1) * rows], jnp.zeros((1, dof_count - rows), jnp.float32)], axis=1
        )
        pack_ref[rows:, :] = jnp.broadcast_to(meta, (ROW_TILE, dof_count)).astype(jnp.bfloat16)


def block_weights(packs, rows, blocks_own):
    first = lax.axis_index("face") * blocks_own
    block_ids = first + lax.broadcasted_iota(jnp.int32, (blocks_own, rows), 0)
    total = None
    for pack in packs:
        slots = pack[rows : rows + ROW_TILE, :].astype(jnp.int32)[:1, :rows]
        hit = (slots == block_ids).astype(jnp.bfloat16)
        part = jnp.dot(hit, pack[:rows, :], preferred_element_type=jnp.float32)
        total = part if total is None else total + part
    return total


def own_kernel(mortar_ref, rate_ref, cell_ref, basis_ref, pack_ref, swapped_ref, pumped_ref, sum_ref, weight_ref, sem):
    blocks_own, columns, dof_count = pumped_ref.shape
    first_block = lax.axis_index("face") * blocks_own
    fetch = pltpu.make_async_copy(mortar_ref.at[pl.ds(first_block, blocks_own)], pumped_ref, sem)
    fetch.start()
    weight_ref[...] = block_weights((pack_ref, swapped_ref), pack_ref.shape[0] - ROW_TILE, blocks_own)
    fetch.wait()

    base = lax.axis_index("sub") * mortar_ref.shape[0] + first_block
    for column in range(columns):
        block = lax.div(cell_ref[column], dof_count) - base
        dof = lax.rem(cell_ref[column], dof_count)

        @pl.when((block >= 0) & (block < blocks_own))
        def _():
            slab = slice(column // ROW_TILE * ROW_TILE, (column // ROW_TILE + 1) * ROW_TILE)
            shape = (ROW_TILE, dof_count)
            at_well = (lax.broadcasted_iota(jnp.int32, shape, 0) == column % ROW_TILE) & (
                lax.broadcasted_iota(jnp.int32, shape, 1) == dof
            )
            well = jnp.where(at_well, rate_ref[column], 0.0)
            pumped_ref[block, slab, :] = (pumped_ref[block, slab, :].astype(jnp.float32) + well).astype(
                jnp.bfloat16
            )

    tile_blocks = blocks_own // TILES
    for tile in range(TILES):
        at = slice(tile * tile_blocks, (tile + 1) * tile_blocks)
        scaled = (pumped_ref[at].astype(jnp.float32) * weight_ref[at][:, None, :]).astype(jnp.bfloat16)
        flux = jnp.dot(
            scaled.reshape(tile_blocks * columns, dof_count), basis_ref[0], preferred_element_type=jnp.float32
        )
        sum_ref[at] = flux.reshape(tile_blocks, columns, dof_count)


def stage_kernel(kinds, pumped_ref, sum_ref, *refs):
    bases, refs = refs[: 2 * len(kinds)], refs[2 * len(kinds) :]
    packs, (out_ref, weight_ref, basis_ref, scaled_ref) = refs[:-4], refs[-4:]
    blocks_own, columns, dof_count = pumped_ref.shape
    face_id = lax.axis_index("face")
    rows = packs[0].shape[0] - ROW_TILE
    count = weight_ref.shape[0]
    for spot in range(count):
        weight_ref[spot] = block_weights(packs[2 * spot : 2 * spot + 2], rows, blocks_own)
    spot = 0
    for at, (far, near) in enumerate(kinds):
        spots = []
        for wanted in (far, near):
            spots.append(spot if wanted else count)
            spot += wanted
        for array, core_0, core_1 in ((bases[2 * at], *spots), (bases[2 * at + 1], *spots[::-1])):
            start = pl.multiple_of(jnp.where(face_id == 0, core_0, core_1) * dof_count, dof_count)
            basis_ref[pl.ds(start, dof_count), :] = array[0]

    tile_blocks = blocks_own // TILES
    for tile in range(TILES):
        at = slice(tile * tile_blocks, (tile + 1) * tile_blocks)
        values = pumped_ref[at].astype(jnp.float32)
        for spot in range(count):
            scaled = (values * weight_ref[spot, at][:, None, :]).astype(jnp.bfloat16)
            scaled_ref[tile % 2, :, spot * dof_count : (spot + 1) * dof_count] = scaled.reshape(
                tile_blocks * columns, dof_count
            )
        total = jnp.dot(
            scaled_ref[tile % 2], basis_ref[: count * dof_count, :], preferred_element_type=jnp.float32
        )
        out_ref[at] = total.reshape(tile_blocks, columns, dof_count) + sum_ref[at]


def last_kernel(pumped_ref, sum_ref, projection_ref, *refs):
    arrays, (result_ref, weight_ref, basis_ref, scaled_ref, out_ref, sems) = refs[:-6], refs[-6:]
    blocks_own, columns, dof_count = pumped_ref.shape
    count = weight_ref.shape[0]
    for at in range(count):
        basis, basis_swapped, pack, pack_swapped = arrays[4 * at : 4 * at + 4]
        weight_ref[at] = block_weights((pack, pack_swapped), pack.shape[0] - ROW_TILE, blocks_own)
        for core, array in ((1, basis), (0, basis_swapped)):

            @pl.when(lax.axis_index("face") == core)
            def _():
                basis_ref[at * dof_count : (at + 1) * dof_count, :] = array[0]

    tiles = sems.shape[0]
    tile_blocks = blocks_own // tiles
    copies = []
    for tile in range(tiles):
        at = slice(tile * tile_blocks, (tile + 1) * tile_blocks)
        values = pumped_ref[at].astype(jnp.float32)
        for spot in range(count):
            scaled = (values * weight_ref[spot, at][:, None, :]).astype(jnp.bfloat16)
            scaled_ref[tile % 2, :, spot * dof_count : (spot + 1) * dof_count] = scaled.reshape(
                tile_blocks * columns, dof_count
            )
        total = jnp.dot(scaled_ref[tile % 2], basis_ref[...], preferred_element_type=jnp.float32)
        total = total + sum_ref[at].reshape(tile_blocks * columns, dof_count)
        result = jnp.dot(
            total.astype(jnp.bfloat16), projection_ref[...], preferred_element_type=jnp.float32
        )
        out_ref[at] = result.reshape(tile_blocks, columns, dof_count)
        copies.append(pltpu.make_async_copy(out_ref.at[at], result_ref.at[at], sems.at[tile]))
        copies[-1].start()
    for copy in copies:
        copy.wait()


def on_device(
    mortar_in, pump_rate, well_cell, face_owner, face_slot, face_scale, section, basis, projection
):
    blocks_dev, cols_dev, dof_count = mortar_in.shape
    faces_dev = face_slot.shape[0]
    subdomains, rights, halves = lax.axis_size("sub"), lax.axis_size("rhs"), lax.axis_size("face")
    others = subdomains - 1
    blocks_own = blocks_dev // halves
    capacity = max(2, 2 * faces_dev // subdomains)
    pack_rows = -(-capacity // ROW_TILE) * ROW_TILE + ROW_TILE
    block_shape = (blocks_own, cols_dev, dof_count)
    swap = [(i, i ^ 1) for i in range(halves)]

    def flat(sub, right, face):
        return (sub * rights + right) * halves + face

    partners = sorted(range(1, subdomains), key=lambda p: (p < subdomains // 2, p))
    groups = [partners[i : i + 3] for i in range(0, others, 3)]
    groups = [tuple(g) if len(g) == 3 else (g[0], g[-1], g[0]) for g in groups]
    firsts = []
    for a, b, c in groups:
        pairs = [
            (flat(s, r, face), flat(s ^ (c if face else b if r % 2 else a), r, face))
            for s in range(subdomains)
            for r in range(rights)
            for face in range(halves)
        ]
        firsts.append(lax.ppermute(basis, ("sub", "rhs", "face"), pairs))

    kinds = [(a != b, c != a or a == b) for a, b, c in groups]
    near = [(c, c) for (_, _, c), (_, has) in zip(groups, kinds) if has]
    far = [(a, b) for (a, b, _), (has, _) in zip(groups, kinds) if has]
    ways = [(0, 0), *near, *far, *[(b, a) for a, b in far]]
    packs = pl.pallas_call(
        functools.partial(pack_kernel, ways),
        out_shape=[jax.ShapeDtypeStruct((pack_rows, dof_count), jnp.bfloat16)] * len(ways),
        in_specs=[VMEM, VMEM, VMEM, SMEM],
        out_specs=[VMEM] * len(ways),
        cost_estimate=WORK,
        name="pack_weights",
    )(face_owner.reshape(1, faces_dev), face_slot.reshape(1, faces_dev), face_scale, section)

    def along_sub(way, pack):
        pairs = [
            (s * rights + r, (s ^ way[r % 2]) * rights + r) for s in range(subdomains) for r in range(rights)
        ]
        return lax.ppermute(pack, ("sub", "rhs"), pairs)

    early_count = 1 + len(near) + len(far)
    arrived = [along_sub(way, pack) for way, pack in zip(ways[1:early_count], packs[1:])]
    own_swapped = lax.ppermute(packs[0], "face", swap)

    firsts, own_swapped = lax.optimization_barrier((firsts, own_swapped))
    pumped, own_sum = pl.pallas_call(
        own_kernel,
        out_shape=[
            jax.ShapeDtypeStruct(block_shape, jnp.bfloat16),
            jax.ShapeDtypeStruct(block_shape, jnp.float32),
        ],
        in_specs=[HBM, SMEM, SMEM, VMEM, VMEM, VMEM],
        out_specs=[VMEM, VMEM],
        scratch_shapes=[pltpu.VMEM((blocks_own, dof_count), jnp.float32), pltpu.SemaphoreType.DMA(())],
        compiler_params=pltpu.CompilerParams(vmem_limit_bytes=32 * MIB),
        cost_estimate=WORK,
        name="own_blocks",
    )(mortar_in, pump_rate, well_cell, basis, packs[0], own_swapped)

    pairs = [
        (r * halves + face, r * halves if face else (r ^ 1) * halves + 1)
        for r in range(rights)
        for face in range(halves)
    ]
    early, late = [], []
    for (has_far, _), first in zip(kinds, firsts):
        early += [first, lax.ppermute(first, "face", swap)]
        if has_far:
            second = lax.ppermute(first, ("rhs", "face"), pairs)
            late.append([second, lax.ppermute(second, "face", swap)])
    *late_packs, firsts = lax.optimization_barrier((*packs[early_count:], firsts))
    late_arrived = [along_sub(way, pack) for way, pack in zip(ways[early_count:], late_packs)]
    arrived, own_sum, early = lax.optimization_barrier((arrived, own_sum, early))
    swapped = [lax.ppermute(array, "face", swap) for array in arrived]
    places = dict(zip(ways[1:early_count], zip(arrived, swapped)))
    weights = []
    for (a, b, c), (has_far, has_near) in zip(groups, kinds):
        weights += list(places[a, b]) * has_far + list(places[c, c]) * has_near
    for arrays, array in zip(late, late_arrived):
        arrays += [array, lax.ppermute(array, "face", swap)]

    late_count = len(late)
    count = others - late_count
    operands = [pumped, own_sum, *early, *weights]
    total = pl.pallas_call(
        functools.partial(stage_kernel, kinds),
        out_shape=jax.ShapeDtypeStruct(block_shape, jnp.float32),
        in_specs=[VMEM] * len(operands),
        out_specs=VMEM,
        scratch_shapes=[
            pltpu.VMEM((count, blocks_own, dof_count), jnp.float32),
            pltpu.VMEM(((count + 1) * dof_count, dof_count), jnp.bfloat16),
            pltpu.VMEM((2, blocks_own // TILES * cols_dev, count * dof_count), jnp.bfloat16),
        ],
        input_output_aliases={1: 0},
        compiler_params=pltpu.CompilerParams(vmem_limit_bytes=40 * MIB),
        cost_estimate=WORK,
        name="stage",
    )(*operands)

    operands = [pumped, total, projection, *sum(late, [])]
    return pl.pallas_call(
        last_kernel,
        out_shape=jax.ShapeDtypeStruct(block_shape, jnp.float32),
        in_specs=[VMEM] * len(operands),
        out_specs=HBM,
        scratch_shapes=[
            pltpu.VMEM((late_count, blocks_own, dof_count), jnp.float32),
            pltpu.VMEM((late_count * dof_count, dof_count), jnp.bfloat16),
            pltpu.VMEM((2, blocks_own // LAST_TILES * cols_dev, late_count * dof_count), jnp.bfloat16),
            pltpu.VMEM(block_shape, jnp.float32),
            pltpu.SemaphoreType.DMA((LAST_TILES,)),
        ],
        compiler_params=pltpu.CompilerParams(vmem_limit_bytes=40 * MIB),
        name="last_stage",
    )(*operands)


def solution(mesh):
    in_specs = (
        P(("groups", "sub"), "rhs", None),
        P(("groups", "rhs")),
        P(("groups", "rhs")),
        P(("groups", "sub", "face"), None),
        P(("groups", "sub", "face")),
        P(("groups", "sub", "face"), None),
        P(("groups", "sub")),
        P(("groups", "sub"), None, None),
        P(),
    )
    out_specs = P(("groups", "sub", "face"), "rhs", None)
    return jax.shard_map(
        on_device, mesh=mesh, in_specs=in_specs, out_specs=out_specs, check_vma=False
    )
```

```python
import functools

import jax
import jax.numpy as jnp
from jax import lax
from jax.experimental import pallas as pl
from jax.experimental.pallas import tpu as pltpu
from jax.sharding import PartitionSpec as P

ROW_TILE = 16
VMEM = pl.BlockSpec(memory_space=pltpu.VMEM)
HBM = pl.BlockSpec(memory_space=pltpu.HBM)
SMEM = pl.BlockSpec(memory_space=pltpu.SMEM)
MIB = 1024 * 1024
TILES = 4
LAST_TILES = 8
LIGHT = pl.CostEstimate(flops=1_000_000, bytes_accessed=1024, transcendentals=0)
WORK = pl.CostEstimate(flops=4_000_000_000, bytes_accessed=8 * MIB, transcendentals=0)


def on_even(even, odd):
    return jnp.where(lax.rem(lax.axis_index("rhs"), 2) == 0, even, odd)


def pack_kernel(partners, owner_ref, slot_ref, scale_ref, section_ref, *packs):
    rows, dof_count = packs[0].shape
    rows -= ROW_TILE
    faces = owner_ref.shape[1]
    sign = (1 - 2 * section_ref[0]).astype(jnp.float32)
    here = lax.axis_index("sub")
    owners = jnp.concatenate(
        [jnp.full((1, faces), here ^ on_even(even, odd), jnp.int32) for even, odd in partners], axis=0
    )
    named = owners == owner_ref[...]
    earlier = lax.broadcasted_iota(jnp.int32, (faces, faces), 0) < lax.broadcasted_iota(
        jnp.int32, (faces, faces), 1
    )
    rank = jnp.dot(
        named.astype(jnp.bfloat16), earlier.astype(jnp.bfloat16), preferred_element_type=jnp.float32
    )
    place = jnp.where(named, rank, -1.0)
    at = lax.broadcasted_iota(jnp.int32, (rows, faces), 0).astype(jnp.float32)
    hit = jnp.concatenate([place[p : p + 1, :] == at for p in range(len(packs))], axis=0)
    hit = hit.astype(jnp.bfloat16)
    packed = jnp.dot(hit, scale_ref[...], preferred_element_type=jnp.float32) * sign
    listed = lax.dot_general(
        slot_ref[...].astype(jnp.bfloat16), hit, (((1,), (1,)), ((), ())), preferred_element_type=jnp.float32
    )
    packed = packed.astype(jnp.bfloat16)
    for p, pack_ref in enumerate(packs):
        pack_ref[:rows, :] = packed[p * rows : (p + 1) * rows, :]
        meta = jnp.concatenate(
            [listed[:, p * rows : (p + 1) * rows], jnp.zeros((1, dof_count - rows), jnp.float32)], axis=1
        )
        pack_ref[rows:, :] = jnp.broadcast_to(meta, (ROW_TILE, dof_count)).astype(jnp.bfloat16)


def block_weights(packs, rows, blocks_own):
    first = lax.axis_index("face") * blocks_own
    block_ids = first + lax.broadcasted_iota(jnp.int32, (blocks_own, rows), 0)
    total = None
    for pack in packs:
        slots = pack[rows : rows + ROW_TILE, :].astype(jnp.int32)[:1, :rows]
        hit = (slots == block_ids).astype(jnp.bfloat16)
        part = jnp.dot(hit, pack[:rows, :], preferred_element_type=jnp.float32)
        total = part if total is None else total + part
    return total


def own_kernel(
    mortar_ref, rate_ref, cell_ref, basis_ref, pack_any, swapped_ref, pumped_ref, sum_ref, weight_ref, pack_ref, sem, pack_sem
):
    blocks_own, columns, dof_count = pumped_ref.shape
    first_block = lax.axis_index("face") * blocks_own
    pack_fetch = pltpu.make_async_copy(pack_any, pack_ref, pack_sem)
    fetch = pltpu.make_async_copy(mortar_ref.at[pl.ds(first_block, blocks_own)], pumped_ref, sem)
    pack_fetch.start()
    fetch.start()
    pack_fetch.wait()
    weight_ref[...] = block_weights((pack_ref, swapped_ref), pack_ref.shape[0] - ROW_TILE, blocks_own)
    fetch.wait()

    base = lax.axis_index("sub") * mortar_ref.shape[0] + first_block
    for column in range(columns):
        block = lax.div(cell_ref[column], dof_count) - base
        dof = lax.rem(cell_ref[column], dof_count)

        @pl.when((block >= 0) & (block < blocks_own))
        def _():
            slab = slice(column // ROW_TILE * ROW_TILE, (column // ROW_TILE + 1) * ROW_TILE)
            shape = (ROW_TILE, dof_count)
            at_well = (lax.broadcasted_iota(jnp.int32, shape, 0) == column % ROW_TILE) & (
                lax.broadcasted_iota(jnp.int32, shape, 1) == dof
            )
            well = jnp.where(at_well, rate_ref[column], 0.0)
            pumped_ref[block, slab, :] = (pumped_ref[block, slab, :].astype(jnp.float32) + well).astype(
                jnp.bfloat16
            )

    tile_blocks = blocks_own // TILES
    for tile in range(TILES):
        at = slice(tile * tile_blocks, (tile + 1) * tile_blocks)
        scaled = (pumped_ref[at].astype(jnp.float32) * weight_ref[at][:, None, :]).astype(jnp.bfloat16)
        flux = jnp.dot(
            scaled.reshape(tile_blocks * columns, dof_count), basis_ref[0], preferred_element_type=jnp.float32
        )
        sum_ref[at] = flux.reshape(tile_blocks, columns, dof_count)


def stage_kernel(kinds, pumped_ref, sum_ref, *refs):
    bases, refs = refs[: 2 * len(kinds)], refs[2 * len(kinds) :]
    packs, (out_ref, weight_ref, basis_ref, scaled_ref) = refs[:-4], refs[-4:]
    blocks_own, columns, dof_count = pumped_ref.shape
    face_id = lax.axis_index("face")
    rows = packs[0].shape[0] - ROW_TILE
    count = weight_ref.shape[0]
    for spot in range(count):
        weight_ref[spot] = block_weights(packs[2 * spot : 2 * spot + 2], rows, blocks_own)
    spot = 0
    for at, (far, near) in enumerate(kinds):
        spots = []
        for wanted in (far, near):
            spots.append(spot if wanted else count)
            spot += wanted
        for array, core_0, core_1 in ((bases[2 * at], *spots), (bases[2 * at + 1], *spots[::-1])):
            start = pl.multiple_of(jnp.where(face_id == 0, core_0, core_1) * dof_count, dof_count)
            basis_ref[pl.ds(start, dof_count), :] = array[0]

    tile_blocks = blocks_own // TILES
    for tile in range(TILES):
        at = slice(tile * tile_blocks, (tile + 1) * tile_blocks)
        values = pumped_ref[at].astype(jnp.float32)
        for spot in range(count):
            scaled = (values * weight_ref[spot, at][:, None, :]).astype(jnp.bfloat16)
            scaled_ref[tile % 2, :, spot * dof_count : (spot + 1) * dof_count] = scaled.reshape(
                tile_blocks * columns, dof_count
            )
        total = jnp.dot(
            scaled_ref[tile % 2], basis_ref[: count * dof_count, :], preferred_element_type=jnp.float32
        )
        out_ref[at] = total.reshape(tile_blocks, columns, dof_count) + sum_ref[at]


def last_kernel(pumped_ref, sum_ref, projection_ref, *refs):
    arrays, (result_ref, weight_ref, basis_ref, scaled_ref, out_ref, sems) = refs[:-6], refs[-6:]
    blocks_own, columns, dof_count = pumped_ref.shape
    count = weight_ref.shape[0]
    for at in range(count):
        basis, basis_swapped, pack, pack_swapped = arrays[4 * at : 4 * at + 4]
        weight_ref[at] = block_weights((pack, pack_swapped), pack.shape[0] - ROW_TILE, blocks_own)
        for core, array in ((1, basis), (0, basis_swapped)):

            @pl.when(lax.axis_index("face") == core)
            def _():
                basis_ref[at * dof_count : (at + 1) * dof_count, :] = array[0]

    tiles = sems.shape[0]
    tile_blocks = blocks_own // tiles
    copies = []
    for tile in range(tiles):
        at = slice(tile * tile_blocks, (tile + 1) * tile_blocks)
        values = pumped_ref[at].astype(jnp.float32)
        for spot in range(count):
            scaled = (values * weight_ref[spot, at][:, None, :]).astype(jnp.bfloat16)
            scaled_ref[tile % 2, :, spot * dof_count : (spot + 1) * dof_count] = scaled.reshape(
                tile_blocks * columns, dof_count
            )
        total = jnp.dot(scaled_ref[tile % 2], basis_ref[...], preferred_element_type=jnp.float32)
        total = total + sum_ref[at].reshape(tile_blocks * columns, dof_count)
        result = jnp.dot(
            total.astype(jnp.bfloat16), projection_ref[...], preferred_element_type=jnp.float32
        )
        out_ref[at] = result.reshape(tile_blocks, columns, dof_count)
        copies.append(pltpu.make_async_copy(out_ref.at[at], result_ref.at[at], sems.at[tile]))
        copies[-1].start()
    for copy in copies:
        copy.wait()


def on_device(
    mortar_in, pump_rate, well_cell, face_owner, face_slot, face_scale, section, basis, projection
):
    blocks_dev, cols_dev, dof_count = mortar_in.shape
    faces_dev = face_slot.shape[0]
    subdomains, rights, halves = lax.axis_size("sub"), lax.axis_size("rhs"), lax.axis_size("face")
    others = subdomains - 1
    blocks_own = blocks_dev // halves
    capacity = max(2, 2 * faces_dev // subdomains)
    pack_rows = -(-capacity // ROW_TILE) * ROW_TILE + ROW_TILE
    block_shape = (blocks_own, cols_dev, dof_count)
    swap = [(i, i ^ 1) for i in range(halves)]

    def flat(sub, right, face):
        return (sub * rights + right) * halves + face

    partners = sorted(range(1, subdomains), key=lambda p: (p < subdomains // 2, p))
    groups = [partners[i : i + 3] for i in range(0, others, 3)]
    groups = [tuple(g) if len(g) == 3 else (g[0], g[-1], g[0]) for g in groups]
    firsts = []
    for a, b, c in groups:
        pairs = [
            (flat(s, r, face), flat(s ^ (c if face else b if r % 2 else a), r, face))
            for s in range(subdomains)
            for r in range(rights)
            for face in range(halves)
        ]
        firsts.append(lax.ppermute(basis, ("sub", "rhs", "face"), pairs))

    kinds = [(a != b, c != a or a == b) for a, b, c in groups]
    near = [(c, c) for (_, _, c), (_, has) in zip(groups, kinds) if has]
    far = [(a, b) for (a, b, _), (has, _) in zip(groups, kinds) if has]
    ways = [(0, 0), *near, *far, *[(b, a) for a, b in far]]
    packs = pl.pallas_call(
        functools.partial(pack_kernel, ways),
        out_shape=[jax.ShapeDtypeStruct((pack_rows, dof_count), jnp.bfloat16)] * len(ways),
        in_specs=[VMEM, VMEM, VMEM, SMEM],
        out_specs=[VMEM] * len(ways),
        cost_estimate=WORK,
        name="pack_weights",
    )(face_owner.reshape(1, faces_dev), face_slot.reshape(1, faces_dev), face_scale, section)

    def along_sub(way, pack):
        pairs = [
            (s * rights + r, (s ^ way[r % 2]) * rights + r) for s in range(subdomains) for r in range(rights)
        ]
        return lax.ppermute(pack, ("sub", "rhs"), pairs)

    arrived = [along_sub(way, pack) for way, pack in zip(ways[1:], packs[1:])]
    own_swapped = lax.ppermute(packs[0], "face", swap)

    firsts, own_swapped = lax.optimization_barrier((firsts, own_swapped))
    pumped, own_sum = pl.pallas_call(
        own_kernel,
        out_shape=[
            jax.ShapeDtypeStruct(block_shape, jnp.bfloat16),
            jax.ShapeDtypeStruct(block_shape, jnp.float32),
        ],
        in_specs=[HBM, SMEM, SMEM, VMEM, HBM, VMEM],
        out_specs=[VMEM, VMEM],
        scratch_shapes=[
            pltpu.VMEM((blocks_own, dof_count), jnp.float32),
            pltpu.VMEM((pack_rows, dof_count), jnp.bfloat16),
            pltpu.SemaphoreType.DMA(()),
            pltpu.SemaphoreType.DMA(()),
        ],
        compiler_params=pltpu.CompilerParams(vmem_limit_bytes=32 * MIB),
        cost_estimate=WORK,
        name="own_blocks",
    )(mortar_in, pump_rate, well_cell, basis, packs[0], own_swapped)

    pairs = [
        (r * halves + face, r * halves if face else (r ^ 1) * halves + 1)
        for r in range(rights)
        for face in range(halves)
    ]
    early, late = [], []
    for (has_far, _), first in zip(kinds, firsts):
        early += [first, lax.ppermute(first, "face", swap)]
        if has_far:
            second = lax.ppermute(first, ("rhs", "face"), pairs)
            late.append([second, lax.ppermute(second, "face", swap)])
    arrived, own_sum, early = lax.optimization_barrier((arrived, own_sum, early))
    swapped = [lax.ppermute(array, "face", swap) for array in arrived]
    places = dict(zip(ways[1:], zip(arrived, swapped)))
    weights = []
    for (a, b, c), (has_far, has_near) in zip(groups, kinds):
        weights += list(places[a, b]) * has_far + list(places[c, c]) * has_near
    for arrays, (a, b) in zip(late, far):
        arrays += places[b, a]

    late_count = len(late)
    count = others - late_count
    operands = [pumped, own_sum, *early, *weights]
    total = pl.pallas_call(
        functools.partial(stage_kernel, kinds),
        out_shape=jax.ShapeDtypeStruct(block_shape, jnp.float32),
        in_specs=[VMEM] * len(operands),
        out_specs=VMEM,
        scratch_shapes=[
            pltpu.VMEM((count, blocks_own, dof_count), jnp.float32),
            pltpu.VMEM(((count + 1) * dof_count, dof_count), jnp.bfloat16),
            pltpu.VMEM((2, blocks_own // TILES * cols_dev, count * dof_count), jnp.bfloat16),
        ],
        input_output_aliases={1: 0},
        compiler_params=pltpu.CompilerParams(vmem_limit_bytes=40 * MIB),
        cost_estimate=WORK,
        name="stage",
    )(*operands)

    operands = [pumped, total, projection, *sum(late, [])]
    return pl.pallas_call(
        last_kernel,
        out_shape=jax.ShapeDtypeStruct(block_shape, jnp.float32),
        in_specs=[VMEM] * len(operands),
        out_specs=HBM,
        scratch_shapes=[
            pltpu.VMEM((late_count, blocks_own, dof_count), jnp.float32),
            pltpu.VMEM((late_count * dof_count, dof_count), jnp.bfloat16),
            pltpu.VMEM((2, blocks_own // LAST_TILES * cols_dev, late_count * dof_count), jnp.bfloat16),
            pltpu.VMEM(block_shape, jnp.float32),
            pltpu.SemaphoreType.DMA((LAST_TILES,)),
        ],
        compiler_params=pltpu.CompilerParams(vmem_limit_bytes=40 * MIB),
        name="last_stage",
    )(*operands)


def solution(mesh):
    in_specs = (
        P(("groups", "sub"), "rhs", None),
        P(("groups", "rhs")),
        P(("groups", "rhs")),
        P(("groups", "sub", "face"), None),
        P(("groups", "sub", "face")),
        P(("groups", "sub", "face"), None),
        P(("groups", "sub")),
        P(("groups", "sub"), None, None),
        P(),
    )
    out_specs = P(("groups", "sub", "face"), "rhs", None)
    return jax.shard_map(
        on_device, mesh=mesh, in_specs=in_specs, out_specs=out_specs, check_vma=False
    )
```

```python
import functools

import jax
import jax.numpy as jnp
from jax import lax
from jax.experimental import pallas as pl
from jax.experimental.pallas import tpu as pltpu
from jax.sharding import PartitionSpec as P

ROW_TILE = 16
VMEM = pl.BlockSpec(memory_space=pltpu.VMEM)
HBM = pl.BlockSpec(memory_space=pltpu.HBM)
SMEM = pl.BlockSpec(memory_space=pltpu.SMEM)
MIB = 1024 * 1024
TILES = 4
LAST_TILES = 8
LIGHT = pl.CostEstimate(flops=1_000_000, bytes_accessed=1024, transcendentals=0)
WORK = pl.CostEstimate(flops=4_000_000_000, bytes_accessed=8 * MIB, transcendentals=0)


def on_even(even, odd):
    return jnp.where(lax.rem(lax.axis_index("rhs"), 2) == 0, even, odd)


def pack_kernel(partners, owner_ref, slot_ref, scale_ref, section_ref, *packs):
    rows, dof_count = packs[0].shape
    rows -= ROW_TILE
    faces = owner_ref.shape[1]
    sign = (1 - 2 * section_ref[0]).astype(jnp.float32)
    here = lax.axis_index("sub")
    owners = jnp.concatenate(
        [jnp.full((1, faces), here ^ on_even(even, odd), jnp.int32) for even, odd in partners], axis=0
    )
    named = owners == owner_ref[...]
    earlier = lax.broadcasted_iota(jnp.int32, (faces, faces), 0) < lax.broadcasted_iota(
        jnp.int32, (faces, faces), 1
    )
    rank = jnp.dot(
        named.astype(jnp.bfloat16), earlier.astype(jnp.bfloat16), preferred_element_type=jnp.float32
    )
    place = jnp.where(named, rank, -1.0)
    at = lax.broadcasted_iota(jnp.int32, (rows, faces), 0).astype(jnp.float32)
    hit = jnp.concatenate([place[p : p + 1, :] == at for p in range(len(packs))], axis=0)
    hit = hit.astype(jnp.bfloat16)
    packed = jnp.dot(hit, scale_ref[...], preferred_element_type=jnp.float32) * sign
    listed = lax.dot_general(
        slot_ref[...].astype(jnp.bfloat16), hit, (((1,), (1,)), ((), ())), preferred_element_type=jnp.float32
    )
    packed = packed.astype(jnp.bfloat16)
    for p, pack_ref in enumerate(packs):
        pack_ref[:rows, :] = packed[p * rows : (p + 1) * rows, :]
        meta = jnp.concatenate(
            [listed[:, p * rows : (p + 1) * rows], jnp.zeros((1, dof_count - rows), jnp.float32)], axis=1
        )
        pack_ref[rows:, :] = jnp.broadcast_to(meta, (ROW_TILE, dof_count)).astype(jnp.bfloat16)


def block_weights(packs, rows, blocks_own):
    first = lax.axis_index("face") * blocks_own
    block_ids = first + lax.broadcasted_iota(jnp.int32, (blocks_own, rows), 0)
    total = None
    for pack in packs:
        slots = pack[rows : rows + ROW_TILE, :].astype(jnp.int32)[:1, :rows]
        hit = (slots == block_ids).astype(jnp.bfloat16)
        part = jnp.dot(hit, pack[:rows, :], preferred_element_type=jnp.float32)
        total = part if total is None else total + part
    return total


def own_kernel(
    mortar_ref,
    rate_ref,
    cell_ref,
    owner_ref,
    slot_ref,
    scale_ref,
    section_ref,
    basis_ref,
    swapped_ref,
    pumped_ref,
    sum_ref,
    weight_ref,
):
    blocks_own, columns, dof_count = pumped_ref.shape
    faces = owner_ref.shape[1]
    here = lax.axis_index("sub")
    first_block = lax.axis_index("face") * blocks_own
    sign = (1 - 2 * section_ref[0]).astype(jnp.float32)
    block_ids = first_block + lax.broadcasted_iota(jnp.int32, (blocks_own, faces), 0)
    hit = (slot_ref[...] == block_ids) & (owner_ref[...] == here)
    weight = jnp.dot(hit.astype(jnp.bfloat16), scale_ref[...], preferred_element_type=jnp.float32) * sign
    weight_ref[...] = weight + block_weights((swapped_ref,), swapped_ref.shape[0] - ROW_TILE, blocks_own)
    pumped_ref[...] = mortar_ref[pl.ds(first_block, blocks_own)]

    base = here * mortar_ref.shape[0] + first_block
    for column in range(columns):
        block = lax.div(cell_ref[column], dof_count) - base
        dof = lax.rem(cell_ref[column], dof_count)

        @pl.when((block >= 0) & (block < blocks_own))
        def _():
            slab = slice(column // ROW_TILE * ROW_TILE, (column // ROW_TILE + 1) * ROW_TILE)
            shape = (ROW_TILE, dof_count)
            at_well = (lax.broadcasted_iota(jnp.int32, shape, 0) == column % ROW_TILE) & (
                lax.broadcasted_iota(jnp.int32, shape, 1) == dof
            )
            well = jnp.where(at_well, rate_ref[column], 0.0)
            pumped_ref[block, slab, :] = (pumped_ref[block, slab, :].astype(jnp.float32) + well).astype(
                jnp.bfloat16
            )

    tile_blocks = blocks_own // TILES
    for tile in range(TILES):
        at = slice(tile * tile_blocks, (tile + 1) * tile_blocks)
        scaled = (pumped_ref[at].astype(jnp.float32) * weight_ref[at][:, None, :]).astype(jnp.bfloat16)
        flux = jnp.dot(
            scaled.reshape(tile_blocks * columns, dof_count), basis_ref[0], preferred_element_type=jnp.float32
        )
        sum_ref[at] = flux.reshape(tile_blocks, columns, dof_count)


def stage_kernel(kinds, pumped_ref, sum_ref, *refs):
    bases, refs = refs[: 2 * len(kinds)], refs[2 * len(kinds) :]
    packs, (out_ref, weight_ref, basis_ref, scaled_ref) = refs[:-4], refs[-4:]
    blocks_own, columns, dof_count = pumped_ref.shape
    face_id = lax.axis_index("face")
    rows = packs[0].shape[0] - ROW_TILE
    count = weight_ref.shape[0]
    for spot in range(count):
        weight_ref[spot] = block_weights(packs[2 * spot : 2 * spot + 2], rows, blocks_own)
    spot = 0
    for at, (far, near) in enumerate(kinds):
        spots = []
        for wanted in (far, near):
            spots.append(spot if wanted else count)
            spot += wanted
        for array, core_0, core_1 in ((bases[2 * at], *spots), (bases[2 * at + 1], *spots[::-1])):
            start = pl.multiple_of(jnp.where(face_id == 0, core_0, core_1) * dof_count, dof_count)
            basis_ref[pl.ds(start, dof_count), :] = array[0]

    tile_blocks = blocks_own // TILES
    for tile in range(TILES):
        at = slice(tile * tile_blocks, (tile + 1) * tile_blocks)
        values = pumped_ref[at].astype(jnp.float32)
        for spot in range(count):
            scaled = (values * weight_ref[spot, at][:, None, :]).astype(jnp.bfloat16)
            scaled_ref[tile % 2, :, spot * dof_count : (spot + 1) * dof_count] = scaled.reshape(
                tile_blocks * columns, dof_count
            )
        total = jnp.dot(
            scaled_ref[tile % 2], basis_ref[: count * dof_count, :], preferred_element_type=jnp.float32
        )
        out_ref[at] = total.reshape(tile_blocks, columns, dof_count) + sum_ref[at]


def last_kernel(pumped_ref, sum_ref, projection_ref, *refs):
    arrays, (result_ref, weight_ref, basis_ref, scaled_ref, out_ref, sems) = refs[:-6], refs[-6:]
    blocks_own, columns, dof_count = pumped_ref.shape
    count = weight_ref.shape[0]
    for at in range(count):
        basis, basis_swapped, pack, pack_swapped = arrays[4 * at : 4 * at + 4]
        weight_ref[at] = block_weights((pack, pack_swapped), pack.shape[0] - ROW_TILE, blocks_own)
        for core, array in ((1, basis), (0, basis_swapped)):

            @pl.when(lax.axis_index("face") == core)
            def _():
                basis_ref[at * dof_count : (at + 1) * dof_count, :] = array[0]

    tiles = sems.shape[0]
    tile_blocks = blocks_own // tiles
    copies = []
    for tile in range(tiles):
        at = slice(tile * tile_blocks, (tile + 1) * tile_blocks)
        values = pumped_ref[at].astype(jnp.float32)
        for spot in range(count):
            scaled = (values * weight_ref[spot, at][:, None, :]).astype(jnp.bfloat16)
            scaled_ref[tile % 2, :, spot * dof_count : (spot + 1) * dof_count] = scaled.reshape(
                tile_blocks * columns, dof_count
            )
        total = jnp.dot(scaled_ref[tile % 2], basis_ref[...], preferred_element_type=jnp.float32)
        total = total + sum_ref[at].reshape(tile_blocks * columns, dof_count)
        result = jnp.dot(
            total.astype(jnp.bfloat16), projection_ref[...], preferred_element_type=jnp.float32
        )
        out_ref[at] = result.reshape(tile_blocks, columns, dof_count)
        copies.append(pltpu.make_async_copy(out_ref.at[at], result_ref.at[at], sems.at[tile]))
        copies[-1].start()
    for copy in copies:
        copy.wait()


def on_device(
    mortar_in, pump_rate, well_cell, face_owner, face_slot, face_scale, section, basis, projection
):
    blocks_dev, cols_dev, dof_count = mortar_in.shape
    faces_dev = face_slot.shape[0]
    subdomains, rights, halves = lax.axis_size("sub"), lax.axis_size("rhs"), lax.axis_size("face")
    others = subdomains - 1
    blocks_own = blocks_dev // halves
    capacity = max(2, 2 * faces_dev // subdomains)
    pack_rows = -(-capacity // ROW_TILE) * ROW_TILE + ROW_TILE
    block_shape = (blocks_own, cols_dev, dof_count)
    swap = [(i, i ^ 1) for i in range(halves)]

    def flat(sub, right, face):
        return (sub * rights + right) * halves + face

    partners = sorted(range(1, subdomains), key=lambda p: (p < subdomains // 2, p))
    groups = [partners[i : i + 3] for i in range(0, others, 3)]
    groups = [tuple(g) if len(g) == 3 else (g[0], g[-1], g[0]) for g in groups]
    firsts = []
    for a, b, c in groups:
        pairs = [
            (flat(s, r, face), flat(s ^ (c if face else b if r % 2 else a), r, face))
            for s in range(subdomains)
            for r in range(rights)
            for face in range(halves)
        ]
        firsts.append(lax.ppermute(basis, ("sub", "rhs", "face"), pairs))

    kinds = [(a != b, c != a or a == b) for a, b, c in groups]
    near = [(c, c) for (_, _, c), (_, has) in zip(groups, kinds) if has]
    far = [(a, b) for (a, b, _), (has, _) in zip(groups, kinds) if has]
    ways = [(0, 0), *near, *far, *[(b, a) for a, b in far]]
    faces = [face_owner.reshape(1, faces_dev), face_slot.reshape(1, faces_dev), face_scale]
    packs = pl.pallas_call(
        functools.partial(pack_kernel, ways),
        out_shape=[jax.ShapeDtypeStruct((pack_rows, dof_count), jnp.bfloat16)] * len(ways),
        in_specs=[VMEM, VMEM, VMEM, SMEM],
        out_specs=[VMEM] * len(ways),
        cost_estimate=WORK,
        name="pack_weights",
    )(*faces, section)

    def along_sub(way, pack):
        pairs = [
            (s * rights + r, (s ^ way[r % 2]) * rights + r) for s in range(subdomains) for r in range(rights)
        ]
        return lax.ppermute(pack, ("sub", "rhs"), pairs)

    arrived = [along_sub(way, pack) for way, pack in zip(ways[1:], packs[1:])]
    own_swapped = lax.ppermute(packs[0], "face", swap)

    firsts, own_swapped = lax.optimization_barrier((firsts, own_swapped))
    pumped, own_sum = pl.pallas_call(
        own_kernel,
        out_shape=[
            jax.ShapeDtypeStruct(block_shape, jnp.bfloat16),
            jax.ShapeDtypeStruct(block_shape, jnp.float32),
        ],
        in_specs=[VMEM, SMEM, SMEM, VMEM, VMEM, VMEM, SMEM, VMEM, VMEM],
        out_specs=[VMEM, VMEM],
        scratch_shapes=[pltpu.VMEM((blocks_own, dof_count), jnp.float32)],
        compiler_params=pltpu.CompilerParams(vmem_limit_bytes=32 * MIB),
        cost_estimate=WORK,
        name="own_blocks",
    )(mortar_in, pump_rate, well_cell, *faces, section, basis, own_swapped)

    pairs = [
        (r * halves + face, r * halves if face else (r ^ 1) * halves + 1)
        for r in range(rights)
        for face in range(halves)
    ]
    early, late = [], []
    for (has_far, _), first in zip(kinds, firsts):
        early += [first, lax.ppermute(first, "face", swap)]
        if has_far:
            second = lax.ppermute(first, ("rhs", "face"), pairs)
            late.append([second, lax.ppermute(second, "face", swap)])
    soon = len(near) + len(far)
    arrived[:soon], own_sum, early = lax.optimization_barrier((arrived[:soon], own_sum, early))
    swapped = [lax.ppermute(array, "face", swap) for array in arrived]
    places = dict(zip(ways[1:], zip(arrived, swapped)))
    weights = []
    for (a, b, c), (has_far, has_near) in zip(groups, kinds):
        weights += list(places[a, b]) * has_far + list(places[c, c]) * has_near
    for arrays, (a, b) in zip(late, far):
        arrays += places[b, a]

    late_count = len(late)
    count = others - late_count
    operands = [pumped, own_sum, *early, *weights]
    total = pl.pallas_call(
        functools.partial(stage_kernel, kinds),
        out_shape=jax.ShapeDtypeStruct(block_shape, jnp.float32),
        in_specs=[VMEM] * len(operands),
        out_specs=VMEM,
        scratch_shapes=[
            pltpu.VMEM((count, blocks_own, dof_count), jnp.float32),
            pltpu.VMEM(((count + 1) * dof_count, dof_count), jnp.bfloat16),
            pltpu.VMEM((2, blocks_own // TILES * cols_dev, count * dof_count), jnp.bfloat16),
        ],
        input_output_aliases={1: 0},
        compiler_params=pltpu.CompilerParams(vmem_limit_bytes=40 * MIB),
        cost_estimate=WORK,
        name="stage",
    )(*operands)

    operands = [pumped, total, projection, *sum(late, [])]
    return pl.pallas_call(
        last_kernel,
        out_shape=jax.ShapeDtypeStruct(block_shape, jnp.float32),
        in_specs=[VMEM] * len(operands),
        out_specs=HBM,
        scratch_shapes=[
            pltpu.VMEM((late_count, blocks_own, dof_count), jnp.float32),
            pltpu.VMEM((late_count * dof_count, dof_count), jnp.bfloat16),
            pltpu.VMEM((2, blocks_own // LAST_TILES * cols_dev, late_count * dof_count), jnp.bfloat16),
            pltpu.VMEM(block_shape, jnp.float32),
            pltpu.SemaphoreType.DMA((LAST_TILES,)),
        ],
        compiler_params=pltpu.CompilerParams(vmem_limit_bytes=40 * MIB),
        name="last_stage",
    )(*operands)


def solution(mesh):
    in_specs = (
        P(("groups", "sub"), "rhs", None),
        P(("groups", "rhs")),
        P(("groups", "rhs")),
        P(("groups", "sub", "face"), None),
        P(("groups", "sub", "face")),
        P(("groups", "sub", "face"), None),
        P(("groups", "sub")),
        P(("groups", "sub"), None, None),
        P(),
    )
    out_specs = P(("groups", "sub", "face"), "rhs", None)
    return jax.shard_map(
        on_device, mesh=mesh, in_specs=in_specs, out_specs=out_specs, check_vma=False
    )
```

```python
import functools

import jax
import jax.numpy as jnp
from jax import lax
from jax.experimental import pallas as pl
from jax.experimental.pallas import tpu as pltpu
from jax.sharding import PartitionSpec as P

ROW_TILE = 16
SLOT_ROWS = 8
VMEM = pl.BlockSpec(memory_space=pltpu.VMEM)
HBM = pl.BlockSpec(memory_space=pltpu.HBM)
SMEM = pl.BlockSpec(memory_space=pltpu.SMEM)
MIB = 1024 * 1024
TILES = 4
LAST_TILES = 8
LIGHT = pl.CostEstimate(flops=1_000_000, bytes_accessed=1024, transcendentals=0)
WORK = pl.CostEstimate(flops=4_000_000_000, bytes_accessed=8 * MIB, transcendentals=0)


def on_even(even, odd):
    return jnp.where(lax.rem(lax.axis_index("rhs"), 2) == 0, even, odd)


def pack_kernel(partners, owner_ref, slot_ref, scale_ref, section_ref, *packs):
    rows, dof_count = packs[0].shape
    rows -= SLOT_ROWS
    faces = owner_ref.shape[1]
    sign = (1 - 2 * section_ref[0]).astype(jnp.float32)
    here = lax.axis_index("sub")
    owners = jnp.concatenate(
        [jnp.full((1, faces), here ^ on_even(even, odd), jnp.int32) for even, odd in partners], axis=0
    )
    named = owners == owner_ref[...]
    earlier = lax.broadcasted_iota(jnp.int32, (faces, faces), 0) < lax.broadcasted_iota(
        jnp.int32, (faces, faces), 1
    )
    rank = jnp.dot(
        named.astype(jnp.bfloat16), earlier.astype(jnp.bfloat16), preferred_element_type=jnp.float32
    )
    place = jnp.where(named, rank, -1.0)
    at = lax.broadcasted_iota(jnp.int32, (rows, faces), 0).astype(jnp.float32)
    hit = jnp.concatenate([place[p : p + 1, :] == at for p in range(len(packs))], axis=0)
    hit = hit.astype(jnp.bfloat16)
    packed = jnp.dot(hit, scale_ref[...], preferred_element_type=jnp.float32) * sign
    listed = lax.dot_general(
        slot_ref[...].astype(jnp.bfloat16), hit, (((1,), (1,)), ((), ())), preferred_element_type=jnp.float32
    )
    packed = packed.astype(jnp.bfloat16)
    for p, pack_ref in enumerate(packs):
        pack_ref[:rows, :] = packed[p * rows : (p + 1) * rows, :]
        meta = jnp.concatenate(
            [listed[:, p * rows : (p + 1) * rows], jnp.zeros((1, dof_count - rows), jnp.float32)], axis=1
        )
        pack_ref[rows:, :] = jnp.broadcast_to(meta, (SLOT_ROWS, dof_count)).astype(jnp.bfloat16)


def block_weights(packs, rows, blocks_own):
    first = lax.axis_index("face") * blocks_own
    block_ids = first + lax.broadcasted_iota(jnp.int32, (blocks_own, rows), 0)
    total = None
    for pack in packs:
        slots = pack[rows : rows + SLOT_ROWS, :].astype(jnp.int32)[:1, :rows]
        hit = (slots == block_ids).astype(jnp.bfloat16)
        part = jnp.dot(hit, pack[:rows, :], preferred_element_type=jnp.float32)
        total = part if total is None else total + part
    return total


def own_kernel(
    mortar_ref,
    rate_ref,
    cell_ref,
    owner_ref,
    slot_ref,
    scale_ref,
    section_ref,
    basis_ref,
    swapped_ref,
    pumped_ref,
    sum_ref,
    weight_ref,
):
    blocks_own, columns, dof_count = pumped_ref.shape
    faces = owner_ref.shape[1]
    here = lax.axis_index("sub")
    first_block = lax.axis_index("face") * blocks_own
    sign = (1 - 2 * section_ref[0]).astype(jnp.float32)
    block_ids = first_block + lax.broadcasted_iota(jnp.int32, (blocks_own, faces), 0)
    hit = (slot_ref[...] == block_ids) & (owner_ref[...] == here)
    weight = jnp.dot(hit.astype(jnp.bfloat16), scale_ref[...], preferred_element_type=jnp.float32) * sign
    weight_ref[...] = weight + block_weights((swapped_ref,), swapped_ref.shape[0] - SLOT_ROWS, blocks_own)
    pumped_ref[...] = mortar_ref[pl.ds(first_block, blocks_own)]

    base = here * mortar_ref.shape[0] + first_block
    bits = dof_count.bit_length() - 1
    for column in range(columns):
        block = (cell_ref[column] >> bits) - base
        dof = cell_ref[column] & (dof_count - 1)

        @pl.when((block >= 0) & (block < blocks_own))
        def _():
            slab = slice(column // ROW_TILE * ROW_TILE, (column // ROW_TILE + 1) * ROW_TILE)
            shape = (ROW_TILE, dof_count)
            at_well = (lax.broadcasted_iota(jnp.int32, shape, 0) == column % ROW_TILE) & (
                lax.broadcasted_iota(jnp.int32, shape, 1) == dof
            )
            well = jnp.where(at_well, rate_ref[column], 0.0)
            pumped_ref[block, slab, :] = (pumped_ref[block, slab, :].astype(jnp.float32) + well).astype(
                jnp.bfloat16
            )

    tile_blocks = blocks_own // TILES
    for tile in range(TILES):
        at = slice(tile * tile_blocks, (tile + 1) * tile_blocks)
        scaled = (pumped_ref[at].astype(jnp.float32) * weight_ref[at][:, None, :]).astype(jnp.bfloat16)
        flux = jnp.dot(
            scaled.reshape(tile_blocks * columns, dof_count), basis_ref[0], preferred_element_type=jnp.float32
        )
        sum_ref[at] = flux.reshape(tile_blocks, columns, dof_count)


def stage_kernel(kinds, pumped_ref, sum_ref, *refs):
    bases, refs = refs[: 2 * len(kinds)], refs[2 * len(kinds) :]
    packs, (out_ref, weight_ref, basis_ref, scaled_ref) = refs[:-4], refs[-4:]
    blocks_own, columns, dof_count = pumped_ref.shape
    face_id = lax.axis_index("face")
    rows = packs[0].shape[0] - SLOT_ROWS
    count = weight_ref.shape[0]
    for spot in range(count):
        weight_ref[spot] = block_weights(packs[2 * spot : 2 * spot + 2], rows, blocks_own)
    spot = 0
    for at, (far, near) in enumerate(kinds):
        spots = []
        for wanted in (far, near):
            spots.append(spot if wanted else count)
            spot += wanted
        for array, core_0, core_1 in ((bases[2 * at], *spots), (bases[2 * at + 1], *spots[::-1])):
            start = pl.multiple_of(jnp.where(face_id == 0, core_0, core_1) * dof_count, dof_count)
            basis_ref[pl.ds(start, dof_count), :] = array[0]

    tile_blocks = blocks_own // TILES
    for tile in range(TILES):
        at = slice(tile * tile_blocks, (tile + 1) * tile_blocks)
        values = pumped_ref[at].astype(jnp.float32)
        for spot in range(count):
            scaled = (values * weight_ref[spot, at][:, None, :]).astype(jnp.bfloat16)
            scaled_ref[tile % 2, :, spot * dof_count : (spot + 1) * dof_count] = scaled.reshape(
                tile_blocks * columns, dof_count
            )
        total = jnp.dot(
            scaled_ref[tile % 2], basis_ref[: count * dof_count, :], preferred_element_type=jnp.float32
        )
        out_ref[at] = total.reshape(tile_blocks, columns, dof_count) + sum_ref[at]


def last_kernel(pumped_ref, sum_ref, projection_ref, *refs):
    arrays, (result_ref, weight_ref, basis_ref, scaled_ref, out_ref, sems) = refs[:-6], refs[-6:]
    blocks_own, columns, dof_count = pumped_ref.shape
    count = weight_ref.shape[0]
    for at in range(count):
        basis, basis_swapped, pack, pack_swapped = arrays[4 * at : 4 * at + 4]
        weight_ref[at] = block_weights((pack, pack_swapped), pack.shape[0] - SLOT_ROWS, blocks_own)
        for core, array in ((1, basis), (0, basis_swapped)):

            @pl.when(lax.axis_index("face") == core)
            def _():
                basis_ref[at * dof_count : (at + 1) * dof_count, :] = array[0]

    tiles = sems.shape[0]
    tile_blocks = blocks_own // tiles
    copies = []
    for tile in range(tiles):
        at = slice(tile * tile_blocks, (tile + 1) * tile_blocks)
        values = pumped_ref[at].astype(jnp.float32)
        for spot in range(count):
            scaled = (values * weight_ref[spot, at][:, None, :]).astype(jnp.bfloat16)
            scaled_ref[tile % 2, :, spot * dof_count : (spot + 1) * dof_count] = scaled.reshape(
                tile_blocks * columns, dof_count
            )
        total = jnp.dot(scaled_ref[tile % 2], basis_ref[...], preferred_element_type=jnp.float32)
        total = total + sum_ref[at].reshape(tile_blocks * columns, dof_count)
        result = jnp.dot(
            total.astype(jnp.bfloat16), projection_ref[...], preferred_element_type=jnp.float32
        )
        out_ref[at] = result.reshape(tile_blocks, columns, dof_count)
        copies.append(pltpu.make_async_copy(out_ref.at[at], result_ref.at[at], sems.at[tile]))
        copies[-1].start()
    for copy in copies:
        copy.wait()


def on_device(
    mortar_in, pump_rate, well_cell, face_owner, face_slot, face_scale, section, basis, projection
):
    blocks_dev, cols_dev, dof_count = mortar_in.shape
    faces_dev = face_slot.shape[0]
    subdomains, rights, halves = lax.axis_size("sub"), lax.axis_size("rhs"), lax.axis_size("face")
    others = subdomains - 1
    blocks_own = blocks_dev // halves
    capacity = max(2, 2 * faces_dev // subdomains)
    pack_rows = -(-capacity // ROW_TILE) * ROW_TILE + SLOT_ROWS
    block_shape = (blocks_own, cols_dev, dof_count)
    swap = [(i, i ^ 1) for i in range(halves)]

    def flat(sub, right, face):
        return (sub * rights + right) * halves + face

    partners = sorted(range(1, subdomains), key=lambda p: (p < subdomains // 2, p))
    groups = [partners[i : i + 3] for i in range(0, others, 3)]
    groups = [tuple(g) if len(g) == 3 else (g[0], g[-1], g[0]) for g in groups]
    firsts = []
    for a, b, c in groups:
        pairs = [
            (flat(s, r, face), flat(s ^ (c if face else b if r % 2 else a), r, face))
            for s in range(subdomains)
            for r in range(rights)
            for face in range(halves)
        ]
        firsts.append(lax.ppermute(basis, ("sub", "rhs", "face"), pairs))

    kinds = [(a != b, c != a or a == b) for a, b, c in groups]
    near = [(c, c) for (_, _, c), (_, has) in zip(groups, kinds) if has]
    far = [(a, b) for (a, b, _), (has, _) in zip(groups, kinds) if has]
    ways = [(0, 0), *near, *far, *[(b, a) for a, b in far]]
    faces = [face_owner.reshape(1, faces_dev), face_slot.reshape(1, faces_dev), face_scale]
    packs = pl.pallas_call(
        functools.partial(pack_kernel, ways),
        out_shape=[jax.ShapeDtypeStruct((pack_rows, dof_count), jnp.bfloat16)] * len(ways),
        in_specs=[VMEM, VMEM, VMEM, SMEM],
        out_specs=[VMEM] * len(ways),
        cost_estimate=WORK,
        name="pack_weights",
    )(*faces, section)

    def along_sub(way, pack):
        pairs = [
            (s * rights + r, (s ^ way[r % 2]) * rights + r) for s in range(subdomains) for r in range(rights)
        ]
        return lax.ppermute(pack, ("sub", "rhs"), pairs)

    soon = len(near) + len(far)
    arrived = [along_sub(way, pack) for way, pack in zip(ways[1 : 1 + soon], packs[1:])]
    own_swapped = lax.ppermute(packs[0], "face", swap)

    firsts, own_swapped = lax.optimization_barrier((firsts, own_swapped))
    pumped, own_sum = pl.pallas_call(
        own_kernel,
        out_shape=[
            jax.ShapeDtypeStruct(block_shape, jnp.bfloat16),
            jax.ShapeDtypeStruct(block_shape, jnp.float32),
        ],
        in_specs=[VMEM, SMEM, SMEM, VMEM, VMEM, VMEM, SMEM, VMEM, VMEM],
        out_specs=[VMEM, VMEM],
        scratch_shapes=[pltpu.VMEM((blocks_own, dof_count), jnp.float32)],
        compiler_params=pltpu.CompilerParams(vmem_limit_bytes=32 * MIB),
        cost_estimate=WORK,
        name="own_blocks",
    )(mortar_in, pump_rate, well_cell, *faces, section, basis, own_swapped)

    pairs = [
        (r * halves + face, r * halves if face else (r ^ 1) * halves + 1)
        for r in range(rights)
        for face in range(halves)
    ]
    early, late = [], []
    for (has_far, _), first in zip(kinds, firsts):
        early += [first, lax.ppermute(first, "face", swap)]
        if has_far:
            second = lax.ppermute(first, ("rhs", "face"), pairs)
            late.append([second, lax.ppermute(second, "face", swap)])
    late_packs, own_sum = lax.optimization_barrier((packs[1 + soon :], own_sum))
    late_arrived = [along_sub(way, pack) for way, pack in zip(ways[1 + soon :], late_packs)]
    arrived, own_sum, early = lax.optimization_barrier((arrived, own_sum, early))
    arrived += late_arrived
    swapped = [lax.ppermute(array, "face", swap) for array in arrived]
    places = dict(zip(ways[1:], zip(arrived, swapped)))
    weights = []
    for (a, b, c), (has_far, has_near) in zip(groups, kinds):
        weights += list(places[a, b]) * has_far + list(places[c, c]) * has_near
    for arrays, (a, b) in zip(late, far):
        arrays += places[b, a]

    late_count = len(late)
    count = others - late_count
    operands = [pumped, own_sum, *early, *weights]
    total = pl.pallas_call(
        functools.partial(stage_kernel, kinds),
        out_shape=jax.ShapeDtypeStruct(block_shape, jnp.float32),
        in_specs=[VMEM] * len(operands),
        out_specs=VMEM,
        scratch_shapes=[
            pltpu.VMEM((count, blocks_own, dof_count), jnp.float32),
            pltpu.VMEM(((count + 1) * dof_count, dof_count), jnp.bfloat16),
            pltpu.VMEM((2, blocks_own // TILES * cols_dev, count * dof_count), jnp.bfloat16),
        ],
        input_output_aliases={1: 0},
        compiler_params=pltpu.CompilerParams(vmem_limit_bytes=40 * MIB),
        cost_estimate=WORK,
        name="stage",
    )(*operands)

    operands = [pumped, total, projection, *sum(late, [])]
    return pl.pallas_call(
        last_kernel,
        out_shape=jax.ShapeDtypeStruct(block_shape, jnp.float32),
        in_specs=[VMEM] * len(operands),
        out_specs=HBM,
        scratch_shapes=[
            pltpu.VMEM((late_count, blocks_own, dof_count), jnp.float32),
            pltpu.VMEM((late_count * dof_count, dof_count), jnp.bfloat16),
            pltpu.VMEM((2, blocks_own // LAST_TILES * cols_dev, late_count * dof_count), jnp.bfloat16),
            pltpu.VMEM(block_shape, jnp.float32),
            pltpu.SemaphoreType.DMA((LAST_TILES,)),
        ],
        compiler_params=pltpu.CompilerParams(vmem_limit_bytes=40 * MIB),
        name="last_stage",
    )(*operands)


def solution(mesh):
    in_specs = (
        P(("groups", "sub"), "rhs", None),
        P(("groups", "rhs")),
        P(("groups", "rhs")),
        P(("groups", "sub", "face"), None),
        P(("groups", "sub", "face")),
        P(("groups", "sub", "face"), None),
        P(("groups", "sub")),
        P(("groups", "sub"), None, None),
        P(),
    )
    out_specs = P(("groups", "sub", "face"), "rhs", None)
    return jax.shard_map(
        on_device, mesh=mesh, in_specs=in_specs, out_specs=out_specs, check_vma=False
    )
```

```python
import functools

import jax
import jax.numpy as jnp
from jax import lax
from jax.experimental import pallas as pl
from jax.experimental.pallas import tpu as pltpu
from jax.sharding import PartitionSpec as P

ROW_TILE = 16
SLOT_ROWS = 8
VMEM = pl.BlockSpec(memory_space=pltpu.VMEM)
HBM = pl.BlockSpec(memory_space=pltpu.HBM)
SMEM = pl.BlockSpec(memory_space=pltpu.SMEM)
MIB = 1024 * 1024
TILES = 4
LAST_TILES = 8
LIGHT = pl.CostEstimate(flops=1_000_000, bytes_accessed=1024, transcendentals=0)
WORK = pl.CostEstimate(flops=4_000_000_000, bytes_accessed=8 * MIB, transcendentals=0)


def on_even(even, odd):
    return jnp.where(lax.rem(lax.axis_index("rhs"), 2) == 0, even, odd)


def pack_kernel(partners, owner_ref, slot_ref, scale_ref, section_ref, *packs):
    rows, dof_count = packs[0].shape
    rows -= SLOT_ROWS
    faces = owner_ref.shape[1]
    sign = (1 - 2 * section_ref[0]).astype(jnp.float32)
    here = lax.axis_index("sub")
    owners = jnp.concatenate(
        [jnp.full((1, faces), here ^ on_even(even, odd), jnp.int32) for even, odd in partners], axis=0
    )
    named = owners == owner_ref[...]
    earlier = lax.broadcasted_iota(jnp.int32, (faces, faces), 0) < lax.broadcasted_iota(
        jnp.int32, (faces, faces), 1
    )
    rank = jnp.dot(
        named.astype(jnp.bfloat16), earlier.astype(jnp.bfloat16), preferred_element_type=jnp.float32
    )
    place = jnp.where(named, rank, -1.0)
    at = lax.broadcasted_iota(jnp.int32, (rows, faces), 0).astype(jnp.float32)
    hit = jnp.concatenate([place[p : p + 1, :] == at for p in range(len(packs))], axis=0)
    hit = hit.astype(jnp.bfloat16)
    packed = jnp.dot(hit, scale_ref[...], preferred_element_type=jnp.float32) * sign
    listed = lax.dot_general(
        slot_ref[...].astype(jnp.bfloat16), hit, (((1,), (1,)), ((), ())), preferred_element_type=jnp.float32
    )
    packed = packed.astype(jnp.bfloat16)
    for p, pack_ref in enumerate(packs):
        pack_ref[:rows, :] = packed[p * rows : (p + 1) * rows, :]
        meta = jnp.concatenate(
            [listed[:, p * rows : (p + 1) * rows], jnp.zeros((1, dof_count - rows), jnp.float32)], axis=1
        )
        pack_ref[rows:, :] = jnp.broadcast_to(meta, (SLOT_ROWS, dof_count)).astype(jnp.bfloat16)


def block_weights(packs, rows, blocks_own):
    first = lax.axis_index("face") * blocks_own
    block_ids = first + lax.broadcasted_iota(jnp.int32, (blocks_own, rows), 0)
    total = None
    for pack in packs:
        slots = pack[rows : rows + SLOT_ROWS, :].astype(jnp.int32)[:1, :rows]
        hit = (slots == block_ids).astype(jnp.bfloat16)
        part = jnp.dot(hit, pack[:rows, :], preferred_element_type=jnp.float32)
        total = part if total is None else total + part
    return total


def own_kernel(
    mortar_ref,
    rate_ref,
    cell_ref,
    owner_ref,
    slot_ref,
    scale_ref,
    section_ref,
    basis_ref,
    swapped_ref,
    pumped_ref,
    sum_ref,
    weight_ref,
):
    blocks_own, columns, dof_count = pumped_ref.shape
    faces = owner_ref.shape[1]
    here = lax.axis_index("sub")
    first_block = lax.axis_index("face") * blocks_own
    sign = (1 - 2 * section_ref[0]).astype(jnp.float32)
    block_ids = first_block + lax.broadcasted_iota(jnp.int32, (blocks_own, faces), 0)
    hit = (slot_ref[...] == block_ids) & (owner_ref[...] == here)
    weight = jnp.dot(hit.astype(jnp.bfloat16), scale_ref[...], preferred_element_type=jnp.float32) * sign
    weight_ref[...] = weight + block_weights((swapped_ref,), swapped_ref.shape[0] - SLOT_ROWS, blocks_own)

    square = (columns, columns)
    diagonal = lax.broadcasted_iota(jnp.int32, square, 0) == lax.broadcasted_iota(jnp.int32, square, 1)
    cells = jnp.sum(jnp.where(diagonal, cell_ref[...], 0), axis=1, keepdims=True)
    rates = jnp.sum(jnp.where(diagonal, rate_ref[...], 0.0), axis=1, keepdims=True)
    base = (here * mortar_ref.shape[0] + first_block) * dof_count
    offsets = cells - base - lax.broadcasted_iota(jnp.int32, (columns, dof_count), 1)
    rates = jnp.broadcast_to(rates, (columns, dof_count))
    tile_blocks = blocks_own // TILES
    for tile in range(TILES):
        at = slice(tile * tile_blocks, (tile + 1) * tile_blocks)
        values = mortar_ref[pl.ds(first_block + tile * tile_blocks, tile_blocks)].astype(jnp.float32)
        wells = jnp.stack(
            [jnp.where(offsets == block * dof_count, rates, 0.0) for block in range(at.start, at.stop)], axis=0
        )
        pumped = (values + wells).astype(jnp.bfloat16)
        pumped_ref[at] = pumped
        scaled = (pumped.astype(jnp.float32) * weight_ref[at][:, None, :]).astype(jnp.bfloat16)
        flux = jnp.dot(
            scaled.reshape(tile_blocks * columns, dof_count), basis_ref[0], preferred_element_type=jnp.float32
        )
        sum_ref[at] = flux.reshape(tile_blocks, columns, dof_count)


def stage_kernel(kinds, pumped_ref, sum_ref, *refs):
    bases, refs = refs[: 2 * len(kinds)], refs[2 * len(kinds) :]
    packs, (out_ref, weight_ref, basis_ref, scaled_ref) = refs[:-4], refs[-4:]
    blocks_own, columns, dof_count = pumped_ref.shape
    face_id = lax.axis_index("face")
    rows = packs[0].shape[0] - SLOT_ROWS
    count = weight_ref.shape[0]
    for spot in range(count):
        weight_ref[spot] = block_weights(packs[2 * spot : 2 * spot + 2], rows, blocks_own)
    spot = 0
    for at, (far, near) in enumerate(kinds):
        spots = []
        for wanted in (far, near):
            spots.append(spot if wanted else count)
            spot += wanted
        for array, core_0, core_1 in ((bases[2 * at], *spots), (bases[2 * at + 1], *spots[::-1])):
            start = pl.multiple_of(jnp.where(face_id == 0, core_0, core_1) * dof_count, dof_count)
            basis_ref[pl.ds(start, dof_count), :] = array[0]

    tile_blocks = blocks_own // TILES
    for tile in range(TILES):
        at = slice(tile * tile_blocks, (tile + 1) * tile_blocks)
        values = pumped_ref[at].astype(jnp.float32)
        for spot in range(count):
            scaled = (values * weight_ref[spot, at][:, None, :]).astype(jnp.bfloat16)
            scaled_ref[tile % 2, :, spot * dof_count : (spot + 1) * dof_count] = scaled.reshape(
                tile_blocks * columns, dof_count
            )
        total = jnp.dot(
            scaled_ref[tile % 2], basis_ref[: count * dof_count, :], preferred_element_type=jnp.float32
        )
        out_ref[at] = total.reshape(tile_blocks, columns, dof_count) + sum_ref[at]


def last_kernel(pumped_ref, sum_ref, projection_ref, *refs):
    arrays, (result_ref, weight_ref, basis_ref, scaled_ref, out_ref, sems) = refs[:-6], refs[-6:]
    blocks_own, columns, dof_count = pumped_ref.shape
    count = weight_ref.shape[0]
    for at in range(count):
        basis, basis_swapped, pack, pack_swapped = arrays[4 * at : 4 * at + 4]
        weight_ref[at] = block_weights((pack, pack_swapped), pack.shape[0] - SLOT_ROWS, blocks_own)
        for core, array in ((1, basis), (0, basis_swapped)):

            @pl.when(lax.axis_index("face") == core)
            def _():
                basis_ref[at * dof_count : (at + 1) * dof_count, :] = array[0]

    tiles = sems.shape[0]
    tile_blocks = blocks_own // tiles
    copies = []
    for tile in range(tiles):
        at = slice(tile * tile_blocks, (tile + 1) * tile_blocks)
        values = pumped_ref[at].astype(jnp.float32)
        for spot in range(count):
            scaled = (values * weight_ref[spot, at][:, None, :]).astype(jnp.bfloat16)
            scaled_ref[tile % 2, :, spot * dof_count : (spot + 1) * dof_count] = scaled.reshape(
                tile_blocks * columns, dof_count
            )
        total = jnp.dot(scaled_ref[tile % 2], basis_ref[...], preferred_element_type=jnp.float32)
        total = total + sum_ref[at].reshape(tile_blocks * columns, dof_count)
        result = jnp.dot(
            total.astype(jnp.bfloat16), projection_ref[...], preferred_element_type=jnp.float32
        )
        out_ref[at] = result.reshape(tile_blocks, columns, dof_count)
        copies.append(pltpu.make_async_copy(out_ref.at[at], result_ref.at[at], sems.at[tile]))
        copies[-1].start()
    for copy in copies:
        copy.wait()


def on_device(
    mortar_in, pump_rate, well_cell, face_owner, face_slot, face_scale, section, basis, projection
):
    blocks_dev, cols_dev, dof_count = mortar_in.shape
    faces_dev = face_slot.shape[0]
    subdomains, rights, halves = lax.axis_size("sub"), lax.axis_size("rhs"), lax.axis_size("face")
    others = subdomains - 1
    blocks_own = blocks_dev // halves
    capacity = max(2, 2 * faces_dev // subdomains)
    pack_rows = -(-capacity // ROW_TILE) * ROW_TILE + SLOT_ROWS
    block_shape = (blocks_own, cols_dev, dof_count)
    swap = [(i, i ^ 1) for i in range(halves)]

    def flat(sub, right, face):
        return (sub * rights + right) * halves + face

    partners = sorted(range(1, subdomains), key=lambda p: (p < subdomains // 2, p))
    groups = [partners[i : i + 3] for i in range(0, others, 3)]
    groups = [tuple(g) if len(g) == 3 else (g[0], g[-1], g[0]) for g in groups]
    firsts = []
    for a, b, c in groups:
        pairs = [
            (flat(s, r, face), flat(s ^ (c if face else b if r % 2 else a), r, face))
            for s in range(subdomains)
            for r in range(rights)
            for face in range(halves)
        ]
        firsts.append(lax.ppermute(basis, ("sub", "rhs", "face"), pairs))

    kinds = [(a != b, c != a or a == b) for a, b, c in groups]
    near = [(c, c) for (_, _, c), (_, has) in zip(groups, kinds) if has]
    far = [(a, b) for (a, b, _), (has, _) in zip(groups, kinds) if has]
    ways = [(0, 0), *far, *[(b, a) for a, b in far], *near]
    faces = [face_owner.reshape(1, faces_dev), face_slot.reshape(1, faces_dev), face_scale]
    packs = pl.pallas_call(
        functools.partial(pack_kernel, ways),
        out_shape=[jax.ShapeDtypeStruct((pack_rows, dof_count), jnp.bfloat16)] * len(ways),
        in_specs=[VMEM, VMEM, VMEM, SMEM],
        out_specs=[VMEM] * len(ways),
        cost_estimate=WORK,
        name="pack_weights",
    )(*faces, section)

    def along_sub(way, pack):
        pairs = [
            (s * rights + r, (s ^ way[r % 2]) * rights + r) for s in range(subdomains) for r in range(rights)
        ]
        return lax.ppermute(pack, ("sub", "rhs"), pairs)

    arrived = [along_sub(way, pack) for way, pack in zip(ways[1:], packs[1:])]
    own_swapped = lax.ppermute(packs[0], "face", swap)

    firsts, own_swapped = lax.optimization_barrier((firsts, own_swapped))
    pumped, own_sum = pl.pallas_call(
        own_kernel,
        out_shape=[
            jax.ShapeDtypeStruct(block_shape, jnp.bfloat16),
            jax.ShapeDtypeStruct(block_shape, jnp.float32),
        ],
        in_specs=[VMEM] * 6 + [SMEM, VMEM, VMEM],
        out_specs=[VMEM, VMEM],
        scratch_shapes=[pltpu.VMEM((blocks_own, dof_count), jnp.float32)],
        compiler_params=pltpu.CompilerParams(vmem_limit_bytes=32 * MIB),
        cost_estimate=WORK,
        name="own_blocks",
    )(
        mortar_in,
        pump_rate.reshape(1, cols_dev),
        well_cell.reshape(1, cols_dev),
        *faces,
        section,
        basis,
        own_swapped,
    )

    pairs = [
        (r * halves + face, r * halves if face else (r ^ 1) * halves + 1)
        for r in range(rights)
        for face in range(halves)
    ]
    early, late = [], []
    for (has_far, _), first in zip(kinds, firsts):
        early += [first, lax.ppermute(first, "face", swap)]
        if has_far:
            second = lax.ppermute(first, ("rhs", "face"), pairs)
            late.append([second, lax.ppermute(second, "face", swap)])
    count = len(far)
    soon, own_sum, early = lax.optimization_barrier((arrived[:count] + arrived[2 * count :], own_sum, early))
    arrived = soon[:count] + arrived[count : 2 * count] + soon[count:]
    swapped = [lax.ppermute(array, "face", swap) for array in arrived]
    places = dict(zip(ways[1:], zip(arrived, swapped)))
    weights = []
    for (a, b, c), (has_far, has_near) in zip(groups, kinds):
        weights += list(places[a, b]) * has_far + list(places[c, c]) * has_near
    for arrays, (a, b) in zip(late, far):
        arrays += places[b, a]

    late_count = len(late)
    count = others - late_count
    operands = [pumped, own_sum, *early, *weights]
    total = pl.pallas_call(
        functools.partial(stage_kernel, kinds),
        out_shape=jax.ShapeDtypeStruct(block_shape, jnp.float32),
        in_specs=[VMEM] * len(operands),
        out_specs=VMEM,
        scratch_shapes=[
            pltpu.VMEM((count, blocks_own, dof_count), jnp.float32),
            pltpu.VMEM(((count + 1) * dof_count, dof_count), jnp.bfloat16),
            pltpu.VMEM((2, blocks_own // TILES * cols_dev, count * dof_count), jnp.bfloat16),
        ],
        input_output_aliases={1: 0},
        compiler_params=pltpu.CompilerParams(vmem_limit_bytes=40 * MIB),
        cost_estimate=WORK,
        name="stage",
    )(*operands)

    operands = [pumped, total, projection, *sum(late, [])]
    return pl.pallas_call(
        last_kernel,
        out_shape=jax.ShapeDtypeStruct(block_shape, jnp.float32),
        in_specs=[VMEM] * len(operands),
        out_specs=HBM,
        scratch_shapes=[
            pltpu.VMEM((late_count, blocks_own, dof_count), jnp.float32),
            pltpu.VMEM((late_count * dof_count, dof_count), jnp.bfloat16),
            pltpu.VMEM((2, blocks_own // LAST_TILES * cols_dev, late_count * dof_count), jnp.bfloat16),
            pltpu.VMEM(block_shape, jnp.float32),
            pltpu.SemaphoreType.DMA((LAST_TILES,)),
        ],
        compiler_params=pltpu.CompilerParams(vmem_limit_bytes=40 * MIB),
        name="last_stage",
    )(*operands)


def solution(mesh):
    in_specs = (
        P(("groups", "sub"), "rhs", None),
        P(("groups", "rhs")),
        P(("groups", "rhs")),
        P(("groups", "sub", "face"), None),
        P(("groups", "sub", "face")),
        P(("groups", "sub", "face"), None),
        P(("groups", "sub")),
        P(("groups", "sub"), None, None),
        P(),
    )
    out_specs = P(("groups", "sub", "face"), "rhs", None)
    return jax.shard_map(
        on_device, mesh=mesh, in_specs=in_specs, out_specs=out_specs, check_vma=False
    )
```

```python
import functools

import jax
import jax.numpy as jnp
from jax import lax
from jax.experimental import pallas as pl
from jax.experimental.pallas import tpu as pltpu
from jax.sharding import PartitionSpec as P

ROW_TILE = 16
SLOT_ROWS = 8
VMEM = pl.BlockSpec(memory_space=pltpu.VMEM)
HBM = pl.BlockSpec(memory_space=pltpu.HBM)
SMEM = pl.BlockSpec(memory_space=pltpu.SMEM)
MIB = 1024 * 1024
TILES = 4
LAST_TILES = 8
LIGHT = pl.CostEstimate(flops=1_000_000, bytes_accessed=1024, transcendentals=0)
WORK = pl.CostEstimate(flops=4_000_000_000, bytes_accessed=8 * MIB, transcendentals=0)


def pack_kernel(partners, owner_ref, slot_ref, scale_ref, section_ref, *packs):
    rows, dof_count = packs[0].shape
    rows -= SLOT_ROWS
    faces = owner_ref.shape[1]
    sign = (1 - 2 * section_ref[0]).astype(jnp.float32)
    here = lax.axis_index("sub")
    owners = jnp.concatenate(
        [jnp.full((1, faces), here ^ partner, jnp.int32) for partner in partners], axis=0
    )
    named = owners == owner_ref[...]
    earlier = lax.broadcasted_iota(jnp.int32, (faces, faces), 0) < lax.broadcasted_iota(
        jnp.int32, (faces, faces), 1
    )
    rank = jnp.dot(
        named.astype(jnp.bfloat16), earlier.astype(jnp.bfloat16), preferred_element_type=jnp.float32
    )
    place = jnp.where(named, rank, -1.0)
    at = lax.broadcasted_iota(jnp.int32, (rows, faces), 0).astype(jnp.float32)
    hit = jnp.concatenate([place[p : p + 1, :] == at for p in range(len(packs))], axis=0)
    hit = hit.astype(jnp.bfloat16)
    packed = jnp.dot(hit, scale_ref[...], preferred_element_type=jnp.float32) * sign
    listed = lax.dot_general(
        slot_ref[...].astype(jnp.bfloat16), hit, (((1,), (1,)), ((), ())), preferred_element_type=jnp.float32
    )
    packed = packed.astype(jnp.bfloat16)
    for p, pack_ref in enumerate(packs):
        pack_ref[:rows, :] = packed[p * rows : (p + 1) * rows, :]
        meta = jnp.concatenate(
            [listed[:, p * rows : (p + 1) * rows], jnp.zeros((1, dof_count - rows), jnp.float32)], axis=1
        )
        pack_ref[rows:, :] = jnp.broadcast_to(meta, (SLOT_ROWS, dof_count)).astype(jnp.bfloat16)


def block_weights(packs, rows, blocks_own):
    first = lax.axis_index("face") * blocks_own
    block_ids = first + lax.broadcasted_iota(jnp.int32, (blocks_own, rows), 0)
    total = None
    for pack in packs:
        slots = pack[rows : rows + SLOT_ROWS, :].astype(jnp.int32)[:1, :rows]
        hit = (slots == block_ids).astype(jnp.bfloat16)
        part = jnp.dot(hit, pack[:rows, :], preferred_element_type=jnp.float32)
        total = part if total is None else total + part
    return total


def own_kernel(
    mortar_ref,
    rate_ref,
    cell_ref,
    owner_ref,
    slot_ref,
    scale_ref,
    section_ref,
    basis_ref,
    swapped_ref,
    pumped_ref,
    sum_ref,
    weight_ref,
):
    blocks_own, columns, dof_count = pumped_ref.shape
    faces = owner_ref.shape[1]
    here = lax.axis_index("sub")
    first_block = lax.axis_index("face") * blocks_own
    sign = (1 - 2 * section_ref[0]).astype(jnp.float32)
    block_ids = first_block + lax.broadcasted_iota(jnp.int32, (blocks_own, faces), 0)
    hit = (slot_ref[...] == block_ids) & (owner_ref[...] == here)
    weight = jnp.dot(hit.astype(jnp.bfloat16), scale_ref[...], preferred_element_type=jnp.float32) * sign
    weight_ref[...] = weight + block_weights((swapped_ref,), swapped_ref.shape[0] - SLOT_ROWS, blocks_own)

    square = (columns, columns)
    diagonal = lax.broadcasted_iota(jnp.int32, square, 0) == lax.broadcasted_iota(jnp.int32, square, 1)
    cells = jnp.sum(jnp.where(diagonal, cell_ref[...], 0), axis=1, keepdims=True)
    rates = jnp.sum(jnp.where(diagonal, rate_ref[...], 0.0), axis=1, keepdims=True)
    base = (here * mortar_ref.shape[0] + first_block) * dof_count
    offsets = cells - base - lax.broadcasted_iota(jnp.int32, (columns, dof_count), 1)
    rates = jnp.broadcast_to(rates, (columns, dof_count))
    tile_blocks = blocks_own // TILES
    for tile in range(TILES):
        at = slice(tile * tile_blocks, (tile + 1) * tile_blocks)
        values = mortar_ref[pl.ds(first_block + tile * tile_blocks, tile_blocks)].astype(jnp.float32)
        wells = jnp.stack(
            [jnp.where(offsets == block * dof_count, rates, 0.0) for block in range(at.start, at.stop)], axis=0
        )
        pumped = (values + wells).astype(jnp.bfloat16)
        pumped_ref[at] = pumped
        scaled = (pumped.astype(jnp.float32) * weight_ref[at][:, None, :]).astype(jnp.bfloat16)
        flux = jnp.dot(
            scaled.reshape(tile_blocks * columns, dof_count), basis_ref[0], preferred_element_type=jnp.float32
        )
        sum_ref[at] = flux.reshape(tile_blocks, columns, dof_count)


def gather_partners(arrays, weight_ref, basis_ref):
    count, blocks_own, dof_count = weight_ref.shape
    for at in range(count):
        base_0, base_1, pack, pack_swapped = arrays[4 * at : 4 * at + 4]
        weight_ref[at] = block_weights((pack, pack_swapped), pack.shape[0] - SLOT_ROWS, blocks_own)
        for core, base in enumerate((base_0, base_1)):

            @pl.when(lax.axis_index("face") == core)
            def _():
                basis_ref[at * dof_count : (at + 1) * dof_count, :] = base[0]


def tile_flux(at, slot, pumped_ref, sum_ref, weight_ref, basis_ref, scaled_ref):
    count, _, dof_count = weight_ref.shape
    rows = scaled_ref.shape[1]
    values = pumped_ref[at].astype(jnp.float32)
    for spot in range(count):
        scaled = (values * weight_ref[spot, at][:, None, :]).astype(jnp.bfloat16)
        scaled_ref[slot, :, spot * dof_count : (spot + 1) * dof_count] = scaled.reshape(rows, dof_count)
    total = jnp.dot(scaled_ref[slot], basis_ref[...], preferred_element_type=jnp.float32)
    return total + sum_ref[at].reshape(rows, dof_count)


def stage_kernel(pumped_ref, sum_ref, *refs):
    arrays, (out_ref, weight_ref, basis_ref, scaled_ref) = refs[:-4], refs[-4:]
    gather_partners(arrays, weight_ref, basis_ref)
    tile_blocks = pumped_ref.shape[0] // TILES
    for tile in range(TILES):
        at = slice(tile * tile_blocks, (tile + 1) * tile_blocks)
        total = tile_flux(at, tile % 2, pumped_ref, sum_ref, weight_ref, basis_ref, scaled_ref)
        out_ref[at] = total.reshape(pumped_ref[at].shape)


def last_kernel(pumped_ref, sum_ref, projection_ref, *refs):
    arrays, (result_ref, weight_ref, basis_ref, scaled_ref, out_ref, sems) = refs[:-6], refs[-6:]
    gather_partners(arrays, weight_ref, basis_ref)
    tiles = sems.shape[0]
    tile_blocks = pumped_ref.shape[0] // tiles
    copies = []
    for tile in range(tiles):
        at = slice(tile * tile_blocks, (tile + 1) * tile_blocks)
        total = tile_flux(at, tile % 2, pumped_ref, sum_ref, weight_ref, basis_ref, scaled_ref)
        result = jnp.dot(
            total.astype(jnp.bfloat16), projection_ref[...], preferred_element_type=jnp.float32
        )
        out_ref[at] = result.reshape(pumped_ref[at].shape)
        copies.append(pltpu.make_async_copy(out_ref.at[at], result_ref.at[at], sems.at[tile]))
        copies[-1].start()
    for copy in copies:
        copy.wait()


def on_device(
    mortar_in, pump_rate, well_cell, face_owner, face_slot, face_scale, section, basis, projection
):
    blocks_dev, cols_dev, dof_count = mortar_in.shape
    faces_dev = face_slot.shape[0]
    subdomains, halves = lax.axis_size("sub"), lax.axis_size("face")
    blocks_own = blocks_dev // halves
    capacity = max(2, 2 * faces_dev // subdomains)
    pack_rows = -(-capacity // ROW_TILE) * ROW_TILE + SLOT_ROWS
    block_shape = (blocks_own, cols_dev, dof_count)
    swap = [(i, i ^ 1) for i in range(halves)]

    def flat(sub, face):
        return sub * halves + face

    evens = list(range(2, subdomains, 2))
    cells = [(s, face) for s in range(subdomains) for face in range(halves)]
    firsts = [
        lax.ppermute(
            basis, ("sub", "face"), [(flat(s, face), flat(s ^ (1 if face else p), face)) for s, face in cells]
        )
        for p in evens
    ]
    partners = [0, *evens, 1, *[p + 1 for p in evens]]
    early_count = 1 + len(evens) + 1
    faces = [face_owner.reshape(1, faces_dev), face_slot.reshape(1, faces_dev), face_scale]
    packs = pl.pallas_call(
        functools.partial(pack_kernel, partners),
        out_shape=[jax.ShapeDtypeStruct((pack_rows, dof_count), jnp.bfloat16)] * len(partners),
        in_specs=[VMEM, VMEM, VMEM, SMEM],
        out_specs=[VMEM] * len(partners),
        cost_estimate=WORK,
        name="pack_weights",
    )(*faces, section)

    arrived = [
        lax.ppermute(pack, "sub", [(i, i ^ p) for i in range(subdomains)]) for p, pack in zip(partners[1:], packs[1:])
    ]
    own_swapped = lax.ppermute(packs[0], "face", swap)

    firsts, own_swapped = lax.optimization_barrier((firsts, own_swapped))
    pumped, own_sum = pl.pallas_call(
        own_kernel,
        out_shape=[
            jax.ShapeDtypeStruct(block_shape, jnp.bfloat16),
            jax.ShapeDtypeStruct(block_shape, jnp.float32),
        ],
        in_specs=[VMEM] * 6 + [SMEM, VMEM, VMEM],
        out_specs=[VMEM, VMEM],
        scratch_shapes=[pltpu.VMEM((blocks_own, dof_count), jnp.float32)],
        compiler_params=pltpu.CompilerParams(vmem_limit_bytes=32 * MIB),
        cost_estimate=WORK,
        name="own_blocks",
    )(
        mortar_in,
        pump_rate.reshape(1, cols_dev),
        well_cell.reshape(1, cols_dev),
        *faces,
        section,
        basis,
        own_swapped,
    )

    pairs = [(flat(s, face), flat(s, 0) if face else flat(s ^ 1, 1)) for s, face in cells]
    seconds = [lax.ppermute(first, ("sub", "face"), pairs) for first in firsts]
    firsts_swapped = [lax.ppermute(first, "face", swap) for first in firsts]
    seconds_swapped = [lax.ppermute(second, "face", swap) for second in seconds]
    soon, own_sum, firsts_swapped = lax.optimization_barrier(
        (arrived[: early_count - 1], own_sum, firsts_swapped)
    )
    arrived = soon + arrived[early_count - 1 :]
    swapped = [lax.ppermute(array, "face", swap) for array in arrived]
    weights = dict(zip(partners[1:], zip(arrived, swapped)))
    early = [[first, other, *weights[p]] for p, first, other in zip(evens, firsts, firsts_swapped)]
    early.append([firsts_swapped[0], firsts[0], *weights[1]])
    late = [[other, second, *weights[p + 1]] for p, second, other in zip(evens, seconds, seconds_swapped)]

    def scratch(count, tiles):
        return [
            pltpu.VMEM((count, blocks_own, dof_count), jnp.float32),
            pltpu.VMEM((count * dof_count, dof_count), jnp.bfloat16),
            pltpu.VMEM((2, blocks_own // tiles * cols_dev, count * dof_count), jnp.bfloat16),
        ]

    operands = [pumped, own_sum, *sum(early, [])]
    total = pl.pallas_call(
        stage_kernel,
        out_shape=jax.ShapeDtypeStruct(block_shape, jnp.float32),
        in_specs=[VMEM] * len(operands),
        out_specs=VMEM,
        scratch_shapes=scratch(len(early), TILES),
        input_output_aliases={1: 0},
        compiler_params=pltpu.CompilerParams(vmem_limit_bytes=40 * MIB),
        cost_estimate=WORK,
        name="stage",
    )(*operands)

    operands = [pumped, total, projection, *sum(late, [])]
    return pl.pallas_call(
        last_kernel,
        out_shape=jax.ShapeDtypeStruct(block_shape, jnp.float32),
        in_specs=[VMEM] * len(operands),
        out_specs=HBM,
        scratch_shapes=[
            *scratch(len(late), LAST_TILES),
            pltpu.VMEM(block_shape, jnp.float32),
            pltpu.SemaphoreType.DMA((LAST_TILES,)),
        ],
        compiler_params=pltpu.CompilerParams(vmem_limit_bytes=40 * MIB),
        name="last_stage",
    )(*operands)


def solution(mesh):
    in_specs = (
        P(("groups", "sub"), "rhs", None),
        P(("groups", "rhs")),
        P(("groups", "rhs")),
        P(("groups", "sub", "face"), None),
        P(("groups", "sub", "face")),
        P(("groups", "sub", "face"), None),
        P(("groups", "sub")),
        P(("groups", "sub"), None, None),
        P(),
    )
    out_specs = P(("groups", "sub", "face"), "rhs", None)
    return jax.shard_map(
        on_device, mesh=mesh, in_specs=in_specs, out_specs=out_specs, check_vma=False
    )
```

```python
import functools

import jax
import jax.numpy as jnp
from jax import lax
from jax.experimental import pallas as pl
from jax.experimental.pallas import tpu as pltpu
from jax.sharding import PartitionSpec as P

ROW_TILE = 16
SLOT_ROWS = 8
VMEM = pl.BlockSpec(memory_space=pltpu.VMEM)
HBM = pl.BlockSpec(memory_space=pltpu.HBM)
SMEM = pl.BlockSpec(memory_space=pltpu.SMEM)
MIB = 1024 * 1024
TILES = 4
LAST_TILES = 8
LIGHT = pl.CostEstimate(flops=1_000_000, bytes_accessed=1024, transcendentals=0)
WORK = pl.CostEstimate(flops=4_000_000_000, bytes_accessed=8 * MIB, transcendentals=0)


def pack_kernel(partners, owner_ref, slot_ref, scale_ref, section_ref, *packs):
    rows, dof_count = packs[0].shape
    rows -= SLOT_ROWS
    faces = owner_ref.shape[1]
    sign = (1 - 2 * section_ref[0]).astype(jnp.float32)
    here = lax.axis_index("sub")
    owners = jnp.concatenate(
        [jnp.full((1, faces), here ^ partner, jnp.int32) for partner in partners], axis=0
    )
    named = owners == owner_ref[...]
    earlier = lax.broadcasted_iota(jnp.int32, (faces, faces), 0) < lax.broadcasted_iota(
        jnp.int32, (faces, faces), 1
    )
    rank = jnp.dot(
        named.astype(jnp.bfloat16), earlier.astype(jnp.bfloat16), preferred_element_type=jnp.float32
    )
    place = jnp.where(named, rank, -1.0)
    at = lax.broadcasted_iota(jnp.int32, (rows, faces), 0).astype(jnp.float32)
    hit = jnp.concatenate([place[p : p + 1, :] == at for p in range(len(packs))], axis=0)
    hit = hit.astype(jnp.bfloat16)
    packed = jnp.dot(hit, scale_ref[...], preferred_element_type=jnp.float32) * sign
    listed = lax.dot_general(
        slot_ref[...].astype(jnp.bfloat16), hit, (((1,), (1,)), ((), ())), preferred_element_type=jnp.float32
    )
    packed = packed.astype(jnp.bfloat16)
    for p, pack_ref in enumerate(packs):
        pack_ref[:rows, :] = packed[p * rows : (p + 1) * rows, :]
        meta = jnp.concatenate(
            [listed[:, p * rows : (p + 1) * rows], jnp.zeros((1, dof_count - rows), jnp.float32)], axis=1
        )
        pack_ref[rows:, :] = jnp.broadcast_to(meta, (SLOT_ROWS, dof_count)).astype(jnp.bfloat16)


def block_weights(packs, rows, blocks_own):
    first = lax.axis_index("face") * blocks_own
    block_ids = first + lax.broadcasted_iota(jnp.int32, (blocks_own, rows), 0)
    total = None
    for pack in packs:
        slots = pack[rows : rows + SLOT_ROWS, :].astype(jnp.int32)[:1, :rows]
        hit = (slots == block_ids).astype(jnp.bfloat16)
        part = jnp.dot(hit, pack[:rows, :], preferred_element_type=jnp.float32)
        total = part if total is None else total + part
    return total


def own_kernel(
    mortar_ref,
    rate_ref,
    cell_ref,
    owner_ref,
    slot_ref,
    scale_ref,
    section_ref,
    basis_ref,
    swapped_ref,
    pumped_ref,
    sum_ref,
    weight_ref,
):
    blocks_own, columns, dof_count = pumped_ref.shape
    faces = owner_ref.shape[1]
    here = lax.axis_index("sub")
    first_block = lax.axis_index("face") * blocks_own
    sign = (1 - 2 * section_ref[0]).astype(jnp.float32)
    block_ids = first_block + lax.broadcasted_iota(jnp.int32, (blocks_own, faces), 0)
    hit = (slot_ref[...] == block_ids) & (owner_ref[...] == here)
    weight = jnp.dot(hit.astype(jnp.bfloat16), scale_ref[...], preferred_element_type=jnp.float32) * sign
    weight_ref[...] = weight + block_weights((swapped_ref,), swapped_ref.shape[0] - SLOT_ROWS, blocks_own)

    square = (columns, columns)
    diagonal = lax.broadcasted_iota(jnp.int32, square, 0) == lax.broadcasted_iota(jnp.int32, square, 1)
    cells = jnp.sum(jnp.where(diagonal, cell_ref[...], 0), axis=1, keepdims=True)
    rates = jnp.sum(jnp.where(diagonal, rate_ref[...], 0.0), axis=1, keepdims=True)
    base = (here * mortar_ref.shape[0] + first_block) * dof_count
    offsets = cells - base - lax.broadcasted_iota(jnp.int32, (columns, dof_count), 1)
    rates = jnp.broadcast_to(rates, (columns, dof_count))
    tile_blocks = blocks_own // TILES
    for tile in range(TILES):
        at = slice(tile * tile_blocks, (tile + 1) * tile_blocks)
        values = mortar_ref[pl.ds(first_block + tile * tile_blocks, tile_blocks)].astype(jnp.float32)
        wells = jnp.stack(
            [jnp.where(offsets == block * dof_count, rates, 0.0) for block in range(at.start, at.stop)], axis=0
        )
        pumped = (values + wells).astype(jnp.bfloat16)
        pumped_ref[at] = pumped
        scaled = (pumped.astype(jnp.float32) * weight_ref[at][:, None, :]).astype(jnp.bfloat16)
        flux = jnp.dot(
            scaled.reshape(tile_blocks * columns, dof_count), basis_ref[0], preferred_element_type=jnp.float32
        )
        sum_ref[at] = flux.reshape(tile_blocks, columns, dof_count)


def gather_partners(arrays, weight_ref, basis_ref):
    count, blocks_own, dof_count = weight_ref.shape
    for at in range(count):
        base_0, base_1, pack, pack_swapped = arrays[4 * at : 4 * at + 4]
        weight_ref[at] = block_weights((pack, pack_swapped), pack.shape[0] - SLOT_ROWS, blocks_own)
        for core, base in enumerate((base_0, base_1)):

            @pl.when(lax.axis_index("face") == core)
            def _():
                basis_ref[at * dof_count : (at + 1) * dof_count, :] = base[0]


def tile_flux(at, slot, pumped_ref, sum_ref, weight_ref, basis_ref, scaled_ref):
    count, _, dof_count = weight_ref.shape
    rows = scaled_ref.shape[1]
    values = pumped_ref[at].astype(jnp.float32)
    for spot in range(count):
        scaled = (values * weight_ref[spot, at][:, None, :]).astype(jnp.bfloat16)
        scaled_ref[slot, :, spot * dof_count : (spot + 1) * dof_count] = scaled.reshape(rows, dof_count)
    total = jnp.dot(scaled_ref[slot], basis_ref[...], preferred_element_type=jnp.float32)
    return total + sum_ref[at].reshape(rows, dof_count)


def stage_kernel(pumped_ref, sum_ref, *refs):
    arrays, (out_ref, weight_ref, basis_ref, scaled_ref) = refs[:-4], refs[-4:]
    gather_partners(arrays, weight_ref, basis_ref)
    tile_blocks = pumped_ref.shape[0] // TILES
    for tile in range(TILES):
        at = slice(tile * tile_blocks, (tile + 1) * tile_blocks)
        total = tile_flux(at, tile % 2, pumped_ref, sum_ref, weight_ref, basis_ref, scaled_ref)
        out_ref[at] = total.reshape(pumped_ref[at].shape)


def last_kernel(pumped_ref, sum_ref, projection_ref, *refs):
    arrays, (result_ref, weight_ref, basis_ref, scaled_ref, out_ref, sems) = refs[:-6], refs[-6:]
    gather_partners(arrays, weight_ref, basis_ref)
    tiles = sems.shape[0]
    tile_blocks = pumped_ref.shape[0] // tiles
    copies = []
    for tile in range(tiles):
        at = slice(tile * tile_blocks, (tile + 1) * tile_blocks)
        total = tile_flux(at, tile % 2, pumped_ref, sum_ref, weight_ref, basis_ref, scaled_ref)
        result = jnp.dot(
            total.astype(jnp.bfloat16), projection_ref[...], preferred_element_type=jnp.float32
        )
        out_ref[at] = result.reshape(pumped_ref[at].shape)
        copies.append(pltpu.make_async_copy(out_ref.at[at], result_ref.at[at], sems.at[tile]))
        copies[-1].start()
    for copy in copies:
        copy.wait()


def on_device(
    mortar_in, pump_rate, well_cell, face_owner, face_slot, face_scale, section, basis, projection
):
    blocks_dev, cols_dev, dof_count = mortar_in.shape
    faces_dev = face_slot.shape[0]
    subdomains, halves = lax.axis_size("sub"), lax.axis_size("face")
    blocks_own = blocks_dev // halves
    capacity = max(2, 2 * faces_dev // subdomains)
    pack_rows = -(-capacity // ROW_TILE) * ROW_TILE + SLOT_ROWS
    block_shape = (blocks_own, cols_dev, dof_count)
    swap = [(i, i ^ 1) for i in range(halves)]

    def flat(sub, face):
        return sub * halves + face

    evens = list(range(2, subdomains, 2))
    cells = [(s, face) for s in range(subdomains) for face in range(halves)]
    firsts = [
        lax.ppermute(
            basis, ("sub", "face"), [(flat(s, face), flat(s ^ (1 if face else p), face)) for s, face in cells]
        )
        for p in evens
    ]
    partners = [0, *evens, 1, *[p + 1 for p in evens]]
    early_count = 1 + len(evens) + 1
    faces = [face_owner.reshape(1, faces_dev), face_slot.reshape(1, faces_dev), face_scale]
    packs = pl.pallas_call(
        functools.partial(pack_kernel, partners),
        out_shape=[jax.ShapeDtypeStruct((pack_rows, dof_count), jnp.bfloat16)] * len(partners),
        in_specs=[VMEM, VMEM, VMEM, SMEM],
        out_specs=[VMEM] * len(partners),
        cost_estimate=WORK,
        name="pack_weights",
    )(*faces, section)

    arrived = [
        lax.ppermute(pack, "sub", [(i, i ^ p) for i in range(subdomains)]) for p, pack in zip(partners[1:], packs[1:])
    ]
    own_swapped = lax.ppermute(packs[0], "face", swap)

    firsts, own_swapped = lax.optimization_barrier((firsts, own_swapped))
    pumped, own_sum = pl.pallas_call(
        own_kernel,
        out_shape=[
            jax.ShapeDtypeStruct(block_shape, jnp.bfloat16),
            jax.ShapeDtypeStruct(block_shape, jnp.float32),
        ],
        in_specs=[VMEM] * 6 + [SMEM, VMEM, VMEM],
        out_specs=[VMEM, VMEM],
        scratch_shapes=[pltpu.VMEM((blocks_own, dof_count), jnp.float32)],
        compiler_params=pltpu.CompilerParams(vmem_limit_bytes=32 * MIB),
        cost_estimate=WORK,
        name="own_blocks",
    )(
        mortar_in,
        pump_rate.reshape(1, cols_dev),
        well_cell.reshape(1, cols_dev),
        *faces,
        section,
        basis,
        own_swapped,
    )

    pairs = [(flat(s, face), flat(s, 0) if face else flat(s ^ 1, 1)) for s, face in cells]
    seconds = [lax.ppermute(first, ("sub", "face"), pairs) for first in firsts]
    firsts_swapped = [lax.ppermute(first, "face", swap) for first in firsts]
    soon, own_sum, firsts_swapped = lax.optimization_barrier(
        (arrived[: early_count - 1], own_sum, firsts_swapped)
    )

    def with_swapped(arrays):
        return [(array, lax.ppermute(array, "face", swap)) for array in arrays]

    weights = with_swapped(soon)
    own_sum, later = lax.optimization_barrier((own_sum, arrived[early_count - 1 :]))
    later = with_swapped(later)
    early = [[first, other, *pair] for first, other, pair in zip(firsts, firsts_swapped, weights)]
    early.append([firsts_swapped[0], firsts[0], *weights[-1]])

    def scratch(count, tiles):
        return [
            pltpu.VMEM((count, blocks_own, dof_count), jnp.float32),
            pltpu.VMEM((count * dof_count, dof_count), jnp.bfloat16),
            pltpu.VMEM((2, blocks_own // tiles * cols_dev, count * dof_count), jnp.bfloat16),
        ]

    operands = [pumped, own_sum, *sum(early, [])]
    total = pl.pallas_call(
        stage_kernel,
        out_shape=jax.ShapeDtypeStruct(block_shape, jnp.float32),
        in_specs=[VMEM] * len(operands),
        out_specs=VMEM,
        scratch_shapes=scratch(len(early), TILES),
        input_output_aliases={1: 0},
        compiler_params=pltpu.CompilerParams(vmem_limit_bytes=40 * MIB),
        cost_estimate=LIGHT,
        name="stage",
    )(*operands)

    seconds, total = lax.optimization_barrier((seconds, total))
    late = [[other, second, *pair] for (second, other), pair in zip(with_swapped(seconds), later)]

    operands = [pumped, total, projection, *sum(late, [])]
    return pl.pallas_call(
        last_kernel,
        out_shape=jax.ShapeDtypeStruct(block_shape, jnp.float32),
        in_specs=[VMEM] * len(operands),
        out_specs=HBM,
        scratch_shapes=[
            *scratch(len(late), LAST_TILES),
            pltpu.VMEM(block_shape, jnp.float32),
            pltpu.SemaphoreType.DMA((LAST_TILES,)),
        ],
        compiler_params=pltpu.CompilerParams(vmem_limit_bytes=40 * MIB),
        name="last_stage",
    )(*operands)


def solution(mesh):
    in_specs = (
        P(("groups", "sub"), "rhs", None),
        P(("groups", "rhs")),
        P(("groups", "rhs")),
        P(("groups", "sub", "face"), None),
        P(("groups", "sub", "face")),
        P(("groups", "sub", "face"), None),
        P(("groups", "sub")),
        P(("groups", "sub"), None, None),
        P(),
    )
    out_specs = P(("groups", "sub", "face"), "rhs", None)
    return jax.shard_map(
        on_device, mesh=mesh, in_specs=in_specs, out_specs=out_specs, check_vma=False
    )
```

```python
import functools

import jax
import jax.numpy as jnp
from jax import lax
from jax.experimental import pallas as pl
from jax.experimental.pallas import tpu as pltpu
from jax.sharding import PartitionSpec as P

ROW_TILE = 16
SLOT_ROWS = 16
VMEM = pl.BlockSpec(memory_space=pltpu.VMEM)
HBM = pl.BlockSpec(memory_space=pltpu.HBM)
SMEM = pl.BlockSpec(memory_space=pltpu.SMEM)
MIB = 1024 * 1024
TILES = 4
LAST_TILES = 8
LIGHT = pl.CostEstimate(flops=1_000_000, bytes_accessed=1024, transcendentals=0)
WORK = pl.CostEstimate(flops=4_000_000_000, bytes_accessed=8 * MIB, transcendentals=0)


def pack_kernel(partners, owner_any, slot_any, scale_any, section_ref, *refs):
    packs, (owner_ref, slot_ref, scale_ref, packed_ref, fetch_sems, sems) = refs[:-6], refs[-6:]
    fetches = [
        pltpu.make_async_copy(source, target, fetch_sems.at[i])
        for i, (source, target) in enumerate(
            [(owner_any, owner_ref), (slot_any, slot_ref), (scale_any, scale_ref)]
        )
    ]
    for fetch in fetches:
        fetch.start()
    _, rows, dof_count = packed_ref.shape
    rows -= SLOT_ROWS
    faces = owner_ref.shape[1]
    sign = (1 - 2 * section_ref[0]).astype(jnp.float32)
    here = lax.axis_index("sub")
    owners = jnp.concatenate(
        [jnp.full((1, faces), here ^ partner, jnp.int32) for partner in partners], axis=0
    )
    earlier = lax.broadcasted_iota(jnp.int32, (faces, faces), 0) < lax.broadcasted_iota(
        jnp.int32, (faces, faces), 1
    )
    earlier = earlier.astype(jnp.bfloat16)
    at = lax.broadcasted_iota(jnp.int32, (rows, faces), 0).astype(jnp.float32)
    fetches[0].wait()
    named = owners == owner_ref[...]
    rank = jnp.dot(named.astype(jnp.bfloat16), earlier, preferred_element_type=jnp.float32)
    place = jnp.where(named, rank, -1.0)
    fetches[1].wait()
    slots = slot_ref[...].astype(jnp.bfloat16)
    fetches[2].wait()
    copies = []
    for p in [*range(1, len(partners)), 0]:
        hit = (place[p : p + 1, :] == at).astype(jnp.bfloat16)
        packed = jnp.dot(hit, scale_ref[...], preferred_element_type=jnp.float32) * sign
        listed = lax.dot_general(
            slots, hit, (((1,), (1,)), ((), ())), preferred_element_type=jnp.float32
        )
        meta = jnp.concatenate([listed, jnp.zeros((1, dof_count - rows), jnp.float32)], axis=1)
        packed_ref[p, :rows, :] = packed.astype(jnp.bfloat16)
        packed_ref[p, rows:, :] = jnp.broadcast_to(meta, (SLOT_ROWS, dof_count)).astype(jnp.bfloat16)
        copies.append(pltpu.make_async_copy(packed_ref.at[p], packs[p], sems.at[p]))
        copies[-1].start()
    for copy in copies:
        copy.wait()


def block_weights(packs, rows, blocks_own):
    first = lax.axis_index("face") * blocks_own
    block_ids = first + lax.broadcasted_iota(jnp.int32, (blocks_own, rows), 0)
    total = None
    for pack in packs:
        slots = pack[rows : rows + SLOT_ROWS, :].astype(jnp.int32)[:1, :rows]
        hit = (slots == block_ids).astype(jnp.bfloat16)
        part = jnp.dot(hit, pack[:rows, :], preferred_element_type=jnp.float32)
        total = part if total is None else total + part
    return total


def own_kernel(
    mortar_ref,
    rate_ref,
    cell_ref,
    owner_ref,
    slot_ref,
    scale_ref,
    section_ref,
    basis_ref,
    swapped_ref,
    pumped_ref,
    sum_ref,
    weight_ref,
):
    blocks_own, columns, dof_count = pumped_ref.shape
    faces = owner_ref.shape[1]
    here = lax.axis_index("sub")
    first_block = lax.axis_index("face") * blocks_own
    sign = (1 - 2 * section_ref[0]).astype(jnp.float32)
    block_ids = first_block + lax.broadcasted_iota(jnp.int32, (blocks_own, faces), 0)
    hit = (slot_ref[...] == block_ids) & (owner_ref[...] == here)
    weight = jnp.dot(hit.astype(jnp.bfloat16), scale_ref[...], preferred_element_type=jnp.float32) * sign
    weight_ref[...] = weight + block_weights((swapped_ref,), swapped_ref.shape[0] - SLOT_ROWS, blocks_own)

    square = (columns, columns)
    diagonal = lax.broadcasted_iota(jnp.int32, square, 0) == lax.broadcasted_iota(jnp.int32, square, 1)
    cells = jnp.sum(jnp.where(diagonal, cell_ref[...], 0), axis=1, keepdims=True)
    rates = jnp.sum(jnp.where(diagonal, rate_ref[...], 0.0), axis=1, keepdims=True)
    base = (here * mortar_ref.shape[0] + first_block) * dof_count
    offsets = cells - base - lax.broadcasted_iota(jnp.int32, (columns, dof_count), 1)
    rates = jnp.broadcast_to(rates, (columns, dof_count))
    tile_blocks = blocks_own // TILES
    for tile in range(TILES):
        at = slice(tile * tile_blocks, (tile + 1) * tile_blocks)
        values = mortar_ref[pl.ds(first_block + tile * tile_blocks, tile_blocks)].astype(jnp.float32)
        wells = jnp.stack(
            [jnp.where(offsets == block * dof_count, rates, 0.0) for block in range(at.start, at.stop)], axis=0
        )
        pumped = (values + wells).astype(jnp.bfloat16)
        pumped_ref[at] = pumped
        scaled = (pumped.astype(jnp.float32) * weight_ref[at][:, None, :]).astype(jnp.bfloat16)
        flux = jnp.dot(
            scaled.reshape(tile_blocks * columns, dof_count), basis_ref[0], preferred_element_type=jnp.float32
        )
        sum_ref[at] = flux.reshape(tile_blocks, columns, dof_count)


def gather_partners(arrays, weight_ref, basis_ref):
    count, blocks_own, dof_count = weight_ref.shape
    for at in range(count):
        base_0, base_1, pack, pack_swapped = arrays[4 * at : 4 * at + 4]
        weight_ref[at] = block_weights((pack, pack_swapped), pack.shape[0] - SLOT_ROWS, blocks_own)
        for core, base in enumerate((base_0, base_1)):

            @pl.when(lax.axis_index("face") == core)
            def _():
                basis_ref[at * dof_count : (at + 1) * dof_count, :] = base[0]


def tile_flux(at, slot, pumped_ref, sum_ref, weight_ref, basis_ref, scaled_ref):
    count, _, dof_count = weight_ref.shape
    rows = scaled_ref.shape[1]
    values = pumped_ref[at].astype(jnp.float32)
    for spot in range(count):
        scaled = (values * weight_ref[spot, at][:, None, :]).astype(jnp.bfloat16)
        scaled_ref[slot, :, spot * dof_count : (spot + 1) * dof_count] = scaled.reshape(rows, dof_count)
    total = jnp.dot(scaled_ref[slot], basis_ref[...], preferred_element_type=jnp.float32)
    return total + sum_ref[at].reshape(rows, dof_count)


def stage_kernel(pumped_ref, sum_ref, *refs):
    arrays, (out_ref, weight_ref, basis_ref, scaled_ref) = refs[:-4], refs[-4:]
    gather_partners(arrays, weight_ref, basis_ref)
    tile_blocks = pumped_ref.shape[0] // TILES
    for tile in range(TILES):
        at = slice(tile * tile_blocks, (tile + 1) * tile_blocks)
        total = tile_flux(at, tile % 2, pumped_ref, sum_ref, weight_ref, basis_ref, scaled_ref)
        out_ref[at] = total.reshape(pumped_ref[at].shape)


def last_kernel(pumped_ref, sum_ref, projection_ref, *refs):
    arrays, (result_ref, weight_ref, basis_ref, scaled_ref, out_ref, sems) = refs[:-6], refs[-6:]
    gather_partners(arrays, weight_ref, basis_ref)
    tiles = sems.shape[0]
    tile_blocks = pumped_ref.shape[0] // tiles
    copies = []
    for tile in range(tiles):
        at = slice(tile * tile_blocks, (tile + 1) * tile_blocks)
        total = tile_flux(at, tile % 2, pumped_ref, sum_ref, weight_ref, basis_ref, scaled_ref)
        result = jnp.dot(
            total.astype(jnp.bfloat16), projection_ref[...], preferred_element_type=jnp.float32
        )
        out_ref[at] = result.reshape(pumped_ref[at].shape)
        copies.append(pltpu.make_async_copy(out_ref.at[at], result_ref.at[at], sems.at[tile]))
        copies[-1].start()
    for copy in copies:
        copy.wait()


def on_device(
    mortar_in, pump_rate, well_cell, face_owner, face_slot, face_scale, section, basis, projection
):
    blocks_dev, cols_dev, dof_count = mortar_in.shape
    faces_dev = face_slot.shape[0]
    subdomains, halves = lax.axis_size("sub"), lax.axis_size("face")
    blocks_own = blocks_dev // halves
    capacity = max(2, 2 * faces_dev // subdomains)
    pack_rows = -(-capacity // ROW_TILE) * ROW_TILE + SLOT_ROWS
    block_shape = (blocks_own, cols_dev, dof_count)
    swap = [(i, i ^ 1) for i in range(halves)]

    def flat(sub, face):
        return sub * halves + face

    evens = list(range(2, subdomains, 2))
    cells = [(s, face) for s in range(subdomains) for face in range(halves)]
    firsts = [
        lax.ppermute(
            basis, ("sub", "face"), [(flat(s, face), flat(s ^ (1 if face else p), face)) for s, face in cells]
        )
        for p in evens
    ]
    partners = [0, *evens, 1, *[p + 1 for p in evens]]
    early_count = 1 + len(evens) + 1
    faces = [face_owner.reshape(1, faces_dev), face_slot.reshape(1, faces_dev), face_scale]
    packs = pl.pallas_call(
        functools.partial(pack_kernel, partners),
        out_shape=[jax.ShapeDtypeStruct((pack_rows, dof_count), jnp.bfloat16)] * len(partners),
        in_specs=[HBM, HBM, HBM, SMEM],
        out_specs=[HBM] * len(partners),
        scratch_shapes=[
            pltpu.VMEM((1, faces_dev), jnp.int32),
            pltpu.VMEM((1, faces_dev), jnp.int32),
            pltpu.VMEM((faces_dev, dof_count), jnp.bfloat16),
            pltpu.VMEM((len(partners), pack_rows, dof_count), jnp.bfloat16),
            pltpu.SemaphoreType.DMA((3,)),
            pltpu.SemaphoreType.DMA((len(partners),)),
        ],
        cost_estimate=WORK,
        name="pack_weights",
    )(*faces, section)

    arrived = [
        lax.ppermute(pack, "sub", [(i, i ^ p) for i in range(subdomains)]) for p, pack in zip(partners[1:], packs[1:])
    ]
    own_swapped = lax.ppermute(packs[0], "face", swap)

    firsts, own_swapped = lax.optimization_barrier((firsts, own_swapped))
    pumped, own_sum = pl.pallas_call(
        own_kernel,
        out_shape=[
            jax.ShapeDtypeStruct(block_shape, jnp.bfloat16),
            jax.ShapeDtypeStruct(block_shape, jnp.float32),
        ],
        in_specs=[VMEM] * 6 + [SMEM, VMEM, VMEM],
        out_specs=[VMEM, VMEM],
        scratch_shapes=[pltpu.VMEM((blocks_own, dof_count), jnp.float32)],
        compiler_params=pltpu.CompilerParams(vmem_limit_bytes=32 * MIB),
        cost_estimate=WORK,
        name="own_blocks",
    )(
        mortar_in,
        pump_rate.reshape(1, cols_dev),
        well_cell.reshape(1, cols_dev),
        *faces,
        section,
        basis,
        own_swapped,
    )

    pairs = [(flat(s, face), flat(s, 0) if face else flat(s ^ 1, 1)) for s, face in cells]
    seconds = [lax.ppermute(first, ("sub", "face"), pairs) for first in firsts]
    firsts_swapped = [lax.ppermute(first, "face", swap) for first in firsts]
    soon, own_sum, firsts_swapped = lax.optimization_barrier(
        (arrived[: early_count - 1], own_sum, firsts_swapped)
    )

    def with_swapped(arrays):
        return [(array, lax.ppermute(array, "face", swap)) for array in arrays]

    weights = with_swapped(soon)
    own_sum, later = lax.optimization_barrier((own_sum, arrived[early_count - 1 :]))
    later = with_swapped(later)
    early = [[first, other, *pair] for first, other, pair in zip(firsts, firsts_swapped, weights)]
    early.append([firsts_swapped[0], firsts[0], *weights[-1]])

    def scratch(count, tiles):
        return [
            pltpu.VMEM((count, blocks_own, dof_count), jnp.float32),
            pltpu.VMEM((count * dof_count, dof_count), jnp.bfloat16),
            pltpu.VMEM((2, blocks_own // tiles * cols_dev, count * dof_count), jnp.bfloat16),
        ]

    operands = [pumped, own_sum, *sum(early, [])]
    total = pl.pallas_call(
        stage_kernel,
        out_shape=jax.ShapeDtypeStruct(block_shape, jnp.float32),
        in_specs=[VMEM] * len(operands),
        out_specs=VMEM,
        scratch_shapes=scratch(len(early), TILES),
        input_output_aliases={1: 0},
        compiler_params=pltpu.CompilerParams(vmem_limit_bytes=40 * MIB),
        cost_estimate=LIGHT,
        name="stage",
    )(*operands)

    seconds, total = lax.optimization_barrier((seconds, total))
    late = [[other, second, *pair] for (second, other), pair in zip(with_swapped(seconds), later)]

    operands = [pumped, total, projection, *sum(late, [])]
    return pl.pallas_call(
        last_kernel,
        out_shape=jax.ShapeDtypeStruct(block_shape, jnp.float32),
        in_specs=[VMEM] * len(operands),
        out_specs=HBM,
        scratch_shapes=[
            *scratch(len(late), LAST_TILES),
            pltpu.VMEM(block_shape, jnp.float32),
            pltpu.SemaphoreType.DMA((LAST_TILES,)),
        ],
        compiler_params=pltpu.CompilerParams(vmem_limit_bytes=40 * MIB),
        name="last_stage",
    )(*operands)


def solution(mesh):
    in_specs = (
        P(("groups", "sub"), "rhs", None),
        P(("groups", "rhs")),
        P(("groups", "rhs")),
        P(("groups", "sub", "face"), None),
        P(("groups", "sub", "face")),
        P(("groups", "sub", "face"), None),
        P(("groups", "sub")),
        P(("groups", "sub"), None, None),
        P(),
    )
    out_specs = P(("groups", "sub", "face"), "rhs", None)
    return jax.shard_map(
        on_device, mesh=mesh, in_specs=in_specs, out_specs=out_specs, check_vma=False
    )
```

```python
import functools

import jax
import jax.numpy as jnp
from jax import lax
from jax.experimental import pallas as pl
from jax.experimental.pallas import tpu as pltpu
from jax.sharding import PartitionSpec as P

ROW_TILE = 16
SLOT_ROWS = 16
VMEM = pl.BlockSpec(memory_space=pltpu.VMEM)
HBM = pl.BlockSpec(memory_space=pltpu.HBM)
SMEM = pl.BlockSpec(memory_space=pltpu.SMEM)
MIB = 1024 * 1024
TILES = 4
LAST_TILES = 8
LIGHT = pl.CostEstimate(flops=1_000_000, bytes_accessed=1024, transcendentals=0)
WORK = pl.CostEstimate(flops=4_000_000_000, bytes_accessed=8 * MIB, transcendentals=0)


def pack_kernel(partners, owner_ref, slot_ref, scale_ref, section_ref, *packs):
    rows, dof_count = packs[0].shape
    rows -= SLOT_ROWS
    faces = owner_ref.shape[1]
    sign = (1 - 2 * section_ref[0]).astype(jnp.float32)
    here = lax.axis_index("sub")
    owners = jnp.concatenate(
        [jnp.full((1, faces), here ^ partner, jnp.int32) for partner in partners], axis=0
    )
    named = owners == owner_ref[...]
    earlier = lax.broadcasted_iota(jnp.int32, (faces, faces), 0) < lax.broadcasted_iota(
        jnp.int32, (faces, faces), 1
    )
    rank = jnp.dot(
        named.astype(jnp.bfloat16), earlier.astype(jnp.bfloat16), preferred_element_type=jnp.float32
    )
    place = jnp.where(named, rank, -1.0)
    at = lax.broadcasted_iota(jnp.int32, (rows, faces), 0).astype(jnp.float32)
    hit = jnp.concatenate([place[p : p + 1, :] == at for p in range(len(packs))], axis=0)
    hit = hit.astype(jnp.bfloat16)
    packed = jnp.dot(hit, scale_ref[...], preferred_element_type=jnp.float32) * sign
    listed = lax.dot_general(
        slot_ref[...].astype(jnp.bfloat16), hit, (((1,), (1,)), ((), ())), preferred_element_type=jnp.float32
    )
    packed = packed.astype(jnp.bfloat16)
    for p, pack_ref in enumerate(packs):
        pack_ref[:rows, :] = packed[p * rows : (p + 1) * rows, :]
        meta = jnp.concatenate(
            [listed[:, p * rows : (p + 1) * rows], jnp.zeros((1, dof_count - rows), jnp.float32)], axis=1
        )
        pack_ref[rows:, :] = jnp.broadcast_to(meta, (SLOT_ROWS, dof_count)).astype(jnp.bfloat16)


def block_weights(packs, rows, blocks_own):
    first = lax.axis_index("face") * blocks_own
    block_ids = first + lax.broadcasted_iota(jnp.int32, (blocks_own, rows), 0)
    total = None
    for pack in packs:
        slots = pack[rows : rows + SLOT_ROWS, :].astype(jnp.int32)[:1, :rows]
        hit = (slots == block_ids).astype(jnp.bfloat16)
        part = jnp.dot(hit, pack[:rows, :], preferred_element_type=jnp.float32)
        total = part if total is None else total + part
    return total


def own_kernel(
    mortar_ref,
    rate_ref,
    cell_ref,
    owner_ref,
    slot_ref,
    scale_ref,
    section_ref,
    basis_ref,
    swapped_ref,
    pumped_ref,
    sum_ref,
    weight_ref,
):
    blocks_own, columns, dof_count = pumped_ref.shape
    faces = owner_ref.shape[1]
    here = lax.axis_index("sub")
    first_block = lax.axis_index("face") * blocks_own
    sign = (1 - 2 * section_ref[0]).astype(jnp.float32)
    block_ids = first_block + lax.broadcasted_iota(jnp.int32, (blocks_own, faces), 0)
    hit = (slot_ref[...] == block_ids) & (owner_ref[...] == here)
    weight = jnp.dot(hit.astype(jnp.bfloat16), scale_ref[...], preferred_element_type=jnp.float32) * sign
    weight_ref[...] = weight + block_weights((swapped_ref,), swapped_ref.shape[0] - SLOT_ROWS, blocks_own)

    square = (columns, columns)
    diagonal = lax.broadcasted_iota(jnp.int32, square, 0) == lax.broadcasted_iota(jnp.int32, square, 1)
    cells = jnp.sum(jnp.where(diagonal, cell_ref[...], 0), axis=1, keepdims=True)
    rates = jnp.sum(jnp.where(diagonal, rate_ref[...], 0.0), axis=1, keepdims=True)
    base = (here * mortar_ref.shape[0] + first_block) * dof_count
    offsets = cells - base - lax.broadcasted_iota(jnp.int32, (columns, dof_count), 1)
    rates = jnp.broadcast_to(rates, (columns, dof_count))
    tile_blocks = blocks_own // TILES
    for tile in range(TILES):
        at = slice(tile * tile_blocks, (tile + 1) * tile_blocks)
        values = mortar_ref[pl.ds(first_block + tile * tile_blocks, tile_blocks)].astype(jnp.float32)
        wells = jnp.stack(
            [jnp.where(offsets == block * dof_count, rates, 0.0) for block in range(at.start, at.stop)], axis=0
        )
        pumped = (values + wells).astype(jnp.bfloat16)
        pumped_ref[at] = pumped
        scaled = (pumped.astype(jnp.float32) * weight_ref[at][:, None, :]).astype(jnp.bfloat16)
        flux = jnp.dot(
            scaled.reshape(tile_blocks * columns, dof_count), basis_ref[0], preferred_element_type=jnp.float32
        )
        sum_ref[at] = flux.reshape(tile_blocks, columns, dof_count)


def gather_partners(arrays, weight_ref, basis_ref):
    count, blocks_own, dof_count = weight_ref.shape
    for at in range(count):
        base_0, base_1, pack, pack_swapped = arrays[4 * at : 4 * at + 4]
        weight_ref[at] = block_weights((pack, pack_swapped), pack.shape[0] - SLOT_ROWS, blocks_own)
        for core, base in enumerate((base_0, base_1)):

            @pl.when(lax.axis_index("face") == core)
            def _():
                basis_ref[at * dof_count : (at + 1) * dof_count, :] = base[0]


def tile_flux(at, slot, pumped_ref, sum_ref, weight_ref, basis_ref, scaled_ref):
    count, _, dof_count = weight_ref.shape
    rows = scaled_ref.shape[1]
    values = pumped_ref[at].astype(jnp.float32)
    for spot in range(count):
        scaled = (values * weight_ref[spot, at][:, None, :]).astype(jnp.bfloat16)
        scaled_ref[slot, :, spot * dof_count : (spot + 1) * dof_count] = scaled.reshape(rows, dof_count)
    total = jnp.dot(scaled_ref[slot], basis_ref[...], preferred_element_type=jnp.float32)
    return total + sum_ref[at].reshape(rows, dof_count)


def stage_kernel(pumped_ref, sum_ref, *refs):
    arrays, (out_ref, weight_ref, basis_ref, scaled_ref) = refs[:-4], refs[-4:]
    gather_partners(arrays, weight_ref, basis_ref)
    tile_blocks = pumped_ref.shape[0] // TILES
    for tile in range(TILES):
        at = slice(tile * tile_blocks, (tile + 1) * tile_blocks)
        total = tile_flux(at, tile % 2, pumped_ref, sum_ref, weight_ref, basis_ref, scaled_ref)
        out_ref[at] = total.reshape(pumped_ref[at].shape)


def last_kernel(pumped_ref, sum_ref, projection_ref, *refs):
    arrays, (result_ref, weight_ref, basis_ref, scaled_ref, out_ref, sems) = refs[:-6], refs[-6:]
    gather_partners(arrays, weight_ref, basis_ref)
    tiles = sems.shape[0]
    tile_blocks = pumped_ref.shape[0] // tiles
    copies = []
    for tile in range(tiles):
        at = slice(tile * tile_blocks, (tile + 1) * tile_blocks)
        total = tile_flux(at, tile % 2, pumped_ref, sum_ref, weight_ref, basis_ref, scaled_ref)
        result = jnp.dot(
            total.astype(jnp.bfloat16), projection_ref[...], preferred_element_type=jnp.float32
        )
        out_ref[at] = result.reshape(pumped_ref[at].shape)
        copies.append(pltpu.make_async_copy(out_ref.at[at], result_ref.at[at], sems.at[tile]))
        copies[-1].start()
    for copy in copies:
        copy.wait()


def on_device(
    mortar_in, pump_rate, well_cell, face_owner, face_slot, face_scale, section, basis, projection
):
    blocks_dev, cols_dev, dof_count = mortar_in.shape
    faces_dev = face_slot.shape[0]
    subdomains, halves = lax.axis_size("sub"), lax.axis_size("face")
    blocks_own = blocks_dev // halves
    capacity = max(2, 2 * faces_dev // subdomains)
    pack_rows = -(-capacity // ROW_TILE) * ROW_TILE + SLOT_ROWS
    block_shape = (blocks_own, cols_dev, dof_count)
    swap = [(i, i ^ 1) for i in range(halves)]

    def flat(sub, face):
        return sub * halves + face

    evens = list(range(2, subdomains, 2))
    cells = [(s, face) for s in range(subdomains) for face in range(halves)]
    firsts = [
        lax.ppermute(
            basis, ("sub", "face"), [(flat(s, face), flat(s ^ (1 if face else p), face)) for s, face in cells]
        )
        for p in evens
    ]
    partners = [0, *evens, 1, *[p + 1 for p in evens]]
    early_count = 1 + len(evens) + 1
    faces = [face_owner.reshape(1, faces_dev), face_slot.reshape(1, faces_dev), face_scale]
    packs = pl.pallas_call(
        functools.partial(pack_kernel, partners),
        out_shape=[pltpu.VMEM((pack_rows, dof_count), jnp.bfloat16)] * len(partners),
        in_specs=[VMEM, VMEM, VMEM, SMEM],
        out_specs=[VMEM] * len(partners),
        cost_estimate=WORK,
        name="pack_weights",
    )(*faces, section)

    arrived = [
        lax.ppermute(pack, "sub", [(i, i ^ p) for i in range(subdomains)]) for p, pack in zip(partners[1:], packs[1:])
    ]
    own_swapped = lax.ppermute(packs[0], "face", swap)

    firsts, own_swapped = lax.optimization_barrier((firsts, own_swapped))
    pumped, own_sum = pl.pallas_call(
        own_kernel,
        out_shape=[
            jax.ShapeDtypeStruct(block_shape, jnp.bfloat16),
            jax.ShapeDtypeStruct(block_shape, jnp.float32),
        ],
        in_specs=[VMEM] * 6 + [SMEM, VMEM, VMEM],
        out_specs=[VMEM, VMEM],
        scratch_shapes=[pltpu.VMEM((blocks_own, dof_count), jnp.float32)],
        compiler_params=pltpu.CompilerParams(vmem_limit_bytes=32 * MIB),
        cost_estimate=WORK,
        name="own_blocks",
    )(
        mortar_in,
        pump_rate.reshape(1, cols_dev),
        well_cell.reshape(1, cols_dev),
        *faces,
        section,
        basis,
        own_swapped,
    )

    pairs = [(flat(s, face), flat(s, 0) if face else flat(s ^ 1, 1)) for s, face in cells]
    seconds = [lax.ppermute(first, ("sub", "face"), pairs) for first in firsts]
    firsts_swapped = [lax.ppermute(first, "face", swap) for first in firsts]
    soon, own_sum, firsts_swapped = lax.optimization_barrier(
        (arrived[: early_count - 1], own_sum, firsts_swapped)
    )

    def with_swapped(arrays):
        return [(array, lax.ppermute(array, "face", swap)) for array in arrays]

    weights = with_swapped(soon)
    own_sum, later = lax.optimization_barrier((own_sum, arrived[early_count - 1 :]))
    later = with_swapped(later)
    early = [[first, other, *pair] for first, other, pair in zip(firsts, firsts_swapped, weights)]
    early.append([firsts_swapped[0], firsts[0], *weights[-1]])

    def scratch(count, tiles):
        return [
            pltpu.VMEM((count, blocks_own, dof_count), jnp.float32),
            pltpu.VMEM((count * dof_count, dof_count), jnp.bfloat16),
            pltpu.VMEM((2, blocks_own // tiles * cols_dev, count * dof_count), jnp.bfloat16),
        ]

    operands = [pumped, own_sum, *sum(early, [])]
    total = pl.pallas_call(
        stage_kernel,
        out_shape=jax.ShapeDtypeStruct(block_shape, jnp.float32),
        in_specs=[VMEM] * len(operands),
        out_specs=VMEM,
        scratch_shapes=scratch(len(early), TILES),
        input_output_aliases={1: 0},
        compiler_params=pltpu.CompilerParams(vmem_limit_bytes=40 * MIB),
        cost_estimate=LIGHT,
        name="stage",
    )(*operands)

    seconds, total = lax.optimization_barrier((seconds, total))
    late = [[other, second, *pair] for (second, other), pair in zip(with_swapped(seconds), later)]

    operands = [pumped, total, projection, *sum(late, [])]
    return pl.pallas_call(
        last_kernel,
        out_shape=jax.ShapeDtypeStruct(block_shape, jnp.float32),
        in_specs=[VMEM] * len(operands),
        out_specs=HBM,
        scratch_shapes=[
            *scratch(len(late), LAST_TILES),
            pltpu.VMEM(block_shape, jnp.float32),
            pltpu.SemaphoreType.DMA((LAST_TILES,)),
        ],
        compiler_params=pltpu.CompilerParams(vmem_limit_bytes=40 * MIB),
        name="last_stage",
    )(*operands)


def solution(mesh):
    in_specs = (
        P(("groups", "sub"), "rhs", None),
        P(("groups", "rhs")),
        P(("groups", "rhs")),
        P(("groups", "sub", "face"), None),
        P(("groups", "sub", "face")),
        P(("groups", "sub", "face"), None),
        P(("groups", "sub")),
        P(("groups", "sub"), None, None),
        P(),
    )
    out_specs = P(("groups", "sub", "face"), "rhs", None)
    return jax.shard_map(
        on_device, mesh=mesh, in_specs=in_specs, out_specs=out_specs, check_vma=False
    )
```

```python
import functools

import jax
import jax.numpy as jnp
from jax import lax
from jax.experimental import pallas as pl
from jax.experimental.pallas import tpu as pltpu
from jax.sharding import PartitionSpec as P

ROW_TILE = 16
SLOT_ROWS = 16
VMEM = pl.BlockSpec(memory_space=pltpu.VMEM)
HBM = pl.BlockSpec(memory_space=pltpu.HBM)
SMEM = pl.BlockSpec(memory_space=pltpu.SMEM)
MIB = 1024 * 1024
TILES = 4
LAST_TILES = 8
LIGHT = pl.CostEstimate(flops=1_000_000, bytes_accessed=1024, transcendentals=0)
WORK = pl.CostEstimate(flops=4_000_000_000, bytes_accessed=8 * MIB, transcendentals=0)


def pack_kernel(partners, owner_ref, slot_ref, scale_ref, section_ref, *packs):
    rows, dof_count = packs[0].shape
    rows -= SLOT_ROWS
    faces = owner_ref.shape[1]
    sign = (1 - 2 * section_ref[0]).astype(jnp.float32)
    here = lax.axis_index("sub")
    owners = jnp.concatenate(
        [jnp.full((1, faces), here ^ partner, jnp.int32) for partner in partners], axis=0
    )
    named = owners == owner_ref[...]
    earlier = lax.broadcasted_iota(jnp.int32, (faces, faces), 0) < lax.broadcasted_iota(
        jnp.int32, (faces, faces), 1
    )
    rank = jnp.dot(
        named.astype(jnp.bfloat16), earlier.astype(jnp.bfloat16), preferred_element_type=jnp.float32
    )
    place = jnp.where(named, rank, -1.0)
    at = lax.broadcasted_iota(jnp.int32, (rows, faces), 0).astype(jnp.float32)
    hit = jnp.concatenate([place[p : p + 1, :] == at for p in range(len(packs))], axis=0)
    hit = hit.astype(jnp.bfloat16)
    packed = jnp.dot(hit, scale_ref[...], preferred_element_type=jnp.float32) * sign
    listed = lax.dot_general(
        slot_ref[...].astype(jnp.bfloat16), hit, (((1,), (1,)), ((), ())), preferred_element_type=jnp.float32
    )
    packed = packed.astype(jnp.bfloat16)
    for p, pack_ref in enumerate(packs):
        pack_ref[:rows, :] = packed[p * rows : (p + 1) * rows, :]
        meta = jnp.concatenate(
            [listed[:, p * rows : (p + 1) * rows], jnp.zeros((1, dof_count - rows), jnp.float32)], axis=1
        )
        pack_ref[rows:, :] = jnp.broadcast_to(meta, (SLOT_ROWS, dof_count)).astype(jnp.bfloat16)


def block_weights(packs, rows, blocks_own):
    first = lax.axis_index("face") * blocks_own
    block_ids = first + lax.broadcasted_iota(jnp.int32, (blocks_own, rows), 0)
    total = None
    for pack in packs:
        slots = pack[rows : rows + SLOT_ROWS, :].astype(jnp.int32)[:1, :rows]
        hit = (slots == block_ids).astype(jnp.bfloat16)
        part = jnp.dot(hit, pack[:rows, :], preferred_element_type=jnp.float32)
        total = part if total is None else total + part
    return total


def own_kernel(
    mortar_ref,
    rate_ref,
    cell_ref,
    owner_ref,
    slot_ref,
    scale_ref,
    section_ref,
    basis_ref,
    swapped_ref,
    pumped_ref,
    sum_ref,
    weight_ref,
):
    blocks_own, columns, dof_count = pumped_ref.shape
    faces = owner_ref.shape[1]
    here = lax.axis_index("sub")
    first_block = lax.axis_index("face") * blocks_own
    sign = (1 - 2 * section_ref[0]).astype(jnp.float32)
    block_ids = first_block + lax.broadcasted_iota(jnp.int32, (blocks_own, faces), 0)
    hit = (slot_ref[...] == block_ids) & (owner_ref[...] == here)
    weight = jnp.dot(hit.astype(jnp.bfloat16), scale_ref[...], preferred_element_type=jnp.float32) * sign
    weight_ref[...] = weight + block_weights((swapped_ref,), swapped_ref.shape[0] - SLOT_ROWS, blocks_own)

    square = (columns, columns)
    diagonal = lax.broadcasted_iota(jnp.int32, square, 0) == lax.broadcasted_iota(jnp.int32, square, 1)
    cells = jnp.sum(jnp.where(diagonal, cell_ref[...], 0), axis=1, keepdims=True)
    rates = jnp.sum(jnp.where(diagonal, rate_ref[...], 0.0), axis=1, keepdims=True)
    base = (here * mortar_ref.shape[0] + first_block) * dof_count
    offsets = cells - base - lax.broadcasted_iota(jnp.int32, (columns, dof_count), 1)
    rates = jnp.broadcast_to(rates, (columns, dof_count))
    tile_blocks = blocks_own // TILES
    for tile in range(TILES):
        at = slice(tile * tile_blocks, (tile + 1) * tile_blocks)
        values = mortar_ref[pl.ds(first_block + tile * tile_blocks, tile_blocks)].astype(jnp.float32)
        wells = jnp.stack(
            [jnp.where(offsets == block * dof_count, rates, 0.0) for block in range(at.start, at.stop)], axis=0
        )
        pumped = (values + wells).astype(jnp.bfloat16)
        pumped_ref[at] = pumped
        scaled = (pumped.astype(jnp.float32) * weight_ref[at][:, None, :]).astype(jnp.bfloat16)
        flux = jnp.dot(
            scaled.reshape(tile_blocks * columns, dof_count), basis_ref[0], preferred_element_type=jnp.float32
        )
        sum_ref[at] = flux.reshape(tile_blocks, columns, dof_count)


def gather_partners(arrays, weight_ref, basis_ref):
    count, blocks_own, dof_count = weight_ref.shape
    for at in range(count):
        base_0, base_1, pack, pack_swapped = arrays[4 * at : 4 * at + 4]
        weight_ref[at] = block_weights((pack, pack_swapped), pack.shape[0] - SLOT_ROWS, blocks_own)
        for core, base in enumerate((base_0, base_1)):

            @pl.when(lax.axis_index("face") == core)
            def _():
                basis_ref[at * dof_count : (at + 1) * dof_count, :] = base[0]


def tile_flux(at, slot, pumped_ref, sum_ref, weight_ref, basis_ref, scaled_ref):
    count, _, dof_count = weight_ref.shape
    rows = scaled_ref.shape[1]
    values = pumped_ref[at].astype(jnp.float32)
    for spot in range(count):
        scaled = (values * weight_ref[spot, at][:, None, :]).astype(jnp.bfloat16)
        scaled_ref[slot, :, spot * dof_count : (spot + 1) * dof_count] = scaled.reshape(rows, dof_count)
    total = jnp.dot(scaled_ref[slot], basis_ref[...], preferred_element_type=jnp.float32)
    return total + sum_ref[at].reshape(rows, dof_count)


def stage_kernel(pumped_ref, sum_ref, *refs):
    arrays, (out_ref, weight_ref, basis_ref, scaled_ref) = refs[:-4], refs[-4:]
    gather_partners(arrays, weight_ref, basis_ref)
    tile_blocks = pumped_ref.shape[0] // TILES
    for tile in range(TILES):
        at = slice(tile * tile_blocks, (tile + 1) * tile_blocks)
        total = tile_flux(at, tile % 2, pumped_ref, sum_ref, weight_ref, basis_ref, scaled_ref)
        out_ref[at] = total.reshape(pumped_ref[at].shape)


def last_kernel(pumped_ref, sum_ref, projection_ref, *refs):
    arrays, (result_ref, weight_ref, basis_ref, scaled_ref, out_ref, sems) = refs[:-6], refs[-6:]
    gather_partners(arrays, weight_ref, basis_ref)
    tiles = sems.shape[0]
    tile_blocks = pumped_ref.shape[0] // tiles
    copies = []
    for tile in range(tiles):
        at = slice(tile * tile_blocks, (tile + 1) * tile_blocks)
        total = tile_flux(at, tile % 2, pumped_ref, sum_ref, weight_ref, basis_ref, scaled_ref)
        result = jnp.dot(
            total.astype(jnp.bfloat16), projection_ref[...], preferred_element_type=jnp.float32
        )
        out_ref[at] = result.reshape(pumped_ref[at].shape)
        copies.append(pltpu.make_async_copy(out_ref.at[at], result_ref.at[at], sems.at[tile]))
        copies[-1].start()
    for copy in copies:
        copy.wait()


def on_device(
    mortar_in, pump_rate, well_cell, face_owner, face_slot, face_scale, section, basis, projection
):
    blocks_dev, cols_dev, dof_count = mortar_in.shape
    faces_dev = face_slot.shape[0]
    subdomains, halves = lax.axis_size("sub"), lax.axis_size("face")
    blocks_own = blocks_dev // halves
    capacity = max(2, 2 * faces_dev // subdomains)
    pack_rows = -(-capacity // ROW_TILE) * ROW_TILE + SLOT_ROWS
    block_shape = (blocks_own, cols_dev, dof_count)
    swap = [(i, i ^ 1) for i in range(halves)]

    def flat(sub, face):
        return sub * halves + face

    evens = list(range(2, subdomains, 2))
    cells = [(s, face) for s in range(subdomains) for face in range(halves)]
    firsts = [
        lax.ppermute(
            basis, ("sub", "face"), [(flat(s, face), flat(s ^ (1 if face else p), face)) for s, face in cells]
        )
        for p in evens
    ]
    partners = [0, *evens, 1, *[p + 1 for p in evens]]
    early_count = 1 + len(evens) + 1
    faces = [face_owner.reshape(1, faces_dev), face_slot.reshape(1, faces_dev), face_scale]
    packs = pl.pallas_call(
        functools.partial(pack_kernel, partners),
        out_shape=[pltpu.VMEM((pack_rows, dof_count), jnp.bfloat16)] * len(partners),
        in_specs=[VMEM, VMEM, VMEM, SMEM],
        out_specs=[VMEM] * len(partners),
        cost_estimate=WORK,
        name="pack_weights",
    )(*faces, section)

    arrived = [
        lax.ppermute(pack, "sub", [(i, i ^ p) for i in range(subdomains)]) for p, pack in zip(partners[1:], packs[1:])
    ]
    own_swapped = lax.ppermute(packs[0], "face", swap)

    firsts, own_swapped = lax.optimization_barrier((firsts, own_swapped))
    pumped, own_sum = pl.pallas_call(
        own_kernel,
        out_shape=[
            jax.ShapeDtypeStruct(block_shape, jnp.bfloat16),
            jax.ShapeDtypeStruct(block_shape, jnp.float32),
        ],
        in_specs=[VMEM] * 6 + [SMEM, VMEM, VMEM],
        out_specs=[VMEM, VMEM],
        scratch_shapes=[pltpu.VMEM((blocks_own, dof_count), jnp.float32)],
        compiler_params=pltpu.CompilerParams(vmem_limit_bytes=32 * MIB),
        cost_estimate=WORK,
        name="own_blocks",
    )(
        mortar_in,
        pump_rate.reshape(1, cols_dev),
        well_cell.reshape(1, cols_dev),
        *faces,
        section,
        basis,
        own_swapped,
    )

    pairs = [(flat(s, face), flat(s, 0) if face else flat(s ^ 1, 1)) for s, face in cells]
    seconds = [lax.ppermute(first, ("sub", "face"), pairs) for first in firsts]
    firsts, arrived[len(evens)] = lax.optimization_barrier((firsts, arrived[len(evens)]))
    firsts_swapped = [lax.ppermute(first, "face", swap) for first in firsts]
    soon, own_sum, firsts_swapped = lax.optimization_barrier(
        (arrived[: early_count - 1], own_sum, firsts_swapped)
    )

    def with_swapped(arrays):
        return [(array, lax.ppermute(array, "face", swap)) for array in arrays]

    weights = with_swapped(soon)
    own_sum, later = lax.optimization_barrier((own_sum, arrived[early_count - 1 :]))
    later = with_swapped(later)
    early = [[first, other, *pair] for first, other, pair in zip(firsts, firsts_swapped, weights)]
    early.append([firsts_swapped[0], firsts[0], *weights[-1]])

    def scratch(count, tiles):
        return [
            pltpu.VMEM((count, blocks_own, dof_count), jnp.float32),
            pltpu.VMEM((count * dof_count, dof_count), jnp.bfloat16),
            pltpu.VMEM((2, blocks_own // tiles * cols_dev, count * dof_count), jnp.bfloat16),
        ]

    operands = [pumped, own_sum, *sum(early, [])]
    total = pl.pallas_call(
        stage_kernel,
        out_shape=jax.ShapeDtypeStruct(block_shape, jnp.float32),
        in_specs=[VMEM] * len(operands),
        out_specs=VMEM,
        scratch_shapes=scratch(len(early), TILES),
        input_output_aliases={1: 0},
        compiler_params=pltpu.CompilerParams(vmem_limit_bytes=40 * MIB),
        cost_estimate=LIGHT,
        name="stage",
    )(*operands)

    seconds, total = lax.optimization_barrier((seconds, total))
    late = [[other, second, *pair] for (second, other), pair in zip(with_swapped(seconds), later)]

    operands = [pumped, total, projection, *sum(late, [])]
    return pl.pallas_call(
        last_kernel,
        out_shape=jax.ShapeDtypeStruct(block_shape, jnp.float32),
        in_specs=[VMEM] * len(operands),
        out_specs=HBM,
        scratch_shapes=[
            *scratch(len(late), LAST_TILES),
            pltpu.VMEM(block_shape, jnp.float32),
            pltpu.SemaphoreType.DMA((LAST_TILES,)),
        ],
        compiler_params=pltpu.CompilerParams(vmem_limit_bytes=40 * MIB),
        name="last_stage",
    )(*operands)


def solution(mesh):
    in_specs = (
        P(("groups", "sub"), "rhs", None),
        P(("groups", "rhs")),
        P(("groups", "rhs")),
        P(("groups", "sub", "face"), None),
        P(("groups", "sub", "face")),
        P(("groups", "sub", "face"), None),
        P(("groups", "sub")),
        P(("groups", "sub"), None, None),
        P(),
    )
    out_specs = P(("groups", "sub", "face"), "rhs", None)
    return jax.shard_map(
        on_device, mesh=mesh, in_specs=in_specs, out_specs=out_specs, check_vma=False
    )
```

```python
import functools

import jax
import jax.numpy as jnp
from jax import lax
from jax.experimental import pallas as pl
from jax.experimental.pallas import tpu as pltpu
from jax.sharding import PartitionSpec as P

ROW_TILE = 16
SLOT_ROWS = 16
VMEM = pl.BlockSpec(memory_space=pltpu.VMEM)
HBM = pl.BlockSpec(memory_space=pltpu.HBM)
SMEM = pl.BlockSpec(memory_space=pltpu.SMEM)
MIB = 1024 * 1024
TILES = 4
LAST_TILES = 8
LIGHT = pl.CostEstimate(flops=1_000_000, bytes_accessed=1024, transcendentals=0)
WORK = pl.CostEstimate(flops=4_000_000_000, bytes_accessed=8 * MIB, transcendentals=0)


def pack_kernel(partners, owner_ref, slot_ref, scale_ref, section_ref, *packs):
    rows, dof_count = packs[0].shape
    rows -= SLOT_ROWS
    faces = owner_ref.shape[1]
    sign = (1 - 2 * section_ref[0]).astype(jnp.float32)
    here = lax.axis_index("sub")
    owners = jnp.concatenate(
        [jnp.full((1, faces), here ^ partner, jnp.int32) for partner in partners], axis=0
    )
    named = owners == owner_ref[...]
    earlier = lax.broadcasted_iota(jnp.int32, (faces, faces), 0) < lax.broadcasted_iota(
        jnp.int32, (faces, faces), 1
    )
    rank = jnp.dot(
        named.astype(jnp.bfloat16), earlier.astype(jnp.bfloat16), preferred_element_type=jnp.float32
    )
    place = jnp.where(named, rank, -1.0)
    at = lax.broadcasted_iota(jnp.int32, (rows, faces), 0).astype(jnp.float32)
    hit = jnp.concatenate([place[p : p + 1, :] == at for p in range(len(packs))], axis=0)
    hit = hit.astype(jnp.bfloat16)
    packed = jnp.dot(hit, scale_ref[...], preferred_element_type=jnp.float32) * sign
    listed = lax.dot_general(
        slot_ref[...].astype(jnp.bfloat16), hit, (((1,), (1,)), ((), ())), preferred_element_type=jnp.float32
    )
    packed = packed.astype(jnp.bfloat16)
    for p, pack_ref in enumerate(packs):
        pack_ref[:rows, :] = packed[p * rows : (p + 1) * rows, :]
        meta = jnp.concatenate(
            [listed[:, p * rows : (p + 1) * rows], jnp.zeros((1, dof_count - rows), jnp.float32)], axis=1
        )
        pack_ref[rows:, :] = jnp.broadcast_to(meta, (SLOT_ROWS, dof_count)).astype(jnp.bfloat16)


def block_weights(packs, rows, blocks_own):
    first = lax.axis_index("face") * blocks_own
    block_ids = first + lax.broadcasted_iota(jnp.int32, (blocks_own, rows), 0)
    total = None
    for pack in packs:
        slots = pack[rows : rows + SLOT_ROWS, :].astype(jnp.int32)[:1, :rows]
        hit = (slots == block_ids).astype(jnp.bfloat16)
        part = jnp.dot(hit, pack[:rows, :], preferred_element_type=jnp.float32)
        total = part if total is None else total + part
    return total


def own_kernel(
    mortar_ref,
    rate_ref,
    cell_ref,
    owner_ref,
    slot_ref,
    scale_ref,
    section_ref,
    basis_ref,
    swapped_ref,
    pumped_ref,
    sum_ref,
    weight_ref,
):
    blocks_own, columns, dof_count = pumped_ref.shape
    faces = owner_ref.shape[1]
    here = lax.axis_index("sub")
    first_block = lax.axis_index("face") * blocks_own
    sign = (1 - 2 * section_ref[0]).astype(jnp.float32)
    block_ids = first_block + lax.broadcasted_iota(jnp.int32, (blocks_own, faces), 0)
    hit = (slot_ref[...] == block_ids) & (owner_ref[...] == here)
    weight = jnp.dot(hit.astype(jnp.bfloat16), scale_ref[...], preferred_element_type=jnp.float32) * sign
    weight_ref[...] = weight + block_weights((swapped_ref,), swapped_ref.shape[0] - SLOT_ROWS, blocks_own)

    square = (columns, columns)
    diagonal = lax.broadcasted_iota(jnp.int32, square, 0) == lax.broadcasted_iota(jnp.int32, square, 1)
    cells = jnp.sum(jnp.where(diagonal, cell_ref[...], 0), axis=1, keepdims=True)
    rates = jnp.sum(jnp.where(diagonal, rate_ref[...], 0.0), axis=1, keepdims=True)
    base = (here * mortar_ref.shape[0] + first_block) * dof_count
    offsets = cells - base - lax.broadcasted_iota(jnp.int32, (columns, dof_count), 1)
    rates = jnp.broadcast_to(rates, (columns, dof_count))
    tile_blocks = blocks_own // TILES
    for tile in range(TILES):
        at = slice(tile * tile_blocks, (tile + 1) * tile_blocks)
        values = mortar_ref[pl.ds(first_block + tile * tile_blocks, tile_blocks)].astype(jnp.float32)
        wells = jnp.stack(
            [jnp.where(offsets == block * dof_count, rates, 0.0) for block in range(at.start, at.stop)], axis=0
        )
        pumped = (values + wells).astype(jnp.bfloat16)
        pumped_ref[at] = pumped
        scaled = (pumped.astype(jnp.float32) * weight_ref[at][:, None, :]).astype(jnp.bfloat16)
        flux = jnp.dot(
            scaled.reshape(tile_blocks * columns, dof_count), basis_ref[0], preferred_element_type=jnp.float32
        )
        sum_ref[at] = flux.reshape(tile_blocks, columns, dof_count)


def gather_partners(arrays, weight_ref, basis_ref):
    count, blocks_own, dof_count = weight_ref.shape
    for at in range(count):
        base_0, base_1, pack, pack_swapped = arrays[4 * at : 4 * at + 4]
        weight_ref[at] = block_weights((pack, pack_swapped), pack.shape[0] - SLOT_ROWS, blocks_own)
        for core, base in enumerate((base_0, base_1)):

            @pl.when(lax.axis_index("face") == core)
            def _():
                basis_ref[at * dof_count : (at + 1) * dof_count, :] = base[0]


def tile_flux(at, slot, pumped_ref, sum_ref, weight_ref, basis_ref, scaled_ref):
    count, _, dof_count = weight_ref.shape
    rows = scaled_ref.shape[1]
    values = pumped_ref[at].astype(jnp.float32)
    for spot in range(count):
        scaled = (values * weight_ref[spot, at][:, None, :]).astype(jnp.bfloat16)
        scaled_ref[slot, :, spot * dof_count : (spot + 1) * dof_count] = scaled.reshape(rows, dof_count)
    total = jnp.dot(scaled_ref[slot], basis_ref[...], preferred_element_type=jnp.float32)
    return total + sum_ref[at].reshape(rows, dof_count)


def stage_kernel(pumped_ref, sum_ref, *refs):
    arrays, (out_ref, weight_ref, basis_ref, scaled_ref) = refs[:-4], refs[-4:]
    gather_partners(arrays, weight_ref, basis_ref)
    tile_blocks = pumped_ref.shape[0] // TILES
    for tile in range(TILES):
        at = slice(tile * tile_blocks, (tile + 1) * tile_blocks)
        total = tile_flux(at, tile % 2, pumped_ref, sum_ref, weight_ref, basis_ref, scaled_ref)
        out_ref[at] = total.reshape(pumped_ref[at].shape)


def last_kernel(pumped_ref, sum_ref, projection_ref, *refs):
    arrays, (result_ref, weight_ref, basis_ref, scaled_ref, out_ref, sems) = refs[:-6], refs[-6:]
    gather_partners(arrays, weight_ref, basis_ref)
    tiles = sems.shape[0]
    tile_blocks = pumped_ref.shape[0] // tiles
    copies = []
    for tile in range(tiles):
        at = slice(tile * tile_blocks, (tile + 1) * tile_blocks)
        total = tile_flux(at, tile % 2, pumped_ref, sum_ref, weight_ref, basis_ref, scaled_ref)
        result = jnp.dot(
            total.astype(jnp.bfloat16), projection_ref[...], preferred_element_type=jnp.float32
        )
        out_ref[at] = result.reshape(pumped_ref[at].shape)
        copies.append(pltpu.make_async_copy(out_ref.at[at], result_ref.at[at], sems.at[tile]))
        copies[-1].start()
    for copy in copies:
        copy.wait()


def on_device(
    mortar_in, pump_rate, well_cell, face_owner, face_slot, face_scale, section, basis, projection
):
    blocks_dev, cols_dev, dof_count = mortar_in.shape
    faces_dev = face_slot.shape[0]
    subdomains, halves = lax.axis_size("sub"), lax.axis_size("face")
    blocks_own = blocks_dev // halves
    capacity = max(2, 2 * faces_dev // subdomains)
    pack_rows = -(-capacity // ROW_TILE) * ROW_TILE + SLOT_ROWS
    block_shape = (blocks_own, cols_dev, dof_count)
    swap = [(i, i ^ 1) for i in range(halves)]

    def flat(sub, face):
        return sub * halves + face

    evens = list(range(2, subdomains, 2))
    cells = [(s, face) for s in range(subdomains) for face in range(halves)]
    firsts = [
        lax.ppermute(
            basis, ("sub", "face"), [(flat(s, face), flat(s ^ (1 if face else p), face)) for s, face in cells]
        )
        for p in evens
    ]
    partners = [0, *evens, 1, *[p + 1 for p in evens]]
    early_count = 1 + len(evens) + 1
    faces = [face_owner.reshape(1, faces_dev), face_slot.reshape(1, faces_dev), face_scale]
    packs = pl.pallas_call(
        functools.partial(pack_kernel, partners),
        out_shape=[pltpu.VMEM((pack_rows, dof_count), jnp.bfloat16)] * len(partners),
        in_specs=[VMEM, VMEM, VMEM, SMEM],
        out_specs=[VMEM] * len(partners),
        cost_estimate=WORK,
        name="pack_weights",
    )(*faces, section)

    arrived = [
        lax.ppermute(pack, "sub", [(i, i ^ p) for i in range(subdomains)]) for p, pack in zip(partners[1:], packs[1:])
    ]
    own_swapped = lax.ppermute(packs[0], "face", swap)

    firsts, own_swapped = lax.optimization_barrier((firsts, own_swapped))
    pumped, own_sum = pl.pallas_call(
        own_kernel,
        out_shape=[
            jax.ShapeDtypeStruct(block_shape, jnp.bfloat16),
            jax.ShapeDtypeStruct(block_shape, jnp.float32),
        ],
        in_specs=[VMEM] * 6 + [SMEM, VMEM, VMEM],
        out_specs=[VMEM, VMEM],
        scratch_shapes=[pltpu.VMEM((blocks_own, dof_count), jnp.float32)],
        compiler_params=pltpu.CompilerParams(vmem_limit_bytes=32 * MIB),
        cost_estimate=WORK,
        name="own_blocks",
    )(
        mortar_in,
        pump_rate.reshape(1, cols_dev),
        well_cell.reshape(1, cols_dev),
        *faces,
        section,
        basis,
        own_swapped,
    )

    pairs = [(flat(s, face), flat(s, 0) if face else flat(s ^ 1, 1)) for s, face in cells]
    seconds = [lax.ppermute(first, ("sub", "face"), pairs) for first in firsts]
    firsts, arrived[:len(evens)] = lax.optimization_barrier((firsts, arrived[:len(evens)]))
    firsts_swapped = [lax.ppermute(first, "face", swap) for first in firsts]
    soon, own_sum, firsts_swapped = lax.optimization_barrier(
        (arrived[: early_count - 1], own_sum, firsts_swapped)
    )

    def with_swapped(arrays):
        return [(array, lax.ppermute(array, "face", swap)) for array in arrays]

    weights = with_swapped(soon)
    own_sum, later = lax.optimization_barrier((own_sum, arrived[early_count - 1 :]))
    later = with_swapped(later)
    early = [[first, other, *pair] for first, other, pair in zip(firsts, firsts_swapped, weights)]
    early.append([firsts_swapped[0], firsts[0], *weights[-1]])

    def scratch(count, tiles):
        return [
            pltpu.VMEM((count, blocks_own, dof_count), jnp.float32),
            pltpu.VMEM((count * dof_count, dof_count), jnp.bfloat16),
            pltpu.VMEM((2, blocks_own // tiles * cols_dev, count * dof_count), jnp.bfloat16),
        ]

    operands = [pumped, own_sum, *sum(early, [])]
    total = pl.pallas_call(
        stage_kernel,
        out_shape=jax.ShapeDtypeStruct(block_shape, jnp.float32),
        in_specs=[VMEM] * len(operands),
        out_specs=VMEM,
        scratch_shapes=scratch(len(early), TILES),
        input_output_aliases={1: 0},
        compiler_params=pltpu.CompilerParams(vmem_limit_bytes=40 * MIB),
        cost_estimate=LIGHT,
        name="stage",
    )(*operands)

    seconds, total = lax.optimization_barrier((seconds, total))
    late = [[other, second, *pair] for (second, other), pair in zip(with_swapped(seconds), later)]

    operands = [pumped, total, projection, *sum(late, [])]
    return pl.pallas_call(
        last_kernel,
        out_shape=jax.ShapeDtypeStruct(block_shape, jnp.float32),
        in_specs=[VMEM] * len(operands),
        out_specs=HBM,
        scratch_shapes=[
            *scratch(len(late), LAST_TILES),
            pltpu.VMEM(block_shape, jnp.float32),
            pltpu.SemaphoreType.DMA((LAST_TILES,)),
        ],
        compiler_params=pltpu.CompilerParams(vmem_limit_bytes=40 * MIB),
        name="last_stage",
    )(*operands)


def solution(mesh):
    in_specs = (
        P(("groups", "sub"), "rhs", None),
        P(("groups", "rhs")),
        P(("groups", "rhs")),
        P(("groups", "sub", "face"), None),
        P(("groups", "sub", "face")),
        P(("groups", "sub", "face"), None),
        P(("groups", "sub")),
        P(("groups", "sub"), None, None),
        P(),
    )
    out_specs = P(("groups", "sub", "face"), "rhs", None)
    return jax.shard_map(
        on_device, mesh=mesh, in_specs=in_specs, out_specs=out_specs, check_vma=False
    )
```

```python
import functools

import jax
import jax.numpy as jnp
from jax import lax
from jax.experimental import pallas as pl
from jax.experimental.pallas import tpu as pltpu
from jax.sharding import PartitionSpec as P

ROW_TILE = 16
SLOT_ROWS = 16
VMEM = pl.BlockSpec(memory_space=pltpu.VMEM)
HBM = pl.BlockSpec(memory_space=pltpu.HBM)
SMEM = pl.BlockSpec(memory_space=pltpu.SMEM)
MIB = 1024 * 1024
TILES = 4
LAST_TILES = 8
LIGHT = pl.CostEstimate(flops=1_000_000, bytes_accessed=1024, transcendentals=0)
WORK = pl.CostEstimate(flops=4_000_000_000, bytes_accessed=8 * MIB, transcendentals=0)


def pack_kernel(partners, owner_ref, slot_ref, scale_ref, section_ref, *packs):
    rows, dof_count = packs[0].shape
    rows -= SLOT_ROWS
    faces = owner_ref.shape[1]
    sign = (1 - 2 * section_ref[0]).astype(jnp.float32)
    here = lax.axis_index("sub")
    owners = jnp.concatenate(
        [jnp.full((1, faces), here ^ partner, jnp.int32) for partner in partners], axis=0
    )
    named = owners == owner_ref[...]
    earlier = lax.broadcasted_iota(jnp.int32, (faces, faces), 0) < lax.broadcasted_iota(
        jnp.int32, (faces, faces), 1
    )
    rank = jnp.dot(
        named.astype(jnp.bfloat16), earlier.astype(jnp.bfloat16), preferred_element_type=jnp.float32
    )
    place = jnp.where(named, rank, -1.0)
    at = lax.broadcasted_iota(jnp.int32, (rows, faces), 0).astype(jnp.float32)
    hit = jnp.concatenate([place[p : p + 1, :] == at for p in range(len(packs))], axis=0)
    hit = hit.astype(jnp.bfloat16)
    packed = jnp.dot(hit, scale_ref[...], preferred_element_type=jnp.float32) * sign
    listed = lax.dot_general(
        slot_ref[...].astype(jnp.bfloat16), hit, (((1,), (1,)), ((), ())), preferred_element_type=jnp.float32
    )
    packed = packed.astype(jnp.bfloat16)
    for p, pack_ref in enumerate(packs):
        pack_ref[:rows, :] = packed[p * rows : (p + 1) * rows, :]
        meta = jnp.concatenate(
            [listed[:, p * rows : (p + 1) * rows], jnp.zeros((1, dof_count - rows), jnp.float32)], axis=1
        )
        pack_ref[rows:, :] = jnp.broadcast_to(meta, (SLOT_ROWS, dof_count)).astype(jnp.bfloat16)


def block_weights(packs, rows, blocks_own):
    first = lax.axis_index("face") * blocks_own
    block_ids = first + lax.broadcasted_iota(jnp.int32, (blocks_own, rows), 0)
    total = None
    for pack in packs:
        slots = pack[rows : rows + SLOT_ROWS, :].astype(jnp.int32)[:1, :rows]
        hit = (slots == block_ids).astype(jnp.bfloat16)
        part = jnp.dot(hit, pack[:rows, :], preferred_element_type=jnp.float32)
        total = part if total is None else total + part
    return total


def own_kernel(
    mortar_ref,
    rate_ref,
    cell_ref,
    owner_ref,
    slot_ref,
    scale_ref,
    section_ref,
    basis_ref,
    swapped_ref,
    pumped_ref,
    sum_ref,
    weight_ref,
):
    blocks_own, columns, dof_count = pumped_ref.shape
    faces = owner_ref.shape[1]
    here = lax.axis_index("sub")
    first_block = lax.axis_index("face") * blocks_own
    sign = (1 - 2 * section_ref[0]).astype(jnp.float32)
    block_ids = first_block + lax.broadcasted_iota(jnp.int32, (blocks_own, faces), 0)
    hit = (slot_ref[...] == block_ids) & (owner_ref[...] == here)
    weight = jnp.dot(hit.astype(jnp.bfloat16), scale_ref[...], preferred_element_type=jnp.float32) * sign
    weight_ref[...] = weight + block_weights((swapped_ref,), swapped_ref.shape[0] - SLOT_ROWS, blocks_own)

    square = (columns, columns)
    diagonal = lax.broadcasted_iota(jnp.int32, square, 0) == lax.broadcasted_iota(jnp.int32, square, 1)
    cells = jnp.sum(jnp.where(diagonal, cell_ref[...], 0), axis=1, keepdims=True)
    rates = jnp.sum(jnp.where(diagonal, rate_ref[...], 0.0), axis=1, keepdims=True)
    base = (here * mortar_ref.shape[0] + first_block) * dof_count
    offsets = cells - base - lax.broadcasted_iota(jnp.int32, (columns, dof_count), 1)
    rates = jnp.broadcast_to(rates, (columns, dof_count))
    tile_blocks = blocks_own // TILES
    for tile in range(TILES):
        at = slice(tile * tile_blocks, (tile + 1) * tile_blocks)
        values = mortar_ref[pl.ds(first_block + tile * tile_blocks, tile_blocks)].astype(jnp.float32)
        wells = jnp.stack(
            [jnp.where(offsets == block * dof_count, rates, 0.0) for block in range(at.start, at.stop)], axis=0
        )
        pumped = (values + wells).astype(jnp.bfloat16)
        pumped_ref[at] = pumped
        scaled = (pumped.astype(jnp.float32) * weight_ref[at][:, None, :]).astype(jnp.bfloat16)
        flux = jnp.dot(
            scaled.reshape(tile_blocks * columns, dof_count), basis_ref[0], preferred_element_type=jnp.float32
        )
        sum_ref[at] = flux.reshape(tile_blocks, columns, dof_count)


def gather_partners(arrays, weight_ref, basis_ref):
    count, blocks_own, dof_count = weight_ref.shape
    for at in range(count):
        base_0, base_1, pack, pack_swapped = arrays[4 * at : 4 * at + 4]
        weight_ref[at] = block_weights((pack, pack_swapped), pack.shape[0] - SLOT_ROWS, blocks_own)
        for core, base in enumerate((base_0, base_1)):

            @pl.when(lax.axis_index("face") == core)
            def _():
                basis_ref[at * dof_count : (at + 1) * dof_count, :] = base[0]


def tile_flux(at, slot, pumped_ref, sum_ref, weight_ref, basis_ref, scaled_ref):
    count, _, dof_count = weight_ref.shape
    rows = scaled_ref.shape[1]
    values = pumped_ref[at].astype(jnp.float32)
    for spot in range(count):
        scaled = (values * weight_ref[spot, at][:, None, :]).astype(jnp.bfloat16)
        scaled_ref[slot, :, spot * dof_count : (spot + 1) * dof_count] = scaled.reshape(rows, dof_count)
    total = jnp.dot(scaled_ref[slot], basis_ref[...], preferred_element_type=jnp.float32)
    return total + sum_ref[at].reshape(rows, dof_count)


def stage_kernel(pumped_ref, sum_ref, *refs):
    arrays, (out_ref, weight_ref, basis_ref, scaled_ref) = refs[:-4], refs[-4:]
    gather_partners(arrays, weight_ref, basis_ref)
    tile_blocks = pumped_ref.shape[0] // TILES
    for tile in range(TILES):
        at = slice(tile * tile_blocks, (tile + 1) * tile_blocks)
        total = tile_flux(at, tile % 2, pumped_ref, sum_ref, weight_ref, basis_ref, scaled_ref)
        out_ref[at] = total.reshape(pumped_ref[at].shape)


def last_kernel(pumped_ref, sum_ref, projection_ref, *refs):
    arrays, (result_ref, weight_ref, basis_ref, scaled_ref, out_ref, sems) = refs[:-6], refs[-6:]
    gather_partners(arrays, weight_ref, basis_ref)
    tiles = sems.shape[0]
    tile_blocks = pumped_ref.shape[0] // tiles
    copies = []
    for tile in range(tiles):
        at = slice(tile * tile_blocks, (tile + 1) * tile_blocks)
        total = tile_flux(at, tile % 2, pumped_ref, sum_ref, weight_ref, basis_ref, scaled_ref)
        result = jnp.dot(
            total.astype(jnp.bfloat16), projection_ref[...], preferred_element_type=jnp.float32
        )
        out_ref[at] = result.reshape(pumped_ref[at].shape)
        copies.append(pltpu.make_async_copy(out_ref.at[at], result_ref.at[at], sems.at[tile]))
        copies[-1].start()
    for copy in copies:
        copy.wait()


def on_device(
    mortar_in, pump_rate, well_cell, face_owner, face_slot, face_scale, section, basis, projection
):
    blocks_dev, cols_dev, dof_count = mortar_in.shape
    faces_dev = face_slot.shape[0]
    subdomains, halves = lax.axis_size("sub"), lax.axis_size("face")
    blocks_own = blocks_dev // halves
    capacity = max(2, 2 * faces_dev // subdomains)
    pack_rows = -(-capacity // ROW_TILE) * ROW_TILE + SLOT_ROWS
    block_shape = (blocks_own, cols_dev, dof_count)
    swap = [(i, i ^ 1) for i in range(halves)]

    def flat(sub, face):
        return sub * halves + face

    evens = list(range(2, subdomains, 2))
    cells = [(s, face) for s in range(subdomains) for face in range(halves)]
    firsts = [
        lax.ppermute(
            basis, ("sub", "face"), [(flat(s, face), flat(s ^ (1 if face else p), face)) for s, face in cells]
        )
        for p in evens
    ]
    partners = [0, *evens, 1, *[p + 1 for p in evens]]
    early_count = 1 + len(evens) + 1
    faces = [face_owner.reshape(1, faces_dev), face_slot.reshape(1, faces_dev), face_scale]
    packs = pl.pallas_call(
        functools.partial(pack_kernel, partners),
        out_shape=[pltpu.VMEM((pack_rows, dof_count), jnp.bfloat16)] * len(partners),
        in_specs=[VMEM, VMEM, VMEM, SMEM],
        out_specs=[VMEM] * len(partners),
        cost_estimate=WORK,
        name="pack_weights",
    )(*faces, section)

    arrived = [
        lax.ppermute(pack, "sub", [(i, i ^ p) for i in range(subdomains)]) for p, pack in zip(partners[1:], packs[1:])
    ]
    own_swapped = lax.ppermute(packs[0], "face", swap)

    firsts, own_swapped = lax.optimization_barrier((firsts, own_swapped))
    pumped, own_sum = pl.pallas_call(
        own_kernel,
        out_shape=[
            jax.ShapeDtypeStruct(block_shape, jnp.bfloat16),
            jax.ShapeDtypeStruct(block_shape, jnp.float32),
        ],
        in_specs=[VMEM] * 6 + [SMEM, VMEM, VMEM],
        out_specs=[VMEM, VMEM],
        scratch_shapes=[pltpu.VMEM((blocks_own, dof_count), jnp.float32)],
        compiler_params=pltpu.CompilerParams(vmem_limit_bytes=32 * MIB),
        cost_estimate=WORK,
        name="own_blocks",
    )(
        mortar_in,
        pump_rate.reshape(1, cols_dev),
        well_cell.reshape(1, cols_dev),
        *faces,
        section,
        basis,
        own_swapped,
    )

    pairs = [(flat(s, face), flat(s, 0) if face else flat(s ^ 1, 1)) for s, face in cells]
    seconds = [lax.ppermute(first, ("sub", "face"), pairs) for first in firsts]
    firsts, arrived[:len(evens)] = lax.optimization_barrier((firsts, arrived[:len(evens)]))
    firsts_swapped = [lax.ppermute(first, "face", swap) for first in firsts]
    soon, own_sum, firsts_swapped = lax.optimization_barrier(
        (arrived[: early_count - 1], own_sum, firsts_swapped)
    )

    def with_swapped(arrays):
        return [(array, lax.ppermute(array, "face", swap)) for array in arrays]

    weights = with_swapped(soon)
    own_sum, later = lax.optimization_barrier((own_sum, arrived[early_count - 1 :]))
    later = with_swapped(later)
    early = [[first, other, *pair] for first, other, pair in zip(firsts, firsts_swapped, weights)]
    early.append([firsts_swapped[0], firsts[0], *weights[-1]])

    def scratch(count, tiles):
        return [
            pltpu.VMEM((count, blocks_own, dof_count), jnp.float32),
            pltpu.VMEM((count * dof_count, dof_count), jnp.bfloat16),
            pltpu.VMEM((2, blocks_own // tiles * cols_dev, count * dof_count), jnp.bfloat16),
        ]

    operands = [pumped, own_sum, *sum(early, [])]
    total = pl.pallas_call(
        stage_kernel,
        out_shape=jax.ShapeDtypeStruct(block_shape, jnp.float32),
        in_specs=[VMEM] * len(operands),
        out_specs=VMEM,
        scratch_shapes=scratch(len(early), TILES),
        input_output_aliases={1: 0},
        compiler_params=pltpu.CompilerParams(vmem_limit_bytes=40 * MIB),
        cost_estimate=WORK,
        name="stage",
    )(*operands)

    late = [[other, second, *pair] for (second, other), pair in zip(with_swapped(seconds), later)]

    operands = [pumped, total, projection, *sum(late, [])]
    return pl.pallas_call(
        last_kernel,
        out_shape=jax.ShapeDtypeStruct(block_shape, jnp.float32),
        in_specs=[VMEM] * len(operands),
        out_specs=HBM,
        scratch_shapes=[
            *scratch(len(late), LAST_TILES),
            pltpu.VMEM(block_shape, jnp.float32),
            pltpu.SemaphoreType.DMA((LAST_TILES,)),
        ],
        compiler_params=pltpu.CompilerParams(vmem_limit_bytes=40 * MIB),
        name="last_stage",
    )(*operands)


def solution(mesh):
    in_specs = (
        P(("groups", "sub"), "rhs", None),
        P(("groups", "rhs")),
        P(("groups", "rhs")),
        P(("groups", "sub", "face"), None),
        P(("groups", "sub", "face")),
        P(("groups", "sub", "face"), None),
        P(("groups", "sub")),
        P(("groups", "sub"), None, None),
        P(),
    )
    out_specs = P(("groups", "sub", "face"), "rhs", None)
    return jax.shard_map(
        on_device, mesh=mesh, in_specs=in_specs, out_specs=out_specs, check_vma=False
    )
```

```python
import functools

import jax
import jax.numpy as jnp
from jax import lax
from jax.experimental import pallas as pl
from jax.experimental.pallas import tpu as pltpu
from jax.sharding import PartitionSpec as P

ROW_TILE = 16
SLOT_ROWS = 16
VMEM = pl.BlockSpec(memory_space=pltpu.VMEM)
HBM = pl.BlockSpec(memory_space=pltpu.HBM)
SMEM = pl.BlockSpec(memory_space=pltpu.SMEM)
MIB = 1024 * 1024
TILES = 4
LAST_TILES = 8
HANDED_PARTS = 2
LIGHT = pl.CostEstimate(flops=1_000_000, bytes_accessed=1024, transcendentals=0)
WORK = pl.CostEstimate(flops=4_000_000_000, bytes_accessed=8 * MIB, transcendentals=0)


def pack_kernel(partners, owner_ref, slot_ref, scale_ref, section_ref, *packs):
    rows, dof_count = packs[0].shape
    rows -= SLOT_ROWS
    faces = owner_ref.shape[1]
    sign = (1 - 2 * section_ref[0]).astype(jnp.float32)
    here = lax.axis_index("sub")
    owners = jnp.concatenate(
        [jnp.full((1, faces), here ^ partner, jnp.int32) for partner in partners], axis=0
    )
    named = owners == owner_ref[...]
    earlier = lax.broadcasted_iota(jnp.int32, (faces, faces), 0) < lax.broadcasted_iota(
        jnp.int32, (faces, faces), 1
    )
    rank = jnp.dot(
        named.astype(jnp.bfloat16), earlier.astype(jnp.bfloat16), preferred_element_type=jnp.float32
    )
    place = jnp.where(named, rank, -1.0)
    at = lax.broadcasted_iota(jnp.int32, (rows, faces), 0).astype(jnp.float32)
    hit = jnp.concatenate([place[p : p + 1, :] == at for p in range(len(packs))], axis=0)
    hit = hit.astype(jnp.bfloat16)
    packed = jnp.dot(hit, scale_ref[...], preferred_element_type=jnp.float32) * sign
    listed = lax.dot_general(
        slot_ref[...].astype(jnp.bfloat16), hit, (((1,), (1,)), ((), ())), preferred_element_type=jnp.float32
    )
    packed = packed.astype(jnp.bfloat16)
    for p, pack_ref in enumerate(packs):
        pack_ref[:rows, :] = packed[p * rows : (p + 1) * rows, :]
        meta = jnp.concatenate(
            [listed[:, p * rows : (p + 1) * rows], jnp.zeros((1, dof_count - rows), jnp.float32)], axis=1
        )
        pack_ref[rows:, :] = jnp.broadcast_to(meta, (SLOT_ROWS, dof_count)).astype(jnp.bfloat16)


def block_weights(packs, rows, blocks_own):
    first = lax.axis_index("face") * blocks_own
    block_ids = first + lax.broadcasted_iota(jnp.int32, (blocks_own, rows), 0)
    total = None
    for pack in packs:
        slots = pack[rows : rows + SLOT_ROWS, :].astype(jnp.int32)[:1, :rows]
        hit = (slots == block_ids).astype(jnp.bfloat16)
        part = jnp.dot(hit, pack[:rows, :], preferred_element_type=jnp.float32)
        total = part if total is None else total + part
    return total


def own_kernel(
    mortar_ref,
    rate_ref,
    cell_ref,
    owner_ref,
    slot_ref,
    scale_ref,
    section_ref,
    basis_ref,
    swapped_ref,
    pumped_ref,
    sum_ref,
    weight_ref,
):
    blocks_own, columns, dof_count = pumped_ref.shape
    faces = owner_ref.shape[1]
    here = lax.axis_index("sub")
    first_block = lax.axis_index("face") * blocks_own
    sign = (1 - 2 * section_ref[0]).astype(jnp.float32)
    block_ids = first_block + lax.broadcasted_iota(jnp.int32, (blocks_own, faces), 0)
    hit = (slot_ref[...] == block_ids) & (owner_ref[...] == here)
    weight = jnp.dot(hit.astype(jnp.bfloat16), scale_ref[...], preferred_element_type=jnp.float32) * sign
    weight_ref[...] = weight + block_weights((swapped_ref,), swapped_ref.shape[0] - SLOT_ROWS, blocks_own)

    square = (columns, columns)
    diagonal = lax.broadcasted_iota(jnp.int32, square, 0) == lax.broadcasted_iota(jnp.int32, square, 1)
    cells = jnp.sum(jnp.where(diagonal, cell_ref[...], 0), axis=1, keepdims=True)
    rates = jnp.sum(jnp.where(diagonal, rate_ref[...], 0.0), axis=1, keepdims=True)
    base = (here * mortar_ref.shape[0] + first_block) * dof_count
    offsets = cells - base - lax.broadcasted_iota(jnp.int32, (columns, dof_count), 1)
    rates = jnp.broadcast_to(rates, (columns, dof_count))
    tile_blocks = blocks_own // TILES
    for tile in range(TILES):
        at = slice(tile * tile_blocks, (tile + 1) * tile_blocks)
        values = mortar_ref[pl.ds(first_block + tile * tile_blocks, tile_blocks)].astype(jnp.float32)
        wells = jnp.stack(
            [jnp.where(offsets == block * dof_count, rates, 0.0) for block in range(at.start, at.stop)], axis=0
        )
        pumped = (values + wells).astype(jnp.bfloat16)
        pumped_ref[at] = pumped
        scaled = (pumped.astype(jnp.float32) * weight_ref[at][:, None, :]).astype(jnp.bfloat16)
        flux = jnp.dot(
            scaled.reshape(tile_blocks * columns, dof_count), basis_ref[0], preferred_element_type=jnp.float32
        )
        sum_ref[at] = flux.reshape(tile_blocks, columns, dof_count)


def gather_partners(parts, arrays, weight_ref, basis_ref):
    count, blocks_own, dof_count = weight_ref.shape
    each, rows = 2 * parts + 2, dof_count // parts
    for at in range(count):
        *bases, pack, pack_swapped = arrays[each * at : each * (at + 1)]
        weight_ref[at] = block_weights((pack, pack_swapped), pack.shape[0] - SLOT_ROWS, blocks_own)
        for core in range(2):

            @pl.when(lax.axis_index("face") == core)
            def _():
                for part, base in enumerate(bases[core * parts : (core + 1) * parts]):
                    start = at * dof_count + part * rows
                    basis_ref[start : start + rows, :] = base[0]


def tile_flux(at, slot, pumped_ref, sum_ref, weight_ref, basis_ref, scaled_ref):
    count, _, dof_count = weight_ref.shape
    rows = scaled_ref.shape[1]
    values = pumped_ref[at].astype(jnp.float32)
    for spot in range(count):
        scaled = (values * weight_ref[spot, at][:, None, :]).astype(jnp.bfloat16)
        scaled_ref[slot, :, spot * dof_count : (spot + 1) * dof_count] = scaled.reshape(rows, dof_count)
    total = jnp.dot(scaled_ref[slot], basis_ref[...], preferred_element_type=jnp.float32)
    return total + sum_ref[at].reshape(rows, dof_count)


def stage_kernel(pumped_ref, sum_ref, *refs):
    arrays, (out_ref, weight_ref, basis_ref, scaled_ref) = refs[:-4], refs[-4:]
    gather_partners(1, arrays, weight_ref, basis_ref)
    tile_blocks = pumped_ref.shape[0] // TILES
    for tile in range(TILES):
        at = slice(tile * tile_blocks, (tile + 1) * tile_blocks)
        total = tile_flux(at, tile % 2, pumped_ref, sum_ref, weight_ref, basis_ref, scaled_ref)
        out_ref[at] = total.reshape(pumped_ref[at].shape)


def last_kernel(pumped_ref, sum_ref, projection_ref, *refs):
    arrays, (result_ref, weight_ref, basis_ref, scaled_ref, out_ref, sems) = refs[:-6], refs[-6:]
    gather_partners(HANDED_PARTS, arrays, weight_ref, basis_ref)
    tiles = sems.shape[0]
    tile_blocks = pumped_ref.shape[0] // tiles
    copies = []
    for tile in range(tiles):
        at = slice(tile * tile_blocks, (tile + 1) * tile_blocks)
        total = tile_flux(at, tile % 2, pumped_ref, sum_ref, weight_ref, basis_ref, scaled_ref)
        result = jnp.dot(
            total.astype(jnp.bfloat16), projection_ref[...], preferred_element_type=jnp.float32
        )
        out_ref[at] = result.reshape(pumped_ref[at].shape)
        copies.append(pltpu.make_async_copy(out_ref.at[at], result_ref.at[at], sems.at[tile]))
        copies[-1].start()
    for copy in copies:
        copy.wait()


def on_device(
    mortar_in, pump_rate, well_cell, face_owner, face_slot, face_scale, section, basis, projection
):
    blocks_dev, cols_dev, dof_count = mortar_in.shape
    faces_dev = face_slot.shape[0]
    subdomains, halves = lax.axis_size("sub"), lax.axis_size("face")
    blocks_own = blocks_dev // halves
    capacity = max(2, 2 * faces_dev // subdomains)
    pack_rows = -(-capacity // ROW_TILE) * ROW_TILE + SLOT_ROWS
    block_shape = (blocks_own, cols_dev, dof_count)
    swap = [(i, i ^ 1) for i in range(halves)]

    def flat(sub, face):
        return sub * halves + face

    evens = list(range(2, subdomains, 2))
    cells = [(s, face) for s in range(subdomains) for face in range(halves)]
    firsts = [
        lax.ppermute(
            basis, ("sub", "face"), [(flat(s, face), flat(s ^ (1 if face else p), face)) for s, face in cells]
        )
        for p in evens
    ]
    partners = [0, *evens, 1, *[p + 1 for p in evens]]
    early_count = 1 + len(evens) + 1
    faces = [face_owner.reshape(1, faces_dev), face_slot.reshape(1, faces_dev), face_scale]
    packs = pl.pallas_call(
        functools.partial(pack_kernel, partners),
        out_shape=[pltpu.VMEM((pack_rows, dof_count), jnp.bfloat16)] * len(partners),
        in_specs=[VMEM, VMEM, VMEM, SMEM],
        out_specs=[VMEM] * len(partners),
        cost_estimate=WORK,
        name="pack_weights",
    )(*faces, section)

    arrived = [
        lax.ppermute(pack, "sub", [(i, i ^ p) for i in range(subdomains)]) for p, pack in zip(partners[1:], packs[1:])
    ]
    own_swapped = lax.ppermute(packs[0], "face", swap)

    firsts, own_swapped = lax.optimization_barrier((firsts, own_swapped))
    pumped, own_sum = pl.pallas_call(
        own_kernel,
        out_shape=[
            jax.ShapeDtypeStruct(block_shape, jnp.bfloat16),
            jax.ShapeDtypeStruct(block_shape, jnp.float32),
        ],
        in_specs=[VMEM] * 6 + [SMEM, VMEM, VMEM],
        out_specs=[VMEM, VMEM],
        scratch_shapes=[pltpu.VMEM((blocks_own, dof_count), jnp.float32)],
        compiler_params=pltpu.CompilerParams(vmem_limit_bytes=32 * MIB),
        cost_estimate=WORK,
        name="own_blocks",
    )(
        mortar_in,
        pump_rate.reshape(1, cols_dev),
        well_cell.reshape(1, cols_dev),
        *faces,
        section,
        basis,
        own_swapped,
    )

    pairs = [(flat(s, face), flat(s, 0) if face else flat(s ^ 1, 1)) for s, face in cells]
    part_rows = dof_count // HANDED_PARTS
    seconds = [
        lax.ppermute(first[:, i * part_rows : (i + 1) * part_rows], ("sub", "face"), pairs)
        for first in firsts
        for i in range(HANDED_PARTS)
    ]
    firsts, arrived[:len(evens)] = lax.optimization_barrier((firsts, arrived[:len(evens)]))
    firsts_swapped = [lax.ppermute(first, "face", swap) for first in firsts]
    soon, own_sum, firsts_swapped = lax.optimization_barrier(
        (arrived[: early_count - 1], own_sum, firsts_swapped)
    )

    def with_swapped(arrays):
        return [(array, lax.ppermute(array, "face", swap)) for array in arrays]

    weights = with_swapped(soon)
    own_sum, later = lax.optimization_barrier((own_sum, arrived[early_count - 1 :]))
    later = with_swapped(later)
    early = [[first, other, *pair] for first, other, pair in zip(firsts, firsts_swapped, weights)]
    early.append([firsts_swapped[0], firsts[0], *weights[-1]])

    def scratch(count, tiles):
        return [
            pltpu.VMEM((count, blocks_own, dof_count), jnp.float32),
            pltpu.VMEM((count * dof_count, dof_count), jnp.bfloat16),
            pltpu.VMEM((2, blocks_own // tiles * cols_dev, count * dof_count), jnp.bfloat16),
        ]

    operands = [pumped, own_sum, *sum(early, [])]
    total = pl.pallas_call(
        stage_kernel,
        out_shape=jax.ShapeDtypeStruct(block_shape, jnp.float32),
        in_specs=[VMEM] * len(operands),
        out_specs=VMEM,
        scratch_shapes=scratch(len(early), TILES),
        input_output_aliases={1: 0},
        compiler_params=pltpu.CompilerParams(vmem_limit_bytes=40 * MIB),
        cost_estimate=WORK,
        name="stage",
    )(*operands)

    seconds = with_swapped(seconds)
    late = []
    for at, pair in enumerate(later):
        handed = seconds[at * HANDED_PARTS : (at + 1) * HANDED_PARTS]
        late.append([*[other for _, other in handed], *[second for second, _ in handed], *pair])

    operands = [pumped, total, projection, *sum(late, [])]
    return pl.pallas_call(
        last_kernel,
        out_shape=jax.ShapeDtypeStruct(block_shape, jnp.float32),
        in_specs=[VMEM] * len(operands),
        out_specs=HBM,
        scratch_shapes=[
            *scratch(len(late), LAST_TILES),
            pltpu.VMEM(block_shape, jnp.float32),
            pltpu.SemaphoreType.DMA((LAST_TILES,)),
        ],
        compiler_params=pltpu.CompilerParams(vmem_limit_bytes=40 * MIB),
        name="last_stage",
    )(*operands)


def solution(mesh):
    in_specs = (
        P(("groups", "sub"), "rhs", None),
        P(("groups", "rhs")),
        P(("groups", "rhs")),
        P(("groups", "sub", "face"), None),
        P(("groups", "sub", "face")),
        P(("groups", "sub", "face"), None),
        P(("groups", "sub")),
        P(("groups", "sub"), None, None),
        P(),
    )
    out_specs = P(("groups", "sub", "face"), "rhs", None)
    return jax.shard_map(
        on_device, mesh=mesh, in_specs=in_specs, out_specs=out_specs, check_vma=False
    )
```

```python
import functools

import jax
import jax.numpy as jnp
from jax import lax
from jax.experimental import pallas as pl
from jax.experimental.pallas import tpu as pltpu
from jax.sharding import PartitionSpec as P

ROW_TILE = 16
SLOT_ROWS = 16
VMEM = pl.BlockSpec(memory_space=pltpu.VMEM)
HBM = pl.BlockSpec(memory_space=pltpu.HBM)
SMEM = pl.BlockSpec(memory_space=pltpu.SMEM)
MIB = 1024 * 1024
TILES = 4
LAST_TILES = 4
LIGHT = pl.CostEstimate(flops=1_000_000, bytes_accessed=1024, transcendentals=0)
WORK = pl.CostEstimate(flops=4_000_000_000, bytes_accessed=8 * MIB, transcendentals=0)


def pack_kernel(partners, owner_ref, slot_ref, scale_ref, section_ref, *packs):
    rows, dof_count = packs[0].shape
    rows -= SLOT_ROWS
    faces = owner_ref.shape[1]
    sign = (1 - 2 * section_ref[0]).astype(jnp.float32)
    here = lax.axis_index("sub")
    owners = jnp.concatenate(
        [jnp.full((1, faces), here ^ partner, jnp.int32) for partner in partners], axis=0
    )
    named = owners == owner_ref[...]
    earlier = lax.broadcasted_iota(jnp.int32, (faces, faces), 0) < lax.broadcasted_iota(
        jnp.int32, (faces, faces), 1
    )
    rank = jnp.dot(
        named.astype(jnp.bfloat16), earlier.astype(jnp.bfloat16), preferred_element_type=jnp.float32
    )
    place = jnp.where(named, rank, -1.0)
    at = lax.broadcasted_iota(jnp.int32, (rows, faces), 0).astype(jnp.float32)
    hit = jnp.concatenate([place[p : p + 1, :] == at for p in range(len(packs))], axis=0)
    hit = hit.astype(jnp.bfloat16)
    packed = jnp.dot(hit, scale_ref[...], preferred_element_type=jnp.float32) * sign
    listed = lax.dot_general(
        slot_ref[...].astype(jnp.bfloat16), hit, (((1,), (1,)), ((), ())), preferred_element_type=jnp.float32
    )
    packed = packed.astype(jnp.bfloat16)
    for p, pack_ref in enumerate(packs):
        pack_ref[:rows, :] = packed[p * rows : (p + 1) * rows, :]
        meta = jnp.concatenate(
            [listed[:, p * rows : (p + 1) * rows], jnp.zeros((1, dof_count - rows), jnp.float32)], axis=1
        )
        pack_ref[rows:, :] = jnp.broadcast_to(meta, (SLOT_ROWS, dof_count)).astype(jnp.bfloat16)


def block_weights(packs, rows, blocks_own):
    first = lax.axis_index("face") * blocks_own
    block_ids = first + lax.broadcasted_iota(jnp.int32, (blocks_own, rows), 0)
    total = None
    for pack in packs:
        slots = pack[rows : rows + SLOT_ROWS, :].astype(jnp.int32)[:1, :rows]
        hit = (slots == block_ids).astype(jnp.bfloat16)
        part = jnp.dot(hit, pack[:rows, :], preferred_element_type=jnp.float32)
        total = part if total is None else total + part
    return total


def own_kernel(
    mortar_ref,
    rate_ref,
    cell_ref,
    owner_ref,
    slot_ref,
    scale_ref,
    section_ref,
    basis_ref,
    swapped_ref,
    pumped_ref,
    sum_ref,
    weight_ref,
):
    blocks_own, columns, dof_count = pumped_ref.shape
    faces = owner_ref.shape[1]
    here = lax.axis_index("sub")
    first_block = lax.axis_index("face") * blocks_own
    sign = (1 - 2 * section_ref[0]).astype(jnp.float32)
    block_ids = first_block + lax.broadcasted_iota(jnp.int32, (blocks_own, faces), 0)
    hit = (slot_ref[...] == block_ids) & (owner_ref[...] == here)
    weight = jnp.dot(hit.astype(jnp.bfloat16), scale_ref[...], preferred_element_type=jnp.float32) * sign
    weight_ref[...] = weight + block_weights((swapped_ref,), swapped_ref.shape[0] - SLOT_ROWS, blocks_own)

    square = (columns, columns)
    diagonal = lax.broadcasted_iota(jnp.int32, square, 0) == lax.broadcasted_iota(jnp.int32, square, 1)
    cells = jnp.sum(jnp.where(diagonal, cell_ref[...], 0), axis=1, keepdims=True)
    rates = jnp.sum(jnp.where(diagonal, rate_ref[...], 0.0), axis=1, keepdims=True)
    base = (here * mortar_ref.shape[0] + first_block) * dof_count
    offsets = cells - base - lax.broadcasted_iota(jnp.int32, (columns, dof_count), 1)
    rates = jnp.broadcast_to(rates, (columns, dof_count))
    tile_blocks = blocks_own // TILES
    for tile in range(TILES):
        at = slice(tile * tile_blocks, (tile + 1) * tile_blocks)
        values = mortar_ref[pl.ds(first_block + tile * tile_blocks, tile_blocks)].astype(jnp.float32)
        wells = jnp.stack(
            [jnp.where(offsets == block * dof_count, rates, 0.0) for block in range(at.start, at.stop)], axis=0
        )
        pumped = (values + wells).astype(jnp.bfloat16)
        pumped_ref[at] = pumped
        scaled = (pumped.astype(jnp.float32) * weight_ref[at][:, None, :]).astype(jnp.bfloat16)
        flux = jnp.dot(
            scaled.reshape(tile_blocks * columns, dof_count), basis_ref[0], preferred_element_type=jnp.float32
        )
        sum_ref[at] = flux.reshape(tile_blocks, columns, dof_count)


def gather_partners(arrays, weight_ref, basis_ref):
    count, blocks_own, dof_count = weight_ref.shape
    for at in range(count):
        base_0, base_1, pack, pack_swapped = arrays[4 * at : 4 * at + 4]
        weight_ref[at] = block_weights((pack, pack_swapped), pack.shape[0] - SLOT_ROWS, blocks_own)
        for core, base in enumerate((base_0, base_1)):

            @pl.when(lax.axis_index("face") == core)
            def _():
                basis_ref[at * dof_count : (at + 1) * dof_count, :] = base[0]


def tile_flux(at, slot, pumped_ref, sum_ref, weight_ref, basis_ref, scaled_ref):
    count, _, dof_count = weight_ref.shape
    rows = scaled_ref.shape[1]
    values = pumped_ref[at].astype(jnp.float32)
    for spot in range(count):
        scaled = (values * weight_ref[spot, at][:, None, :]).astype(jnp.bfloat16)
        scaled_ref[slot, :, spot * dof_count : (spot + 1) * dof_count] = scaled.reshape(rows, dof_count)
    total = jnp.dot(scaled_ref[slot], basis_ref[...], preferred_element_type=jnp.float32)
    return total + sum_ref[at].reshape(rows, dof_count)


def stage_kernel(pumped_ref, sum_ref, *refs):
    arrays, (out_ref, weight_ref, basis_ref, scaled_ref) = refs[:-4], refs[-4:]
    gather_partners(arrays, weight_ref, basis_ref)
    tile_blocks = pumped_ref.shape[0] // TILES
    for tile in range(TILES):
        at = slice(tile * tile_blocks, (tile + 1) * tile_blocks)
        total = tile_flux(at, tile % 2, pumped_ref, sum_ref, weight_ref, basis_ref, scaled_ref)
        out_ref[at] = total.reshape(pumped_ref[at].shape)


def last_kernel(pumped_ref, sum_ref, projection_ref, *refs):
    arrays, (result_ref, weight_ref, basis_ref, scaled_ref, out_ref, sems) = refs[:-6], refs[-6:]
    gather_partners(arrays, weight_ref, basis_ref)
    tiles = sems.shape[0]
    tile_blocks = pumped_ref.shape[0] // tiles
    copies = []
    for tile in range(tiles):
        at = slice(tile * tile_blocks, (tile + 1) * tile_blocks)
        total = tile_flux(at, tile % 2, pumped_ref, sum_ref, weight_ref, basis_ref, scaled_ref)
        result = jnp.dot(
            total.astype(jnp.bfloat16), projection_ref[...], preferred_element_type=jnp.float32
        )
        out_ref[at] = result.reshape(pumped_ref[at].shape)
        copies.append(pltpu.make_async_copy(out_ref.at[at], result_ref.at[at], sems.at[tile]))
        copies[-1].start()
    for copy in copies:
        copy.wait()


def on_device(
    mortar_in, pump_rate, well_cell, face_owner, face_slot, face_scale, section, basis, projection
):
    blocks_dev, cols_dev, dof_count = mortar_in.shape
    faces_dev = face_slot.shape[0]
    subdomains, halves = lax.axis_size("sub"), lax.axis_size("face")
    blocks_own = blocks_dev // halves
    capacity = max(2, 2 * faces_dev // subdomains)
    pack_rows = -(-capacity // ROW_TILE) * ROW_TILE + SLOT_ROWS
    block_shape = (blocks_own, cols_dev, dof_count)
    swap = [(i, i ^ 1) for i in range(halves)]

    def flat(sub, face):
        return sub * halves + face

    evens = list(range(2, subdomains, 2))
    cells = [(s, face) for s in range(subdomains) for face in range(halves)]
    firsts = [
        lax.ppermute(
            basis, ("sub", "face"), [(flat(s, face), flat(s ^ (1 if face else p), face)) for s, face in cells]
        )
        for p in evens
    ]
    partners = [0, *evens, 1, *[p + 1 for p in evens]]
    early_count = 1 + len(evens) + 1
    faces = [face_owner.reshape(1, faces_dev), face_slot.reshape(1, faces_dev), face_scale]
    packs = pl.pallas_call(
        functools.partial(pack_kernel, partners),
        out_shape=[pltpu.VMEM((pack_rows, dof_count), jnp.bfloat16)] * len(partners),
        in_specs=[VMEM, VMEM, VMEM, SMEM],
        out_specs=[VMEM] * len(partners),
        cost_estimate=WORK,
        name="pack_weights",
    )(*faces, section)

    arrived = [
        lax.ppermute(pack, "sub", [(i, i ^ p) for i in range(subdomains)]) for p, pack in zip(partners[1:], packs[1:])
    ]
    own_swapped = lax.ppermute(packs[0], "face", swap)

    firsts, own_swapped = lax.optimization_barrier((firsts, own_swapped))
    pumped, own_sum = pl.pallas_call(
        own_kernel,
        out_shape=[
            jax.ShapeDtypeStruct(block_shape, jnp.bfloat16),
            jax.ShapeDtypeStruct(block_shape, jnp.float32),
        ],
        in_specs=[VMEM] * 6 + [SMEM, VMEM, VMEM],
        out_specs=[VMEM, VMEM],
        scratch_shapes=[pltpu.VMEM((blocks_own, dof_count), jnp.float32)],
        compiler_params=pltpu.CompilerParams(vmem_limit_bytes=32 * MIB),
        cost_estimate=WORK,
        name="own_blocks",
    )(
        mortar_in,
        pump_rate.reshape(1, cols_dev),
        well_cell.reshape(1, cols_dev),
        *faces,
        section,
        basis,
        own_swapped,
    )

    pairs = [(flat(s, face), flat(s, 0) if face else flat(s ^ 1, 1)) for s, face in cells]
    seconds = [lax.ppermute(first, ("sub", "face"), pairs) for first in firsts]
    firsts, arrived[:len(evens)] = lax.optimization_barrier((firsts, arrived[:len(evens)]))
    firsts_swapped = [lax.ppermute(first, "face", swap) for first in firsts]
    soon, own_sum, firsts_swapped = lax.optimization_barrier(
        (arrived[: early_count - 1], own_sum, firsts_swapped)
    )

    def with_swapped(arrays):
        return [(array, lax.ppermute(array, "face", swap)) for array in arrays]

    weights = with_swapped(soon)
    own_sum, later = lax.optimization_barrier((own_sum, arrived[early_count - 1 :]))
    later = with_swapped(later)
    early = [[first, other, *pair] for first, other, pair in zip(firsts, firsts_swapped, weights)]
    early.append([firsts_swapped[0], firsts[0], *weights[-1]])

    def scratch(count, tiles):
        return [
            pltpu.VMEM((count, blocks_own, dof_count), jnp.float32),
            pltpu.VMEM((count * dof_count, dof_count), jnp.bfloat16),
            pltpu.VMEM((2, blocks_own // tiles * cols_dev, count * dof_count), jnp.bfloat16),
        ]

    operands = [pumped, own_sum, *sum(early, [])]
    total = pl.pallas_call(
        stage_kernel,
        out_shape=jax.ShapeDtypeStruct(block_shape, jnp.float32),
        in_specs=[VMEM] * len(operands),
        out_specs=VMEM,
        scratch_shapes=scratch(len(early), TILES),
        input_output_aliases={1: 0},
        compiler_params=pltpu.CompilerParams(vmem_limit_bytes=40 * MIB),
        cost_estimate=WORK,
        name="stage",
    )(*operands)

    late = [[other, second, *pair] for (second, other), pair in zip(with_swapped(seconds), later)]

    operands = [pumped, total, projection, *sum(late, [])]
    return pl.pallas_call(
        last_kernel,
        out_shape=jax.ShapeDtypeStruct(block_shape, jnp.float32),
        in_specs=[VMEM] * len(operands),
        out_specs=HBM,
        scratch_shapes=[
            *scratch(len(late), LAST_TILES),
            pltpu.VMEM(block_shape, jnp.float32),
            pltpu.SemaphoreType.DMA((LAST_TILES,)),
        ],
        compiler_params=pltpu.CompilerParams(vmem_limit_bytes=40 * MIB),
        name="last_stage",
    )(*operands)


def solution(mesh):
    in_specs = (
        P(("groups", "sub"), "rhs", None),
        P(("groups", "rhs")),
        P(("groups", "rhs")),
        P(("groups", "sub", "face"), None),
        P(("groups", "sub", "face")),
        P(("groups", "sub", "face"), None),
        P(("groups", "sub")),
        P(("groups", "sub"), None, None),
        P(),
    )
    out_specs = P(("groups", "sub", "face"), "rhs", None)
    return jax.shard_map(
        on_device, mesh=mesh, in_specs=in_specs, out_specs=out_specs, check_vma=False
    )
```

```python
import functools

import jax
import jax.numpy as jnp
from jax import lax
from jax.experimental import pallas as pl
from jax.experimental.pallas import tpu as pltpu
from jax.sharding import PartitionSpec as P

ROW_TILE = 16
SLOT_ROWS = 16
VMEM = pl.BlockSpec(memory_space=pltpu.VMEM)
HBM = pl.BlockSpec(memory_space=pltpu.HBM)
SMEM = pl.BlockSpec(memory_space=pltpu.SMEM)
MIB = 1024 * 1024
TILES = 8
LAST_TILES = 16
LIGHT = pl.CostEstimate(flops=1_000_000, bytes_accessed=1024, transcendentals=0)
WORK = pl.CostEstimate(flops=4_000_000_000, bytes_accessed=8 * MIB, transcendentals=0)


def pack_kernel(partners, owner_ref, slot_ref, scale_ref, section_ref, *packs):
    rows, dof_count = packs[0].shape
    rows -= SLOT_ROWS
    faces = owner_ref.shape[1]
    sign = (1 - 2 * section_ref[0]).astype(jnp.float32)
    here = lax.axis_index("sub")
    owners = jnp.concatenate(
        [jnp.full((1, faces), here ^ partner, jnp.int32) for partner in partners], axis=0
    )
    named = owners == owner_ref[...]
    earlier = lax.broadcasted_iota(jnp.int32, (faces, faces), 0) < lax.broadcasted_iota(
        jnp.int32, (faces, faces), 1
    )
    rank = jnp.dot(
        named.astype(jnp.bfloat16), earlier.astype(jnp.bfloat16), preferred_element_type=jnp.float32
    )
    place = jnp.where(named, rank, -1.0)
    at = lax.broadcasted_iota(jnp.int32, (rows, faces), 0).astype(jnp.float32)
    hit = jnp.concatenate([place[p : p + 1, :] == at for p in range(len(packs))], axis=0)
    hit = hit.astype(jnp.bfloat16)
    packed = jnp.dot(hit, scale_ref[...], preferred_element_type=jnp.float32) * sign
    listed = lax.dot_general(
        slot_ref[...].astype(jnp.bfloat16), hit, (((1,), (1,)), ((), ())), preferred_element_type=jnp.float32
    )
    packed = packed.astype(jnp.bfloat16)
    for p, pack_ref in enumerate(packs):
        pack_ref[:rows, :] = packed[p * rows : (p + 1) * rows, :]
        meta = jnp.concatenate(
            [listed[:, p * rows : (p + 1) * rows], jnp.zeros((1, dof_count - rows), jnp.float32)], axis=1
        )
        pack_ref[rows:, :] = jnp.broadcast_to(meta, (SLOT_ROWS, dof_count)).astype(jnp.bfloat16)


def block_weights(packs, rows, blocks_own):
    first = lax.axis_index("face") * blocks_own
    block_ids = first + lax.broadcasted_iota(jnp.int32, (blocks_own, rows), 0)
    total = None
    for pack in packs:
        slots = pack[rows : rows + SLOT_ROWS, :].astype(jnp.int32)[:1, :rows]
        hit = (slots == block_ids).astype(jnp.bfloat16)
        part = jnp.dot(hit, pack[:rows, :], preferred_element_type=jnp.float32)
        total = part if total is None else total + part
    return total


def own_kernel(
    mortar_ref,
    rate_ref,
    cell_ref,
    owner_ref,
    slot_ref,
    scale_ref,
    section_ref,
    basis_ref,
    swapped_ref,
    pumped_ref,
    sum_ref,
    weight_ref,
):
    blocks_own, columns, dof_count = pumped_ref.shape
    faces = owner_ref.shape[1]
    here = lax.axis_index("sub")
    first_block = lax.axis_index("face") * blocks_own
    sign = (1 - 2 * section_ref[0]).astype(jnp.float32)
    block_ids = first_block + lax.broadcasted_iota(jnp.int32, (blocks_own, faces), 0)
    hit = (slot_ref[...] == block_ids) & (owner_ref[...] == here)
    weight = jnp.dot(hit.astype(jnp.bfloat16), scale_ref[...], preferred_element_type=jnp.float32) * sign
    weight_ref[...] = weight + block_weights((swapped_ref,), swapped_ref.shape[0] - SLOT_ROWS, blocks_own)

    square = (columns, columns)
    diagonal = lax.broadcasted_iota(jnp.int32, square, 0) == lax.broadcasted_iota(jnp.int32, square, 1)
    cells = jnp.sum(jnp.where(diagonal, cell_ref[...], 0), axis=1, keepdims=True)
    rates = jnp.sum(jnp.where(diagonal, rate_ref[...], 0.0), axis=1, keepdims=True)
    base = (here * mortar_ref.shape[0] + first_block) * dof_count
    offsets = cells - base - lax.broadcasted_iota(jnp.int32, (columns, dof_count), 1)
    rates = jnp.broadcast_to(rates, (columns, dof_count))
    tile_blocks = blocks_own // TILES
    for tile in range(TILES):
        at = slice(tile * tile_blocks, (tile + 1) * tile_blocks)
        values = mortar_ref[pl.ds(first_block + tile * tile_blocks, tile_blocks)].astype(jnp.float32)
        wells = jnp.stack(
            [jnp.where(offsets == block * dof_count, rates, 0.0) for block in range(at.start, at.stop)], axis=0
        )
        pumped = (values + wells).astype(jnp.bfloat16)
        pumped_ref[at] = pumped
        scaled = (pumped.astype(jnp.float32) * weight_ref[at][:, None, :]).astype(jnp.bfloat16)
        flux = jnp.dot(
            scaled.reshape(tile_blocks * columns, dof_count), basis_ref[0], preferred_element_type=jnp.float32
        )
        sum_ref[at] = flux.reshape(tile_blocks, columns, dof_count)


def gather_partners(arrays, weight_ref, basis_ref):
    count, blocks_own, dof_count = weight_ref.shape
    for at in range(count):
        base_0, base_1, pack, pack_swapped = arrays[4 * at : 4 * at + 4]
        weight_ref[at] = block_weights((pack, pack_swapped), pack.shape[0] - SLOT_ROWS, blocks_own)
        for core, base in enumerate((base_0, base_1)):

            @pl.when(lax.axis_index("face") == core)
            def _():
                basis_ref[at * dof_count : (at + 1) * dof_count, :] = base[0]


def tile_flux(at, slot, pumped_ref, sum_ref, weight_ref, basis_ref, scaled_ref):
    count, _, dof_count = weight_ref.shape
    rows = scaled_ref.shape[1]
    values = pumped_ref[at].astype(jnp.float32)
    for spot in range(count):
        scaled = (values * weight_ref[spot, at][:, None, :]).astype(jnp.bfloat16)
        scaled_ref[slot, :, spot * dof_count : (spot + 1) * dof_count] = scaled.reshape(rows, dof_count)
    total = jnp.dot(scaled_ref[slot], basis_ref[...], preferred_element_type=jnp.float32)
    return total + sum_ref[at].reshape(rows, dof_count)


def stage_kernel(pumped_ref, sum_ref, *refs):
    arrays, (out_ref, weight_ref, basis_ref, scaled_ref) = refs[:-4], refs[-4:]
    gather_partners(arrays, weight_ref, basis_ref)
    tile_blocks = pumped_ref.shape[0] // TILES
    for tile in range(TILES):
        at = slice(tile * tile_blocks, (tile + 1) * tile_blocks)
        total = tile_flux(at, tile % 2, pumped_ref, sum_ref, weight_ref, basis_ref, scaled_ref)
        out_ref[at] = total.reshape(pumped_ref[at].shape)


def last_kernel(pumped_ref, sum_ref, projection_ref, *refs):
    arrays, (result_ref, weight_ref, basis_ref, scaled_ref, out_ref, sems) = refs[:-6], refs[-6:]
    gather_partners(arrays, weight_ref, basis_ref)
    tiles = sems.shape[0]
    tile_blocks = pumped_ref.shape[0] // tiles
    copies = []
    for tile in range(tiles):
        at = slice(tile * tile_blocks, (tile + 1) * tile_blocks)
        total = tile_flux(at, tile % 2, pumped_ref, sum_ref, weight_ref, basis_ref, scaled_ref)
        result = jnp.dot(
            total.astype(jnp.bfloat16), projection_ref[...], preferred_element_type=jnp.float32
        )
        out_ref[at] = result.reshape(pumped_ref[at].shape)
        copies.append(pltpu.make_async_copy(out_ref.at[at], result_ref.at[at], sems.at[tile]))
        copies[-1].start()
    for copy in copies:
        copy.wait()


def on_device(
    mortar_in, pump_rate, well_cell, face_owner, face_slot, face_scale, section, basis, projection
):
    blocks_dev, cols_dev, dof_count = mortar_in.shape
    faces_dev = face_slot.shape[0]
    subdomains, halves = lax.axis_size("sub"), lax.axis_size("face")
    blocks_own = blocks_dev // halves
    capacity = max(2, 2 * faces_dev // subdomains)
    pack_rows = -(-capacity // ROW_TILE) * ROW_TILE + SLOT_ROWS
    block_shape = (blocks_own, cols_dev, dof_count)
    swap = [(i, i ^ 1) for i in range(halves)]

    def flat(sub, face):
        return sub * halves + face

    evens = list(range(2, subdomains, 2))
    cells = [(s, face) for s in range(subdomains) for face in range(halves)]
    firsts = [
        lax.ppermute(
            basis, ("sub", "face"), [(flat(s, face), flat(s ^ (1 if face else p), face)) for s, face in cells]
        )
        for p in evens
    ]
    partners = [0, *evens, 1, *[p + 1 for p in evens]]
    early_count = 1 + len(evens) + 1
    faces = [face_owner.reshape(1, faces_dev), face_slot.reshape(1, faces_dev), face_scale]
    packs = pl.pallas_call(
        functools.partial(pack_kernel, partners),
        out_shape=[pltpu.VMEM((pack_rows, dof_count), jnp.bfloat16)] * len(partners),
        in_specs=[VMEM, VMEM, VMEM, SMEM],
        out_specs=[VMEM] * len(partners),
        cost_estimate=WORK,
        name="pack_weights",
    )(*faces, section)

    arrived = [
        lax.ppermute(pack, "sub", [(i, i ^ p) for i in range(subdomains)]) for p, pack in zip(partners[1:], packs[1:])
    ]
    own_swapped = lax.ppermute(packs[0], "face", swap)

    firsts, own_swapped = lax.optimization_barrier((firsts, own_swapped))
    pumped, own_sum = pl.pallas_call(
        own_kernel,
        out_shape=[
            jax.ShapeDtypeStruct(block_shape, jnp.bfloat16),
            jax.ShapeDtypeStruct(block_shape, jnp.float32),
        ],
        in_specs=[VMEM] * 6 + [SMEM, VMEM, VMEM],
        out_specs=[VMEM, VMEM],
        scratch_shapes=[pltpu.VMEM((blocks_own, dof_count), jnp.float32)],
        compiler_params=pltpu.CompilerParams(vmem_limit_bytes=32 * MIB),
        cost_estimate=WORK,
        name="own_blocks",
    )(
        mortar_in,
        pump_rate.reshape(1, cols_dev),
        well_cell.reshape(1, cols_dev),
        *faces,
        section,
        basis,
        own_swapped,
    )

    pairs = [(flat(s, face), flat(s, 0) if face else flat(s ^ 1, 1)) for s, face in cells]
    seconds = [lax.ppermute(first, ("sub", "face"), pairs) for first in firsts]
    firsts, arrived[:len(evens)] = lax.optimization_barrier((firsts, arrived[:len(evens)]))
    firsts_swapped = [lax.ppermute(first, "face", swap) for first in firsts]
    soon, own_sum, firsts_swapped = lax.optimization_barrier(
        (arrived[: early_count - 1], own_sum, firsts_swapped)
    )

    def with_swapped(arrays):
        return [(array, lax.ppermute(array, "face", swap)) for array in arrays]

    weights = with_swapped(soon)
    own_sum, later = lax.optimization_barrier((own_sum, arrived[early_count - 1 :]))
    later = with_swapped(later)
    early = [[first, other, *pair] for first, other, pair in zip(firsts, firsts_swapped, weights)]
    early.append([firsts_swapped[0], firsts[0], *weights[-1]])

    def scratch(count, tiles):
        return [
            pltpu.VMEM((count, blocks_own, dof_count), jnp.float32),
            pltpu.VMEM((count * dof_count, dof_count), jnp.bfloat16),
            pltpu.VMEM((2, blocks_own // tiles * cols_dev, count * dof_count), jnp.bfloat16),
        ]

    operands = [pumped, own_sum, *sum(early, [])]
    total = pl.pallas_call(
        stage_kernel,
        out_shape=jax.ShapeDtypeStruct(block_shape, jnp.float32),
        in_specs=[VMEM] * len(operands),
        out_specs=VMEM,
        scratch_shapes=scratch(len(early), TILES),
        input_output_aliases={1: 0},
        compiler_params=pltpu.CompilerParams(vmem_limit_bytes=40 * MIB),
        cost_estimate=WORK,
        name="stage",
    )(*operands)

    late = [[other, second, *pair] for (second, other), pair in zip(with_swapped(seconds), later)]

    operands = [pumped, total, projection, *sum(late, [])]
    return pl.pallas_call(
        last_kernel,
        out_shape=jax.ShapeDtypeStruct(block_shape, jnp.float32),
        in_specs=[VMEM] * len(operands),
        out_specs=HBM,
        scratch_shapes=[
            *scratch(len(late), LAST_TILES),
            pltpu.VMEM(block_shape, jnp.float32),
            pltpu.SemaphoreType.DMA((LAST_TILES,)),
        ],
        compiler_params=pltpu.CompilerParams(vmem_limit_bytes=40 * MIB),
        name="last_stage",
    )(*operands)


def solution(mesh):
    in_specs = (
        P(("groups", "sub"), "rhs", None),
        P(("groups", "rhs")),
        P(("groups", "rhs")),
        P(("groups", "sub", "face"), None),
        P(("groups", "sub", "face")),
        P(("groups", "sub", "face"), None),
        P(("groups", "sub")),
        P(("groups", "sub"), None, None),
        P(),
    )
    out_specs = P(("groups", "sub", "face"), "rhs", None)
    return jax.shard_map(
        on_device, mesh=mesh, in_specs=in_specs, out_specs=out_specs, check_vma=False
    )
```

```python
import functools

import jax
import jax.numpy as jnp
from jax import lax
from jax.experimental import pallas as pl
from jax.experimental.pallas import tpu as pltpu
from jax.sharding import PartitionSpec as P

ROW_TILE = 16
SLOT_ROWS = 16
VMEM = pl.BlockSpec(memory_space=pltpu.VMEM)
HBM = pl.BlockSpec(memory_space=pltpu.HBM)
SMEM = pl.BlockSpec(memory_space=pltpu.SMEM)
MIB = 1024 * 1024
TILES = 4
LAST_TILES = 8
LIGHT = pl.CostEstimate(flops=1_000_000, bytes_accessed=1024, transcendentals=0)
WORK = pl.CostEstimate(flops=4_000_000_000, bytes_accessed=8 * MIB, transcendentals=0)


def pack_kernel(partners, owner_ref, slot_ref, scale_ref, section_ref, *packs):
    rows, dof_count = packs[0].shape
    rows -= SLOT_ROWS
    faces = owner_ref.shape[1]
    sign = (1 - 2 * section_ref[0]).astype(jnp.float32)
    here = lax.axis_index("sub")
    owners = jnp.concatenate(
        [jnp.full((1, faces), here ^ partner, jnp.int32) for partner in partners], axis=0
    )
    named = owners == owner_ref[...]
    earlier = lax.broadcasted_iota(jnp.int32, (faces, faces), 0) < lax.broadcasted_iota(
        jnp.int32, (faces, faces), 1
    )
    rank = jnp.dot(
        named.astype(jnp.bfloat16), earlier.astype(jnp.bfloat16), preferred_element_type=jnp.float32
    )
    place = jnp.where(named, rank, -1.0)
    at = lax.broadcasted_iota(jnp.int32, (rows, faces), 0).astype(jnp.float32)
    hit = jnp.concatenate([place[p : p + 1, :] == at for p in range(len(packs))], axis=0)
    hit = hit.astype(jnp.bfloat16)
    packed = jnp.dot(hit, scale_ref[...], preferred_element_type=jnp.float32) * sign
    listed = lax.dot_general(
        slot_ref[...].astype(jnp.bfloat16), hit, (((1,), (1,)), ((), ())), preferred_element_type=jnp.float32
    )
    packed = packed.astype(jnp.bfloat16)
    for p, pack_ref in enumerate(packs):
        pack_ref[:rows, :] = packed[p * rows : (p + 1) * rows, :]
        meta = jnp.concatenate(
            [listed[:, p * rows : (p + 1) * rows], jnp.zeros((1, dof_count - rows), jnp.float32)], axis=1
        )
        pack_ref[rows:, :] = jnp.broadcast_to(meta, (SLOT_ROWS, dof_count)).astype(jnp.bfloat16)


def block_weights(packs, rows, blocks_own):
    first = lax.axis_index("face") * blocks_own
    block_ids = first + lax.broadcasted_iota(jnp.int32, (blocks_own, rows), 0)
    total = None
    for pack in packs:
        slots = pack[rows : rows + SLOT_ROWS, :].astype(jnp.int32)[:1, :rows]
        hit = (slots == block_ids).astype(jnp.bfloat16)
        part = jnp.dot(hit, pack[:rows, :], preferred_element_type=jnp.float32)
        total = part if total is None else total + part
    return total


def own_kernel(
    mortar_ref,
    rate_ref,
    cell_ref,
    owner_ref,
    slot_ref,
    scale_ref,
    section_ref,
    basis_ref,
    swapped_ref,
    pumped_ref,
    sum_ref,
    weight_ref,
):
    blocks_own, columns, dof_count = pumped_ref.shape
    faces = owner_ref.shape[1]
    here = lax.axis_index("sub")
    first_block = lax.axis_index("face") * blocks_own
    sign = (1 - 2 * section_ref[0]).astype(jnp.float32)
    block_ids = first_block + lax.broadcasted_iota(jnp.int32, (blocks_own, faces), 0)
    hit = (slot_ref[...] == block_ids) & (owner_ref[...] == here)
    weight = jnp.dot(hit.astype(jnp.bfloat16), scale_ref[...], preferred_element_type=jnp.float32) * sign
    weight_ref[...] = weight + block_weights((swapped_ref,), swapped_ref.shape[0] - SLOT_ROWS, blocks_own)

    square = (columns, columns)
    diagonal = lax.broadcasted_iota(jnp.int32, square, 0) == lax.broadcasted_iota(jnp.int32, square, 1)
    cells = jnp.sum(jnp.where(diagonal, cell_ref[...], 0), axis=1, keepdims=True)
    rates = jnp.sum(jnp.where(diagonal, rate_ref[...], 0.0), axis=1, keepdims=True)
    base = (here * mortar_ref.shape[0] + first_block) * dof_count
    offsets = cells - base - lax.broadcasted_iota(jnp.int32, (columns, dof_count), 1)
    rates = jnp.broadcast_to(rates, (columns, dof_count))
    tile_blocks = blocks_own // TILES
    for tile in range(TILES):
        at = slice(tile * tile_blocks, (tile + 1) * tile_blocks)
        values = mortar_ref[pl.ds(first_block + tile * tile_blocks, tile_blocks)].astype(jnp.float32)
        wells = jnp.stack(
            [jnp.where(offsets == block * dof_count, rates, 0.0) for block in range(at.start, at.stop)], axis=0
        )
        pumped = (values + wells).astype(jnp.bfloat16)
        pumped_ref[at] = pumped
        scaled = (pumped.astype(jnp.float32) * weight_ref[at][:, None, :]).astype(jnp.bfloat16)
        flux = jnp.dot(
            scaled.reshape(tile_blocks * columns, dof_count), basis_ref[0], preferred_element_type=jnp.float32
        )
        sum_ref[at] = flux.reshape(tile_blocks, columns, dof_count)


def gather_partners(arrays, weight_ref, basis_ref):
    count, blocks_own, dof_count = weight_ref.shape
    for at in range(count):
        base_0, base_1, pack, pack_swapped = arrays[4 * at : 4 * at + 4]
        weight_ref[at] = block_weights((pack, pack_swapped), pack.shape[0] - SLOT_ROWS, blocks_own)
        for core, base in enumerate((base_0, base_1)):

            @pl.when(lax.axis_index("face") == core)
            def _():
                basis_ref[at * dof_count : (at + 1) * dof_count, :] = base[0]


def tile_flux(at, slot, pumped_ref, sum_ref, weight_ref, basis_ref, scaled_ref):
    count, _, dof_count = weight_ref.shape
    rows = scaled_ref.shape[1]
    values = pumped_ref[at].astype(jnp.float32)
    for spot in range(count):
        scaled = (values * weight_ref[spot, at][:, None, :]).astype(jnp.bfloat16)
        scaled_ref[slot, :, spot * dof_count : (spot + 1) * dof_count] = scaled.reshape(rows, dof_count)
    total = jnp.dot(scaled_ref[slot], basis_ref[...], preferred_element_type=jnp.float32)
    return total + sum_ref[at].reshape(rows, dof_count)


def stage_kernel(pumped_ref, sum_ref, *refs):
    arrays, (out_ref, weight_ref, basis_ref, scaled_ref) = refs[:-4], refs[-4:]
    gather_partners(arrays, weight_ref, basis_ref)
    tile_blocks = pumped_ref.shape[0] // TILES
    for tile in range(TILES):
        at = slice(tile * tile_blocks, (tile + 1) * tile_blocks)
        total = tile_flux(at, tile % 2, pumped_ref, sum_ref, weight_ref, basis_ref, scaled_ref)
        out_ref[at] = total.reshape(pumped_ref[at].shape)


def last_kernel(pumped_ref, sum_ref, projection_ref, *refs):
    arrays, (result_ref, weight_ref, basis_ref, scaled_ref, out_ref, sems) = refs[:-6], refs[-6:]
    gather_partners(arrays, weight_ref, basis_ref)
    tiles = sems.shape[0]
    tile_blocks = pumped_ref.shape[0] // tiles
    copies = []
    for tile in range(tiles):
        at = slice(tile * tile_blocks, (tile + 1) * tile_blocks)
        total = tile_flux(at, tile % 2, pumped_ref, sum_ref, weight_ref, basis_ref, scaled_ref)
        result = jnp.dot(
            total.astype(jnp.bfloat16), projection_ref[...], preferred_element_type=jnp.float32
        )
        out_ref[at] = result.reshape(pumped_ref[at].shape)
        copies.append(pltpu.make_async_copy(out_ref.at[at], result_ref.at[at], sems.at[tile]))
        copies[-1].start()
    for copy in copies:
        copy.wait()


def on_device(
    mortar_in, pump_rate, well_cell, face_owner, face_slot, face_scale, section, basis, projection
):
    blocks_dev, cols_dev, dof_count = mortar_in.shape
    faces_dev = face_slot.shape[0]
    subdomains, halves = lax.axis_size("sub"), lax.axis_size("face")
    blocks_own = blocks_dev // halves
    capacity = max(2, 2 * faces_dev // subdomains)
    pack_rows = -(-capacity // ROW_TILE) * ROW_TILE + SLOT_ROWS
    block_shape = (blocks_own, cols_dev, dof_count)
    swap = [(i, i ^ 1) for i in range(halves)]

    def flat(sub, face):
        return sub * halves + face

    evens = list(range(2, subdomains, 2))
    cells = [(s, face) for s in range(subdomains) for face in range(halves)]
    firsts = [
        lax.ppermute(
            basis, ("sub", "face"), [(flat(s, face), flat(s ^ (1 if face else p), face)) for s, face in cells]
        )
        for p in evens
    ]
    partners = [0, *evens, 1, *[p + 1 for p in evens]]
    early_count = 1 + len(evens) + 1
    faces = [face_owner.reshape(1, faces_dev), face_slot.reshape(1, faces_dev), face_scale]
    packs = pl.pallas_call(
        functools.partial(pack_kernel, partners),
        out_shape=[pltpu.VMEM((pack_rows, dof_count), jnp.bfloat16)] * len(partners),
        in_specs=[VMEM, VMEM, VMEM, SMEM],
        out_specs=[VMEM] * len(partners),
        cost_estimate=WORK,
        name="pack_weights",
    )(*faces, section)

    arrived = [
        lax.ppermute(pack, "sub", [(i, i ^ p) for i in range(subdomains)]) for p, pack in zip(partners[1:], packs[1:])
    ]
    own_swapped = lax.ppermute(packs[0], "face", swap)

    firsts, own_swapped = lax.optimization_barrier((firsts, own_swapped))
    pumped, own_sum = pl.pallas_call(
        own_kernel,
        out_shape=[
            jax.ShapeDtypeStruct(block_shape, jnp.bfloat16),
            jax.ShapeDtypeStruct(block_shape, jnp.float32),
        ],
        in_specs=[VMEM] * 6 + [SMEM, VMEM, VMEM],
        out_specs=[VMEM, VMEM],
        scratch_shapes=[pltpu.VMEM((blocks_own, dof_count), jnp.float32)],
        compiler_params=pltpu.CompilerParams(vmem_limit_bytes=32 * MIB),
        cost_estimate=WORK,
        name="own_blocks",
    )(
        mortar_in,
        pump_rate.reshape(1, cols_dev),
        well_cell.reshape(1, cols_dev),
        *faces,
        section,
        basis,
        own_swapped,
    )

    pairs = [(flat(s, face), flat(s, 0) if face else flat(s ^ 1, 1)) for s, face in cells]
    seconds = [lax.ppermute(first, ("sub", "face"), pairs) for first in firsts]
    firsts, arrived[:len(evens)] = lax.optimization_barrier((firsts, arrived[:len(evens)]))
    firsts_swapped = [lax.ppermute(first, "face", swap) for first in firsts]
    soon, own_sum, firsts_swapped = lax.optimization_barrier(
        (arrived[: early_count - 1], own_sum, firsts_swapped)
    )

    def with_swapped(arrays):
        return [(array, lax.ppermute(array, "face", swap)) for array in arrays]

    weights = with_swapped(soon)
    own_sum, later = lax.optimization_barrier((own_sum, arrived[early_count - 1 :]))
    later = with_swapped(later)
    early = [[first, other, *pair] for first, other, pair in zip(firsts, firsts_swapped, weights)]
    early.append([firsts_swapped[0], firsts[0], *weights[-1]])

    def scratch(count, tiles):
        return [
            pltpu.VMEM((count, blocks_own, dof_count), jnp.float32),
            pltpu.VMEM((count * dof_count, dof_count), jnp.bfloat16),
            pltpu.VMEM((2, blocks_own // tiles * cols_dev, count * dof_count), jnp.bfloat16),
        ]

    def stage(total, arrays, cost):
        operands = [pumped, total, *arrays]
        return pl.pallas_call(
            stage_kernel,
            out_shape=jax.ShapeDtypeStruct(block_shape, jnp.float32),
            in_specs=[VMEM] * len(operands),
            out_specs=VMEM,
            scratch_shapes=scratch(len(arrays) // 4, TILES),
            input_output_aliases={1: 0},
            compiler_params=pltpu.CompilerParams(vmem_limit_bytes=40 * MIB),
            cost_estimate=cost,
            name="stage",
        )(*operands)

    total = stage(own_sum, early[-1], LIGHT)
    seconds, total = lax.optimization_barrier((seconds, total))
    late = [[other, second, *pair] for (second, other), pair in zip(with_swapped(seconds), later)]
    total = stage(total, sum(early[:-1], []), WORK)

    operands = [pumped, total, projection, *sum(late, [])]
    return pl.pallas_call(
        last_kernel,
        out_shape=jax.ShapeDtypeStruct(block_shape, jnp.float32),
        in_specs=[VMEM] * len(operands),
        out_specs=HBM,
        scratch_shapes=[
            *scratch(len(late), LAST_TILES),
            pltpu.VMEM(block_shape, jnp.float32),
            pltpu.SemaphoreType.DMA((LAST_TILES,)),
        ],
        compiler_params=pltpu.CompilerParams(vmem_limit_bytes=40 * MIB),
        name="last_stage",
    )(*operands)


def solution(mesh):
    in_specs = (
        P(("groups", "sub"), "rhs", None),
        P(("groups", "rhs")),
        P(("groups", "rhs")),
        P(("groups", "sub", "face"), None),
        P(("groups", "sub", "face")),
        P(("groups", "sub", "face"), None),
        P(("groups", "sub")),
        P(("groups", "sub"), None, None),
        P(),
    )
    out_specs = P(("groups", "sub", "face"), "rhs", None)
    return jax.shard_map(
        on_device, mesh=mesh, in_specs=in_specs, out_specs=out_specs, check_vma=False
    )
```

```python
import functools

import jax
import jax.numpy as jnp
from jax import lax
from jax.experimental import pallas as pl
from jax.experimental.pallas import tpu as pltpu
from jax.sharding import PartitionSpec as P

ROW_TILE = 16
SLOT_ROWS = 16
VMEM = pl.BlockSpec(memory_space=pltpu.VMEM)
HBM = pl.BlockSpec(memory_space=pltpu.HBM)
SMEM = pl.BlockSpec(memory_space=pltpu.SMEM)
MIB = 1024 * 1024
TILES = 4
LAST_TILES = 8
LIGHT = pl.CostEstimate(flops=1_000_000, bytes_accessed=1024, transcendentals=0)
WORK = pl.CostEstimate(flops=4_000_000_000, bytes_accessed=8 * MIB, transcendentals=0)


def pack_kernel(partners, owner_ref, slot_ref, scale_ref, section_ref, *packs):
    rows, dof_count = packs[0].shape
    rows -= SLOT_ROWS
    faces = owner_ref.shape[1]
    sign = (1 - 2 * section_ref[0]).astype(jnp.float32)
    here = lax.axis_index("sub")
    owners = jnp.concatenate(
        [jnp.full((1, faces), here ^ partner, jnp.int32) for partner in partners], axis=0
    )
    named = owners == owner_ref[...]
    earlier = lax.broadcasted_iota(jnp.int32, (faces, faces), 0) < lax.broadcasted_iota(
        jnp.int32, (faces, faces), 1
    )
    rank = jnp.dot(
        named.astype(jnp.bfloat16), earlier.astype(jnp.bfloat16), preferred_element_type=jnp.float32
    )
    place = jnp.where(named, rank, -1.0)
    at = lax.broadcasted_iota(jnp.int32, (rows, faces), 0).astype(jnp.float32)
    hit = jnp.concatenate([place[p : p + 1, :] == at for p in range(len(packs))], axis=0)
    hit = hit.astype(jnp.bfloat16)
    packed = jnp.dot(hit, scale_ref[...], preferred_element_type=jnp.float32) * sign
    listed = lax.dot_general(
        slot_ref[...].astype(jnp.bfloat16), hit, (((1,), (1,)), ((), ())), preferred_element_type=jnp.float32
    )
    packed = packed.astype(jnp.bfloat16)
    for p, pack_ref in enumerate(packs):
        pack_ref[:rows, :] = packed[p * rows : (p + 1) * rows, :]
        meta = jnp.concatenate(
            [listed[:, p * rows : (p + 1) * rows], jnp.zeros((1, dof_count - rows), jnp.float32)], axis=1
        )
        pack_ref[rows:, :] = jnp.broadcast_to(meta, (SLOT_ROWS, dof_count)).astype(jnp.bfloat16)


def block_weights(packs, rows, blocks_own):
    first = lax.axis_index("face") * blocks_own
    block_ids = first + lax.broadcasted_iota(jnp.int32, (blocks_own, rows), 0)
    total = None
    for pack in packs:
        slots = pack[rows : rows + SLOT_ROWS, :].astype(jnp.int32)[:1, :rows]
        hit = (slots == block_ids).astype(jnp.bfloat16)
        part = jnp.dot(hit, pack[:rows, :], preferred_element_type=jnp.float32)
        total = part if total is None else total + part
    return total


def own_kernel(
    mortar_ref,
    rate_ref,
    cell_ref,
    owner_ref,
    slot_ref,
    scale_ref,
    section_ref,
    basis_ref,
    swapped_ref,
    pumped_ref,
    sum_ref,
    weight_ref,
):
    blocks_own, columns, dof_count = pumped_ref.shape
    faces = owner_ref.shape[1]
    here = lax.axis_index("sub")
    first_block = lax.axis_index("face") * blocks_own
    sign = (1 - 2 * section_ref[0]).astype(jnp.float32)
    block_ids = first_block + lax.broadcasted_iota(jnp.int32, (blocks_own, faces), 0)
    hit = (slot_ref[...] == block_ids) & (owner_ref[...] == here)
    weight = jnp.dot(hit.astype(jnp.bfloat16), scale_ref[...], preferred_element_type=jnp.float32) * sign
    weight_ref[...] = weight + block_weights((swapped_ref,), swapped_ref.shape[0] - SLOT_ROWS, blocks_own)

    square = (columns, columns)
    diagonal = lax.broadcasted_iota(jnp.int32, square, 0) == lax.broadcasted_iota(jnp.int32, square, 1)
    cells = jnp.sum(jnp.where(diagonal, cell_ref[...], 0), axis=1, keepdims=True)
    rates = jnp.sum(jnp.where(diagonal, rate_ref[...], 0.0), axis=1, keepdims=True)
    base = (here * mortar_ref.shape[0] + first_block) * dof_count
    offsets = cells - base - lax.broadcasted_iota(jnp.int32, (columns, dof_count), 1)
    rates = jnp.broadcast_to(rates, (columns, dof_count))
    tile_blocks = blocks_own // TILES
    for tile in range(TILES):
        at = slice(tile * tile_blocks, (tile + 1) * tile_blocks)
        values = mortar_ref[pl.ds(first_block + tile * tile_blocks, tile_blocks)].astype(jnp.float32)
        wells = jnp.stack(
            [jnp.where(offsets == block * dof_count, rates, 0.0) for block in range(at.start, at.stop)], axis=0
        )
        pumped = (values + wells).astype(jnp.bfloat16)
        pumped_ref[at] = pumped
        scaled = (pumped.astype(jnp.float32) * weight_ref[at][:, None, :]).astype(jnp.bfloat16)
        flux = jnp.dot(
            scaled.reshape(tile_blocks * columns, dof_count), basis_ref[0], preferred_element_type=jnp.float32
        )
        sum_ref[at] = flux.reshape(tile_blocks, columns, dof_count)


def gather_partners(arrays, weight_ref, basis_ref):
    count, blocks_own, dof_count = weight_ref.shape
    for at in range(count):
        base_0, base_1, pack, pack_swapped = arrays[4 * at : 4 * at + 4]
        weight_ref[at] = block_weights((pack, pack_swapped), pack.shape[0] - SLOT_ROWS, blocks_own)
        for core, base in enumerate((base_0, base_1)):

            @pl.when(lax.axis_index("face") == core)
            def _():
                basis_ref[at * dof_count : (at + 1) * dof_count, :] = base[0]


def tile_flux(at, slot, pumped_ref, sum_ref, weight_ref, basis_ref, scaled_ref):
    count, _, dof_count = weight_ref.shape
    rows = scaled_ref.shape[1]
    values = pumped_ref[at].astype(jnp.float32)
    for spot in range(count):
        scaled = (values * weight_ref[spot, at][:, None, :]).astype(jnp.bfloat16)
        scaled_ref[slot, :, spot * dof_count : (spot + 1) * dof_count] = scaled.reshape(rows, dof_count)
    total = jnp.dot(scaled_ref[slot], basis_ref[...], preferred_element_type=jnp.float32)
    return total + sum_ref[at].reshape(rows, dof_count)


def stage_kernel(pumped_ref, sum_ref, *refs):
    arrays, (out_ref, weight_ref, basis_ref, scaled_ref) = refs[:-4], refs[-4:]
    gather_partners(arrays, weight_ref, basis_ref)
    tile_blocks = pumped_ref.shape[0] // TILES
    for tile in range(TILES):
        at = slice(tile * tile_blocks, (tile + 1) * tile_blocks)
        total = tile_flux(at, tile % 2, pumped_ref, sum_ref, weight_ref, basis_ref, scaled_ref)
        out_ref[at] = total.reshape(pumped_ref[at].shape)


def last_kernel(pumped_ref, sum_ref, projection_ref, *refs):
    arrays, (result_ref, weight_ref, basis_ref, scaled_ref, out_ref, sems) = refs[:-6], refs[-6:]
    gather_partners(arrays, weight_ref, basis_ref)
    tiles = sems.shape[0]
    tile_blocks = pumped_ref.shape[0] // tiles
    copies = []
    for tile in range(tiles):
        at = slice(tile * tile_blocks, (tile + 1) * tile_blocks)
        total = tile_flux(at, tile % 2, pumped_ref, sum_ref, weight_ref, basis_ref, scaled_ref)
        result = jnp.dot(
            total.astype(jnp.bfloat16), projection_ref[...], preferred_element_type=jnp.float32
        )
        out_ref[at] = result.reshape(pumped_ref[at].shape)
        copies.append(pltpu.make_async_copy(out_ref.at[at], result_ref.at[at], sems.at[tile]))
        copies[-1].start()
    for copy in copies:
        copy.wait()


def on_device(
    mortar_in, pump_rate, well_cell, face_owner, face_slot, face_scale, section, basis, projection
):
    blocks_dev, cols_dev, dof_count = mortar_in.shape
    faces_dev = face_slot.shape[0]
    subdomains, halves = lax.axis_size("sub"), lax.axis_size("face")
    blocks_own = blocks_dev // halves
    capacity = max(2, 2 * faces_dev // subdomains)
    pack_rows = -(-capacity // ROW_TILE) * ROW_TILE + SLOT_ROWS
    block_shape = (blocks_own, cols_dev, dof_count)
    swap = [(i, i ^ 1) for i in range(halves)]

    def flat(sub, face):
        return sub * halves + face

    evens = list(range(2, subdomains, 2))
    cells = [(s, face) for s in range(subdomains) for face in range(halves)]
    firsts = [
        lax.ppermute(
            basis, ("sub", "face"), [(flat(s, face), flat(s ^ (1 if face else p), face)) for s, face in cells]
        )
        for p in evens
    ]
    partners = [0, *evens, 1, *[p + 1 for p in evens]]
    early_count = 1 + len(evens) + 1
    faces = [face_owner.reshape(1, faces_dev), face_slot.reshape(1, faces_dev), face_scale]
    packs = pl.pallas_call(
        functools.partial(pack_kernel, partners),
        out_shape=[pltpu.VMEM((pack_rows, dof_count), jnp.bfloat16)] * len(partners),
        in_specs=[VMEM, VMEM, VMEM, SMEM],
        out_specs=[VMEM] * len(partners),
        cost_estimate=WORK,
        name="pack_weights",
    )(*faces, section)

    arrived = [
        lax.ppermute(pack, "sub", [(i, i ^ p) for i in range(subdomains)]) for p, pack in zip(partners[1:], packs[1:])
    ]
    own_swapped = lax.ppermute(packs[0], "face", swap)

    firsts, own_swapped = lax.optimization_barrier((firsts, own_swapped))
    pumped, own_sum = pl.pallas_call(
        own_kernel,
        out_shape=[
            jax.ShapeDtypeStruct(block_shape, jnp.bfloat16),
            jax.ShapeDtypeStruct(block_shape, jnp.float32),
        ],
        in_specs=[VMEM] * 6 + [SMEM, VMEM, VMEM],
        out_specs=[VMEM, VMEM],
        scratch_shapes=[pltpu.VMEM((blocks_own, dof_count), jnp.float32)],
        compiler_params=pltpu.CompilerParams(vmem_limit_bytes=32 * MIB),
        cost_estimate=WORK,
        name="own_blocks",
    )(
        mortar_in,
        pump_rate.reshape(1, cols_dev),
        well_cell.reshape(1, cols_dev),
        *faces,
        section,
        basis,
        own_swapped,
    )

    pairs = [(flat(s, face), flat(s, 0) if face else flat(s ^ 1, 1)) for s, face in cells]
    seconds = [lax.ppermute(first, ("sub", "face"), pairs) for first in firsts]
    firsts, arrived[:len(evens)] = lax.optimization_barrier((firsts, arrived[:len(evens)]))
    firsts_swapped = [lax.ppermute(first, "face", swap) for first in firsts]
    soon, own_sum = lax.optimization_barrier((arrived[: early_count - 1], own_sum))

    def with_swapped(arrays):
        return [(array, lax.ppermute(array, "face", swap)) for array in arrays]

    weights = with_swapped(soon)
    own_sum, later = lax.optimization_barrier((own_sum, arrived[early_count - 1 :]))
    later = with_swapped(later)
    early = [[first, other, *pair] for first, other, pair in zip(firsts, firsts_swapped, weights)]
    early.append([firsts_swapped[0], firsts[0], *weights[-1]])

    def scratch(count, tiles):
        return [
            pltpu.VMEM((count, blocks_own, dof_count), jnp.float32),
            pltpu.VMEM((count * dof_count, dof_count), jnp.bfloat16),
            pltpu.VMEM((2, blocks_own // tiles * cols_dev, count * dof_count), jnp.bfloat16),
        ]

    operands = [pumped, own_sum, *sum(early, [])]
    total = pl.pallas_call(
        stage_kernel,
        out_shape=jax.ShapeDtypeStruct(block_shape, jnp.float32),
        in_specs=[VMEM] * len(operands),
        out_specs=VMEM,
        scratch_shapes=scratch(len(early), TILES),
        input_output_aliases={1: 0},
        compiler_params=pltpu.CompilerParams(vmem_limit_bytes=40 * MIB),
        cost_estimate=WORK,
        name="stage",
    )(*operands)

    late = [[other, second, *pair] for (second, other), pair in zip(with_swapped(seconds), later)]

    operands = [pumped, total, projection, *sum(late, [])]
    return pl.pallas_call(
        last_kernel,
        out_shape=jax.ShapeDtypeStruct(block_shape, jnp.float32),
        in_specs=[VMEM] * len(operands),
        out_specs=HBM,
        scratch_shapes=[
            *scratch(len(late), LAST_TILES),
            pltpu.VMEM(block_shape, jnp.float32),
            pltpu.SemaphoreType.DMA((LAST_TILES,)),
        ],
        compiler_params=pltpu.CompilerParams(vmem_limit_bytes=40 * MIB),
        name="last_stage",
    )(*operands)


def solution(mesh):
    in_specs = (
        P(("groups", "sub"), "rhs", None),
        P(("groups", "rhs")),
        P(("groups", "rhs")),
        P(("groups", "sub", "face"), None),
        P(("groups", "sub", "face")),
        P(("groups", "sub", "face"), None),
        P(("groups", "sub")),
        P(("groups", "sub"), None, None),
        P(),
    )
    out_specs = P(("groups", "sub", "face"), "rhs", None)
    return jax.shard_map(
        on_device, mesh=mesh, in_specs=in_specs, out_specs=out_specs, check_vma=False
    )
```
